128 devices in a mesh: shard: 2 (over y_hi), ctx: 16 (over y_lo, z, core), tp: 4 (over x).
Axes of the slice: x: 4, y: 4 (y_hi: 2, y_lo: 2; y = y_hi * 2 + y_lo), z: 4, core: 2. Of those that a mesh axis runs over, the one named last changes fastest.
Arguments:
- hidden: bfloat16 [4, 4096, 1536], P('shard', 'ctx'), may hold values from -6 to 6
- lengths: int32 [4], P('shard'), may hold values from 1024 to 4096, as said below
- cotangent: bfloat16 [4, 4096, 1536], P('shard', 'ctx'), may hold values from -11 to 11
- in_weight: float32 [3, 1536, 1536], P(None, ('shard', 'ctx'), 'tp'), may hold values from -0.15625 to 0.15625
- in_moment: float32 [3, 1536, 1536], P(None, ('shard', 'ctx'), 'tp'), may hold values from -224 to 224
- in_average: float32 [3, 1536, 1536], P(None, ('shard', 'ctx'), 'tp'), may hold values from -0.15625 to 0.15625
- out_weight: float32 [1536, 1536], P('tp', ('shard', 'ctx')), may hold values from -0.15625 to 0.15625
- out_moment: float32 [1536, 1536], P('tp', ('shard', 'ctx')), may hold values from -224 to 224
- out_average: float32 [1536, 1536], P('tp', ('shard', 'ctx')), may hold values from -0.15625 to 0.15625
- gate_up_weight: float32 [2, 1536, 6912], P(None, ('shard', 'ctx'), 'tp'), may hold values from -0.15625 to 0.15625
- gate_up_moment: float32 [2, 1536, 6912], P(None, ('shard', 'ctx'), 'tp'), may hold values from -224 to 224
- gate_up_average: float32 [2, 1536, 6912], P(None, ('shard', 'ctx'), 'tp'), may hold values from -0.15625 to 0.15625
- down_weight: float32 [6912, 1536], P('tp', ('shard', 'ctx')), may hold values from -0.109375 to 0.109375
- down_moment: float32 [6912, 1536], P('tp', ('shard', 'ctx')), may hold values from -224 to 224
- down_average: float32 [6912, 1536], P('tp', ('shard', 'ctx')), may hold values from -0.109375 to 0.109375
- norm_gains: float32 [2, 1536], replicated, may hold values from 0.5 to 1.5
- gain_moment: float32 [2, 1536], replicated, may hold values from -224 to 224
- gain_average: float32 [2, 1536], replicated, may hold values from 0.5 to 1.5
- conv_taps: float32 [3, 1536], P(None, 'tp'), may hold values from -3.5 to 3.5
- taps_moment: float32 [3, 1536], P(None, 'tp'), may hold values from -224 to 224
- taps_average: float32 [3, 1536], P(None, 'tp'), may hold values from -3.5 to 3.5
Outputs:
- block_output: bfloat16 [4, 4096, 1536], P('shard', 'ctx')
- input_grad: float32 [4, 4096, 1536], P('shard', 'ctx')
- in_moment_new: float32 [3, 1536, 1536], P(None, ('shard', 'ctx'), 'tp')
- in_weight_new: float32 [3, 1536, 1536], P(None, ('shard', 'ctx'), 'tp')
- in_average_new: float32 [3, 1536, 1536], P(None, ('shard', 'ctx'), 'tp')
- out_moment_new: float32 [1536, 1536], P('tp', ('shard', 'ctx'))
- out_weight_new: float32 [1536, 1536], P('tp', ('shard', 'ctx'))
- out_average_new: float32 [1536, 1536], P('tp', ('shard', 'ctx'))
- gate_up_moment_new: float32 [2, 1536, 6912], P(None, ('shard', 'ctx'), 'tp')
- gate_up_weight_new: float32 [2, 1536, 6912], P(None, ('shard', 'ctx'), 'tp')
- gate_up_average_new: float32 [2, 1536, 6912], P(None, ('shard', 'ctx'), 'tp')
- down_moment_new: float32 [6912, 1536], P('tp', ('shard', 'ctx'))
- down_weight_new: float32 [6912, 1536], P('tp', ('shard', 'ctx'))
- down_average_new: float32 [6912, 1536], P('tp', ('shard', 'ctx'))
- gain_moment_new: float32 [2, 1536], replicated
- gains_new: float32 [2, 1536], replicated
- gain_average_new: float32 [2, 1536], replicated
- taps_moment_new: float32 [3, 1536], P(None, 'tp')
- taps_new: float32 [3, 1536], P(None, 'tp')
- taps_average_new: float32 [3, 1536], P(None, 'tp')
The draws below stay inside these ranges and needn't reach their ends.
Inputs may be any that keep to these rules, and one draw needn't show every extreme that they name: `lengths`: in each aligned group of 2 slots one slot is used to its end.
All inputs are finite; a program needn't handle non-finite values.
Results may differ from the reference program's by a relative error of at most 0.012.
Values may be sent and summed in bfloat16 or wider, within the bound.
A program may use at most 256 MiB of HBM per device.

```python
import jax
import jax.numpy as jnp
from jax import lax

D = 1536
FF = 6912
SLOTS_DEV = 2
SLOTS = 4
SLOT_LEN = 4096


def draw_lengths(key, part):
    key = jax.random.fold_in(key, 5)
    first_key, second_key = jax.random.split(key)
    ragged = jax.random.randint(first_key, (SLOTS,), SLOT_LEN // 4, SLOT_LEN + 1)
    chosen = jax.random.randint(second_key, (SLOTS // SLOTS_DEV,), 0, SLOTS_DEV)
    member = jnp.arange(SLOTS) % SLOTS_DEV
    full_slot = member == jnp.repeat(chosen, SLOTS_DEV)
    return jnp.where(full_slot, SLOT_LEN, ragged).astype(jnp.int32)


def draw_cotangent(key, part):
    key = jax.random.fold_in(key, 9)
    fraction = jnp.arange(SLOT_LEN, dtype=jnp.float32) / SLOT_LEN
    ramp_scale = 0.6 + 1.2 * fraction
    values = jax.random.normal(key, (SLOTS, SLOT_LEN, D), jnp.float32)
    return jnp.clip(values * ramp_scale[None, :, None], -11.0, 11.0).astype(jnp.bfloat16)


def block_scale(rng, shape, pieces, low, high):
    def one(axis_at, blocks):
        heights = jax.random.uniform(jax.random.fold_in(jax.random.fold_in(rng, 6), axis_at), (blocks,), jnp.float32, low / len(pieces), high / len(pieces))
        return jnp.repeat(jnp.exp(heights), shape[axis_at] // blocks).reshape((-1,) + (1,) * (len(shape) - axis_at - 1))

    loudness = one(*pieces[0])
    for cut in pieces[1:]:
        loudness = loudness * one(*cut)
    return loudness


def scatter_about(rng, extent, spread, most, cuts=(), kind=jnp.bfloat16):
    values = jax.random.normal(rng, extent, jnp.float32) * spread
    if len(cuts) > 0:
        values = block_scale(rng, extent, cuts, -0.22, 0.18) * values
    return jnp.clip(values, min=-most, max=most).astype(kind)


def setup_inputs(seed: int = 0) -> dict:
    arg_keys = jax.random.split(jax.random.key(seed), 22)
    hidden = scatter_about(arg_keys[0], (SLOTS, SLOT_LEN, D), 1.0, 6.0, ((0, 2), (1, 16)))
    lengths = draw_lengths(jax.random.fold_in(arg_keys[21], 71), 0)
    cotangent = draw_cotangent(jax.random.fold_in(arg_keys[21], 71), 0)
    in_weight = scatter_about(arg_keys[3], (3, D, D), D ** -0.5, 0.15625, ((1, 32), (2, 4)), jnp.float32)
    in_moment = scatter_about(arg_keys[4], (3, D, D), (0.3 * (SLOTS * SLOT_LEN) ** 0.5), 224.0, ((1, 32), (2, 4)), jnp.float32)
    in_average = scatter_about(arg_keys[5], (3, D, D), D ** -0.5, 0.15625, ((1, 32), (2, 4)), jnp.float32)
    out_weight = scatter_about(arg_keys[6], (D, D), D ** -0.5, 0.15625, ((0, 4), (1, 32)), jnp.float32)
    out_moment = scatter_about(arg_keys[7], (D, D), (0.3 * (SLOTS * SLOT_LEN) ** 0.5), 224.0, ((0, 4), (1, 32)), jnp.float32)
    out_average = scatter_about(arg_keys[8], (D, D), D ** -0.5, 0.15625, ((0, 4), (1, 32)), jnp.float32)
    gate_up_weight = scatter_about(arg_keys[9], (2, D, FF), D ** -0.5, 0.15625, ((1, 32), (2, 4)), jnp.float32)
    gate_up_moment = scatter_about(arg_keys[10], (2, D, FF), (0.3 * (SLOTS * SLOT_LEN) ** 0.5), 224.0, ((1, 32), (2, 4)), jnp.float32)
    gate_up_average = scatter_about(arg_keys[11], (2, D, FF), D ** -0.5, 0.15625, ((1, 32), (2, 4)), jnp.float32)
    down_weight = scatter_about(arg_keys[12], (FF, D), (FF // 2) ** -0.5, 0.109375, ((0, 4), (1, 32)), jnp.float32)
    down_moment = scatter_about(arg_keys[13], (FF, D), (0.3 * (SLOTS * SLOT_LEN) ** 0.5), 224.0, ((0, 4), (1, 32)), jnp.float32)
    down_average = scatter_about(arg_keys[14], (FF, D), (FF // 2) ** -0.5, 0.109375, ((0, 4), (1, 32)), jnp.float32)
    norm_gains = jnp.clip(1.0 + 0.1 * jax.random.normal(arg_keys[15], (2, D), jnp.float32), 0.5, 1.5)
    gain_moment = scatter_about(arg_keys[16], (2, D), (0.3 * (SLOTS * SLOT_LEN) ** 0.5), 224.0, (), jnp.float32)
    gain_average = jnp.clip(1.0 + 0.1 * jax.random.normal(arg_keys[17], (2, D), jnp.float32), 0.5, 1.5)
    conv_taps = scatter_about(arg_keys[18], (3, D), 3 ** -0.5, 3.5, ((1, 4),), jnp.float32)
    taps_moment = scatter_about(arg_keys[19], (3, D), (0.3 * (SLOTS * SLOT_LEN) ** 0.5), 224.0, ((1, 4),), jnp.float32)
    taps_average = scatter_about(arg_keys[20], (3, D), 3 ** -0.5, 3.5, ((1, 4),), jnp.float32)
    return {"hidden": hidden, "lengths": lengths, "cotangent": cotangent, "in_weight": in_weight, "in_moment": in_moment, "in_average": in_average, "out_weight": out_weight, "out_moment": out_moment, "out_average": out_average, "gate_up_weight": gate_up_weight, "gate_up_moment": gate_up_moment, "gate_up_average": gate_up_average, "down_weight": down_weight, "down_moment": down_moment, "down_average": down_average, "norm_gains": norm_gains, "gain_moment": gain_moment, "gain_average": gain_average, "conv_taps": conv_taps, "taps_moment": taps_moment, "taps_average": taps_average}


@jax.custom_vjp
def low(v):
    return lax.optimization_barrier(v.astype(jnp.bfloat16)).astype(jnp.float32)

@jax.custom_vjp
def low_back(v):
    return v

def low_keep(v):
    return (low(v), None)

def low_pass(kept, grad):
    return (grad,)

def back_keep(v):
    return (v, None)

def back_low(kept, grad):
    return (low(grad),)
low.defvjp(low_keep, low_pass)
low_back.defvjp(back_keep, back_low)
epsilon = 1e-05
momentum = 0.9
average_decay = 0.9
matrix_rate = 0.0004
small_rate = 0.005

def matmul(left_side, right_side):
    return jnp.dot(left_side, right_side, precision=lax.Precision.HIGHEST)

def rms_scale(values):
    inverse = lax.rsqrt(lax.optimization_barrier(jnp.mean(values * values, axis=-1, keepdims=True)) + epsilon)
    return values * inverse

def conv_block(stream, in_weight, out_weight, gate_up_weight, down_weight, norm_gains, conv_taps):
    seq_len = stream.shape[0]
    normed = low(rms_scale(stream) * norm_gains[0])
    projected = low_back(jnp.stack([matmul(normed, low(in_weight[member])) for member in range(3)]))
    product = projected[0] * projected[2]
    padded = jnp.concatenate([jnp.zeros((2, product.shape[1]), jnp.float32), product], axis=0)
    convolved = conv_taps[0] * padded[:seq_len] + conv_taps[1] * padded[1:seq_len + 1] + conv_taps[2] * padded[2:]
    gated_low = low(projected[1] * convolved)
    mixed_sum = low_back(matmul(gated_low, low(out_weight)))
    residual = stream + mixed_sum
    normed_two = low(rms_scale(residual) * norm_gains[1])
    gate_up = low_back(jnp.stack([matmul(normed_two, low(gate_up_weight[0])), matmul(normed_two, low(gate_up_weight[1]))]))
    inner_low = low(jax.nn.silu(gate_up[0]) * gate_up[1])
    branch = low_back(matmul(inner_low, low(down_weight)))
    return residual + branch

def nesterov(weight, moment, average, gradient, step_rate):
    moment_new = momentum * moment + gradient
    weight_new = weight - step_rate * (gradient + momentum * moment_new)
    average_new = average_decay * average + (1.0 - average_decay) * weight_new
    return (moment_new, weight_new, average_new)

def reference(hidden, lengths, cotangent, in_weight, in_moment, in_average, out_weight, out_moment, out_average, gate_up_weight, gate_up_moment, gate_up_average, down_weight, down_moment, down_average, norm_gains, gain_moment, gain_average, conv_taps, taps_moment, taps_average):
    parameters = (in_weight, out_weight, gate_up_weight, down_weight, norm_gains, conv_taps)
    seq_len = hidden.shape[1]

    def slot_step(totals, slot_items):
        stream, back_slot, length = slot_items
        valid_rows = (jnp.arange(seq_len, dtype=jnp.int32) < length).astype(jnp.float32)[:, None]
        result, pullback = jax.vjp(conv_block, stream, *parameters)
        gradients = pullback(back_slot * valid_rows)
        totals = tuple((running + gradient for running, gradient in zip(totals, gradients[1:])))
        return (totals, (result.astype(jnp.bfloat16), gradients[0]))
    initial = tuple((jnp.zeros_like(weight) for weight in parameters))
    totals, (output, input_grad) = lax.scan(slot_step, initial, (hidden.astype(jnp.float32), cotangent.astype(jnp.float32), lengths))
    in_new = nesterov(in_weight, in_moment, in_average, totals[0], matrix_rate)
    out_new = nesterov(out_weight, out_moment, out_average, totals[1], matrix_rate)
    gate_up_new = nesterov(gate_up_weight, gate_up_moment, gate_up_average, totals[2], matrix_rate)
    down_new = nesterov(down_weight, down_moment, down_average, totals[3], matrix_rate)
    gain_new = nesterov(norm_gains, gain_moment, gain_average, totals[4], small_rate)
    taps_new = nesterov(conv_taps, taps_moment, taps_average, totals[5], small_rate)
    return (output, input_grad, in_new[0], in_new[1], in_new[2], out_new[0], out_new[1], out_new[2], gate_up_new[0], gate_up_new[1], gate_up_new[2], down_new[0], down_new[1], down_new[2], gain_new[0], gain_new[1], gain_new[2], taps_new[0], taps_new[1], taps_new[2])
```

```python
import functools

import jax
import jax.numpy as jnp
from jax import lax
from jax.experimental import pallas as pl
from jax.experimental.pallas import tpu as pltpu
from jax.sharding import PartitionSpec as P

MESH = pl.DeviceIdType.MESH
epsilon = 1e-05
momentum = 0.9
average_decay = 0.9
matrix_rate = 0.0004
small_rate = 0.005
WIDTH = 1536
CHANNELS = 384
HIDDEN = 1728
PADDED = 1792
ROWS = 512
QUARTER = 128
SLOT_ROWS = 256
BLOCK = 48


class Place:
    def __init__(self):
        self.shard = lax.axis_index("shard")
        self.ctx = lax.axis_index("ctx")
        self.tp = lax.axis_index("tp")
        self.y = self.shard * 2 + lax.div(self.ctx, 8)
        self.z = lax.rem(lax.div(self.ctx, 2), 4)
        self.core = lax.rem(self.ctx, 2)
        self.first = self.y * (1 - self.core) + self.z * self.core
        self.second = self.z * (1 - self.core) + self.y * self.core

    def turn(self, value, by):
        return lax.rem(value + by + 4, 4)

    def device(self, y, z, core):
        return (lax.div(y, 2), lax.rem(y, 2) * 8 + z * 2 + core, self.tp)

    def grid_device(self, first, second):
        y = first * (1 - self.core) + second * self.core
        z = second * (1 - self.core) + first * self.core
        return self.device(y, z, self.core)

    def block(self, first, second):
        y = first * (1 - self.core) + second * self.core
        z = second * (1 - self.core) + first * self.core
        return y * 8 + z * 2 + self.core

    def along_first(self, by):
        return self.grid_device(self.turn(self.first, by), self.second)

    def along_second(self, by):
        return self.grid_device(self.first, self.turn(self.second, by))

    def along_tp(self, by):
        return (self.shard, self.ctx, self.turn(self.tp, by))

    def along_ctx(self, by):
        return (self.shard, lax.rem(self.ctx + by + 16, 16), self.tp)

    def sibling(self):
        return self.device(self.y, self.z, 1 - self.core)

    def greet(self):
        barrier = pltpu.get_barrier_semaphore()
        friends = [self.sibling(), self.along_ctx(1), self.along_ctx(-1)]
        for by in (1, 2, 3):
            friends += [self.along_first(by), self.along_second(by), self.along_tp(by)]
        for friend in friends:
            pl.semaphore_signal(barrier, inc=1, device_id=friend, device_id_type=MESH)
        pl.semaphore_wait(barrier, len(friends))


def remote(source, target, sems, at, device):
    return pltpu.make_async_remote_copy(
        src_ref=source,
        dst_ref=target,
        send_sem=sems.at[0, at],
        recv_sem=sems.at[1, at],
        device_id=device,
        device_id_type=MESH,
    )


class Gather:
    SEMS = 31

    def __init__(self, place, local, whole, sems):
        self.place, self.local, self.whole, self.sems = place, local, whole, sems
        self.sent = []

    def send(self, source, block, at, device):
        copy = remote(source, self.whole.at[:, block], self.sems, at, device)
        copy.start()
        self.sent.append(copy)

    def arrived(self, block, at):
        spot = self.whole.at[:, block]
        remote(spot, spot, self.sems, at, self.place.sibling()).wait_recv()

    def start(self):
        p = self.place
        mine = p.block(p.first, p.second)
        for by in (1, 2, 3):
            self.send(self.local, mine, by - 1, p.along_first(by))
        for by in (1, 2, 3):
            self.send(self.local, mine, 3 + by - 1, p.along_second(by))
        self.send(self.local, mine, 15, p.sibling())

    def forward_first(self):
        p = self.place
        for back in (1, 3, 2):
            block = p.block(p.turn(p.first, -back), p.second)
            self.arrived(block, back - 1)
            for by in (1, 2, 3):
                self.send(self.whole.at[:, block], block, 3 + back * 3 + by - 1, p.along_second(by))
            self.send(self.whole.at[:, block], block, 15 + back * 4, p.sibling())

    def forward_second(self):
        p = self.place
        for back in (0, 1, 3, 2):
            for by in (1, 3, 2):
                block = p.block(p.turn(p.first, -back), p.turn(p.second, -by))
                self.arrived(block, 3 + back * 3 + by - 1)
                self.send(self.whole.at[:, block], block, 15 + back * 4 + by, p.sibling())

    def finish(self):
        p = self.place
        for back in range(4):
            for by in range(4):
                self.arrived(p.block(p.turn(p.first, -back), p.turn(p.second, -by)), 15 + back * 4 + by)
        for copy in self.sent:
            copy.wait_send()


def dot(left, right):
    return jnp.dot(left, right, preferred_element_type=jnp.float32)


def dot_t(left, right):
    return lax.dot_general(left, right, (((1,), (1,)), ((), ())), preferred_element_type=jnp.float32)


def forward_kernel(
    io_local,
    gud_local,
    x,
    gains,
    taps,
    io_full,
    gud_full,
    second_low,
    residual,
    projected,
    product,
    convolved,
    gated,
    input_low,
    x_send,
    x_recv,
    own_part,
    io_sems,
    gud_sems,
    x_sems,
    local_sems,
):
    place = Place()
    place.greet()
    mine = place.block(place.first, place.second)
    keep = [
        pltpu.make_async_copy(io_local, io_full.at[:, mine], local_sems.at[0]),
        pltpu.make_async_copy(gud_local, gud_full.at[:, mine], local_sems.at[1]),
    ]
    for copy in keep:
        copy.start()
    io = Gather(place, io_local, io_full, io_sems)
    gud = Gather(place, gud_local, gud_full, gud_sems)
    io.start()

    @pl.loop(0, ROWS, step=64)
    def _(at):
        values = x[pl.ds(at, 64), :].astype(jnp.float32)
        inverse = lax.rsqrt(jnp.mean(values * values, axis=-1, keepdims=True) + epsilon)
        input_low[pl.ds(at, 64), :] = (values * inverse * gains[0:1, :]).astype(jnp.bfloat16)

    io.forward_first()
    io.forward_second()
    gud.start()
    io.finish()
    keep[0].wait()

    for member in (0, 2):
        projected[member] = dot(input_low[...], io_full[member].reshape(WIDTH, CHANNELS))
    product[:, 8:, :] = (projected[0] * projected[2]).reshape(2, SLOT_ROWS, CHANNELS)
    halo = remote(
        product.at[:, pl.ds(SLOT_ROWS, 8)], product.at[:, pl.ds(0, 8)], x_sems, 6, place.along_ctx(1)
    )
    halo.start()
    projected[1] = dot(input_low[...], io_full[1].reshape(WIDTH, CHANNELS))
    halo.wait()
    product[:, :8, :] = jnp.where(place.ctx > 0, product[:, :8, :], 0.0)
    convolved[...] = (
        taps[0:1, :] * product[:, 6 : 6 + SLOT_ROWS, :]
        + taps[1:2, :] * product[:, 7 : 7 + SLOT_ROWS, :]
        + taps[2:3, :] * product[:, 8 : 8 + SLOT_ROWS, :]
    ).reshape(ROWS, CHANNELS)
    gated[...] = (projected[1] * convolved[...]).astype(jnp.bfloat16)

    sent = []
    for by in (2, 1, 3, 0):
        row = place.turn(place.tp, by) * QUARTER
        part = dot_t(gated[pl.ds(row, QUARTER), :], io_full[3].reshape(WIDTH, CHANNELS))
        if by == 0:
            own_part[...] = part
        else:
            x_send[by - 1] = part.astype(jnp.bfloat16)
            copy = remote(x_send.at[by - 1], x_recv.at[by - 1], x_sems, by - 1, place.along_tp(by))
            copy.start()
            sent.append(copy)
    gud.forward_first()
    for copy in sent:
        copy.wait_recv()
    own_rows = pl.ds(place.tp * QUARTER, QUARTER)
    total = (
        own_part[...]
        + x_recv[0].astype(jnp.float32)
        + x_recv[1].astype(jnp.float32)
        + x_recv[2].astype(jnp.float32)
    )
    stream = x[own_rows, :].astype(jnp.float32) + total
    residual[...] = stream
    inverse = lax.rsqrt(jnp.mean(stream * stream, axis=-1, keepdims=True) + epsilon)
    second_low[own_rows, :] = (stream * inverse * gains[1:2, :]).astype(jnp.bfloat16)
    for by in (2, 1, 3):
        spot = second_low.at[own_rows]
        copy = remote(spot, spot, x_sems, 3 + by - 1, place.along_tp(by))
        copy.start()
        sent.append(copy)
    gud.forward_second()
    gud.finish()
    keep[1].wait()
    for copy in sent[3:]:
        copy.wait_recv()
    for copy in sent:
        copy.wait_send()


def forward(io_local, gud_local, x, gains, taps):
    vmem = pl.BlockSpec(memory_space=pltpu.VMEM)
    hbm = pl.BlockSpec(memory_space=pl.ANY)
    f32, b16 = jnp.float32, jnp.bfloat16
    return pl.pallas_call(
        forward_kernel,
        out_shape=(
            jax.ShapeDtypeStruct((4, 32, BLOCK, CHANNELS), b16),
            jax.ShapeDtypeStruct((3, 32, BLOCK, PADDED), b16),
            jax.ShapeDtypeStruct((ROWS, WIDTH), b16),
            jax.ShapeDtypeStruct((QUARTER, WIDTH), f32),
            jax.ShapeDtypeStruct((3, ROWS, CHANNELS), f32),
            jax.ShapeDtypeStruct((2, 8 + SLOT_ROWS, CHANNELS), f32),
            jax.ShapeDtypeStruct((ROWS, CHANNELS), f32),
            jax.ShapeDtypeStruct((ROWS, CHANNELS), b16),
        ),
        in_specs=[hbm, hbm, vmem, vmem, vmem],
        out_specs=(vmem, hbm, vmem, vmem, vmem, vmem, vmem, vmem),
        scratch_shapes=[
            pltpu.VMEM((ROWS, WIDTH), b16),
            pltpu.VMEM((3, QUARTER, WIDTH), b16),
            pltpu.VMEM((3, QUARTER, WIDTH), b16),
            pltpu.VMEM((QUARTER, WIDTH), f32),
            pltpu.SemaphoreType.DMA((2, Gather.SEMS)),
            pltpu.SemaphoreType.DMA((2, Gather.SEMS)),
            pltpu.SemaphoreType.DMA((2, 7)),
            pltpu.SemaphoreType.DMA((2,)),
        ],
        compiler_params=pltpu.CompilerParams(
            collective_id=0, has_side_effects=True, vmem_limit_bytes=56 * 2**20
        ),
        name="forward",
    )(io_local, gud_local, x, gains, taps)


def from_behind(value, axis, steps):
    count = lax.axis_size(axis)
    leading, last = (max(0, -steps), min(count, count - steps))
    return lax.ppermute(value, axis, [(source, source + steps) for source in range(leading, last)])


def from_everyone(array, axis):
    copies = jnp.broadcast_to(array, (lax.axis_size(axis), *array.shape))
    return lax.all_to_all(copies, axis, split_axis=0, concat_axis=0, tiled=True)


def taken_together(array, axis):
    everything = from_everyone(array, axis)
    return jnp.sum(everything, axis=0)


def together(arrays, axis):
    flat, at, outs = (jnp.concatenate([a.reshape(-1) for a in arrays]), 0, [])
    total = taken_together(flat, axis)
    for a in arrays:
        outs.append(total[at : at + a.size].reshape(a.shape))
        at += a.size
    return tuple(outs)


def normalize(values):
    inverse = lax.rsqrt(jnp.mean(values * values, axis=-1, keepdims=True) + epsilon)
    return (values * inverse, inverse)


def norm_back(grad_normed, normed, inverse, gain_row):
    scaled = grad_normed * gain_row
    return inverse * (scaled - normed * jnp.mean(scaled * normed, axis=-1, keepdims=True))


def contract_rows(left_side, right_side):
    return lax.dot_general(
        left_side, right_side, (((0,), (0,)), ((), ())), preferred_element_type=jnp.float32
    )


def contract_cols(left_side, right_side):
    return lax.dot_general(
        left_side, right_side, (((1,), (1,)), ((), ())), preferred_element_type=jnp.float32
    )


def nesterov(weight, moment, average, gradient, step_rate):
    moment_new = momentum * moment + gradient
    weight_new = weight - step_rate * (gradient + momentum * moment_new)
    average_new = average_decay * average + (1.0 - average_decay) * weight_new
    return (moment_new, weight_new, average_new)


def on_device(
    hidden,
    lengths,
    cotangent,
    in_weight,
    in_moment,
    in_average,
    out_weight,
    out_moment,
    out_average,
    gate_up_weight,
    gate_up_moment,
    gate_up_average,
    down_weight,
    down_moment,
    down_average,
    norm_gains,
    gain_moment,
    gain_average,
    conv_taps,
    taps_moment,
    taps_average,
):
    b16 = jnp.bfloat16
    io_local = jnp.concatenate([in_weight.astype(b16), out_weight.astype(b16).T[None]], axis=0)
    gud_local = jnp.concatenate(
        [gate_up_weight.astype(b16), down_weight.astype(b16).T[None]], axis=0
    )
    gud_local = jnp.pad(gud_local, ((0, 0), (0, 0), (0, PADDED - HIDDEN)))
    slot_count, seq_len, model_width = hidden.shape
    row_count = slot_count * seq_len
    io_full, gud_full, second_low, residual_own, projected, extended, convolved, gated_low = forward(
        io_local, gud_local, hidden.reshape(row_count, model_width), norm_gains, conv_taps
    )
    in_full = io_full[:3].reshape(3, WIDTH, CHANNELS)
    out_full = io_full[3].reshape(WIDTH, CHANNELS).T
    gate_up_full = gud_full[:2].reshape(2, WIDTH, PADDED)[:, :, :HIDDEN]
    down_full = gud_full[2].reshape(WIDTH, PADDED)[:, :HIDDEN].T
    channels = CHANNELS
    stream = hidden.astype(jnp.float32).reshape(row_count, model_width)
    positions = lax.axis_index("ctx") * seq_len + jnp.arange(seq_len, dtype=jnp.int32)
    valid_rows = (positions[None, :] < lengths[:, None]).astype(jnp.float32).reshape(row_count, 1)
    normed_one, inverse_one = normalize(stream)
    input_low = (normed_one * norm_gains[0]).astype(jnp.bfloat16)
    extended = extended[:, 6:]
    residual = lax.all_gather(residual_own, "tp", axis=0, tiled=True)
    normed_two, inverse_two = normalize(residual)
    gate_up = jnp.einsum(
        "rd,kdf->krf", second_low, gate_up_full, preferred_element_type=jnp.float32
    )
    sigmoid_gate = jax.nn.sigmoid(gate_up[0])
    activated = gate_up[0] * sigmoid_gate
    inner_low = (activated * gate_up[1]).astype(jnp.bfloat16)
    branch = lax.psum(jnp.dot(inner_low, down_full, preferred_element_type=jnp.float32), "tp")
    block_output = (
        (residual + branch).astype(jnp.bfloat16).reshape(slot_count, seq_len, model_width)
    )
    grad_out = cotangent.astype(jnp.float32).reshape(row_count, model_width) * valid_rows
    grad_low = grad_out.astype(jnp.bfloat16)
    grad_inner = contract_cols(grad_low, down_full)
    down_grad = contract_rows(inner_low, grad_low)
    grad_gate = grad_inner * gate_up[1] * sigmoid_gate * (1.0 + gate_up[0] * (1.0 - sigmoid_gate))
    grad_up = grad_inner * activated
    grad_gate_up = jnp.stack([grad_gate, grad_up]).astype(jnp.bfloat16)
    gate_up_grad = jnp.einsum(
        "rd,krf->kdf", second_low, grad_gate_up, preferred_element_type=jnp.float32
    )
    grad_second = lax.psum(
        jnp.einsum("krf,kdf->rd", grad_gate_up, gate_up_full, preferred_element_type=jnp.float32),
        "tp",
    )
    gain_two = jnp.sum(grad_second * normed_two, axis=0)
    grad_residual = grad_out + norm_back(grad_second, normed_two, inverse_two, norm_gains[1])
    residual_low = grad_residual.astype(jnp.bfloat16)
    grad_gated = contract_cols(residual_low, out_full)
    out_grad = contract_rows(gated_low, residual_low)
    grad_cproj = grad_gated * convolved
    grad_conv = (grad_gated * projected[1]).reshape(slot_count, seq_len, channels)
    following = from_behind(grad_conv[:, :2, :], "ctx", -1)
    grad_extended = jnp.concatenate([grad_conv, following], axis=1)
    grad_product = (
        conv_taps[2] * grad_extended[:, :seq_len]
        + conv_taps[1] * grad_extended[:, 1 : seq_len + 1]
        + conv_taps[0] * grad_extended[:, 2:]
    ).reshape(row_count, channels)
    taps_grad = jnp.stack(
        [
            jnp.sum(grad_conv * extended[:, offset : offset + seq_len], axis=(0, 1))
            for offset in range(3)
        ]
    )
    grad_projected = jnp.stack(
        [grad_product * projected[2], grad_cproj, grad_product * projected[0]]
    ).astype(jnp.bfloat16)
    in_grad = jnp.einsum(
        "rd,kre->kde", input_low, grad_projected, preferred_element_type=jnp.float32
    )
    grad_first = lax.psum(
        jnp.einsum("kre,kde->rd", grad_projected, in_full, preferred_element_type=jnp.float32), "tp"
    )
    gain_one = jnp.sum(grad_first * normed_one, axis=0)
    input_grad = (
        grad_residual + norm_back(grad_first, normed_one, inverse_one, norm_gains[0])
    ).reshape(slot_count, seq_len, model_width)
    gain_total, taps_total = together(
        (jnp.stack([gain_one, gain_two]), taps_grad), ("shard", "ctx")
    )
    in_sum, out_sum, gate_up_sum, down_sum = (
        lax.psum_scatter(in_grad, ("shard", "ctx"), scatter_dimension=1, tiled=True),
        lax.psum_scatter(out_grad, ("shard", "ctx"), scatter_dimension=1, tiled=True),
        lax.psum_scatter(gate_up_grad, ("shard", "ctx"), scatter_dimension=1, tiled=True),
        lax.psum_scatter(down_grad, ("shard", "ctx"), scatter_dimension=1, tiled=True),
    )
    in_new = nesterov(in_weight, in_moment, in_average, in_sum, matrix_rate)
    out_new = nesterov(out_weight, out_moment, out_average, out_sum, matrix_rate)
    gate_up_new = nesterov(
        gate_up_weight, gate_up_moment, gate_up_average, gate_up_sum, matrix_rate
    )
    down_new = nesterov(down_weight, down_moment, down_average, down_sum, matrix_rate)
    gain_new = nesterov(norm_gains, gain_moment, gain_average, gain_total, small_rate)
    taps_new = nesterov(conv_taps, taps_moment, taps_average, taps_total, small_rate)
    return (
        block_output,
        input_grad,
        in_new[0],
        in_new[1],
        in_new[2],
        out_new[0],
        out_new[1],
        out_new[2],
        gate_up_new[0],
        gate_up_new[1],
        gate_up_new[2],
        down_new[0],
        down_new[1],
        down_new[2],
        gain_new[0],
        gain_new[1],
        gain_new[2],
        taps_new[0],
        taps_new[1],
        taps_new[2],
    )


def solution(mesh):
    placed = (
        P("shard", "ctx", None),
        P("shard"),
        P("shard", "ctx", None),
        P(None, ("shard", "ctx"), "tp"),
        P(None, ("shard", "ctx"), "tp"),
        P(None, ("shard", "ctx"), "tp"),
        P("tp", ("shard", "ctx")),
        P("tp", ("shard", "ctx")),
        P("tp", ("shard", "ctx")),
        P(None, ("shard", "ctx"), "tp"),
        P(None, ("shard", "ctx"), "tp"),
        P(None, ("shard", "ctx"), "tp"),
        P("tp", ("shard", "ctx")),
        P("tp", ("shard", "ctx")),
        P("tp", ("shard", "ctx")),
        P(),
        P(),
        P(),
        P(None, "tp"),
        P(None, "tp"),
        P(None, "tp"),
    )
    return jax.shard_map(
        on_device,
        mesh=mesh,
        in_specs=placed,
        out_specs=(
            P("shard", "ctx", None),
            P("shard", "ctx", None),
            P(None, ("shard", "ctx"), "tp"),
            P(None, ("shard", "ctx"), "tp"),
            P(None, ("shard", "ctx"), "tp"),
            P("tp", ("shard", "ctx")),
            P("tp", ("shard", "ctx")),
            P("tp", ("shard", "ctx")),
            P(None, ("shard", "ctx"), "tp"),
            P(None, ("shard", "ctx"), "tp"),
            P(None, ("shard", "ctx"), "tp"),
            P("tp", ("shard", "ctx")),
            P("tp", ("shard", "ctx")),
            P("tp", ("shard", "ctx")),
            P(),
            P(),
            P(),
            P(None, "tp"),
            P(None, "tp"),
            P(None, "tp"),
        ),
        check_vma=False,
    )
```

```python
import functools

import jax
import jax.numpy as jnp
from jax import lax
from jax.experimental import pallas as pl
from jax.experimental.pallas import tpu as pltpu
from jax.sharding import PartitionSpec as P

MESH = pl.DeviceIdType.MESH
epsilon = 1e-05
momentum = 0.9
average_decay = 0.9
matrix_rate = 0.0004
small_rate = 0.005
WIDTH = 1536
CHANNELS = 384
HIDDEN = 1728
TILE = 256
PADDED = 1792
ROWS = 512
QUARTER = 128
SLOT_ROWS = 256
BLOCK = 48


class Place:
    def __init__(self):
        self.shard = lax.axis_index("shard")
        self.ctx = lax.axis_index("ctx")
        self.tp = lax.axis_index("tp")
        self.y = self.shard * 2 + lax.div(self.ctx, 8)
        self.z = lax.rem(lax.div(self.ctx, 2), 4)
        self.core = lax.rem(self.ctx, 2)
        self.first = self.y * (1 - self.core) + self.z * self.core
        self.second = self.z * (1 - self.core) + self.y * self.core

    def turn(self, value, by):
        return lax.rem(value + by + 4, 4)

    def device(self, y, z, core):
        return (lax.div(y, 2), lax.rem(y, 2) * 8 + z * 2 + core, self.tp)

    def grid_device(self, first, second):
        y = first * (1 - self.core) + second * self.core
        z = second * (1 - self.core) + first * self.core
        return self.device(y, z, self.core)

    def block(self, first, second):
        y = first * (1 - self.core) + second * self.core
        z = second * (1 - self.core) + first * self.core
        return y * 8 + z * 2 + self.core

    def along_first(self, by):
        return self.grid_device(self.turn(self.first, by), self.second)

    def along_second(self, by):
        return self.grid_device(self.first, self.turn(self.second, by))

    def along_tp(self, by):
        return (self.shard, self.ctx, self.turn(self.tp, by))

    def along_ctx(self, by):
        return (self.shard, lax.rem(self.ctx + by + 16, 16), self.tp)

    def sibling(self):
        return self.device(self.y, self.z, 1 - self.core)

    def greet(self):
        barrier = pltpu.get_barrier_semaphore()
        friends = [self.sibling(), self.along_ctx(1), self.along_ctx(-1)]
        for by in (1, 2, 3):
            friends += [self.along_first(by), self.along_second(by), self.along_tp(by)]
        for friend in friends:
            pl.semaphore_signal(barrier, inc=1, device_id=friend, device_id_type=MESH)
        pl.semaphore_wait(barrier, len(friends))


def remote(source, target, sems, at, device):
    return pltpu.make_async_remote_copy(
        src_ref=source,
        dst_ref=target,
        send_sem=sems.at[0, at],
        recv_sem=sems.at[1, at],
        device_id=device,
        device_id_type=MESH,
    )


class Gather:
    SEMS = 31

    def __init__(self, place, local, whole, sems):
        self.place, self.local, self.whole, self.sems = place, local, whole, sems
        self.sent = []

    def part(self, block):
        return self.whole.at[:, block] if self.whole.ndim == 4 else self.whole.at[block]

    def send(self, source, block, at, device):
        copy = remote(source, self.part(block), self.sems, at, device)
        copy.start()
        self.sent.append(copy)

    def arrived(self, block, at):
        spot = self.part(block)
        remote(spot, spot, self.sems, at, self.place.sibling()).wait_recv()

    def start(self):
        p = self.place
        mine = p.block(p.first, p.second)
        for by in (1, 2, 3):
            self.send(self.local, mine, by - 1, p.along_first(by))
        for by in (1, 2, 3):
            self.send(self.local, mine, 3 + by - 1, p.along_second(by))
        self.send(self.local, mine, 15, p.sibling())

    def forward_first(self):
        p = self.place
        for back in (1, 3, 2):
            block = p.block(p.turn(p.first, -back), p.second)
            self.arrived(block, back - 1)
            for by in (1, 2, 3):
                self.send(self.part(block), block, 3 + back * 3 + by - 1, p.along_second(by))
            self.send(self.part(block), block, 15 + back * 4, p.sibling())

    def forward_second(self):
        p = self.place
        for back in (0, 1, 3, 2):
            for by in (1, 3, 2):
                block = p.block(p.turn(p.first, -back), p.turn(p.second, -by))
                self.arrived(block, 3 + back * 3 + by - 1)
                self.send(self.part(block), block, 15 + back * 4 + by, p.sibling())

    def finish(self):
        p = self.place
        for back in range(4):
            for by in range(4):
                self.arrived(p.block(p.turn(p.first, -back), p.turn(p.second, -by)), 15 + back * 4 + by)
        for copy in self.sent:
            copy.wait_send()


class Scatter:
    SEMS = 7

    def __init__(self, place, partial, width, recv, out, stage, sems, local_sems):
        self.place, self.width, self.out = place, width, out
        self.sib_recv, self.second_recv, self.first_recv = recv
        self.stage, self.sems, self.local_sems = stage, sems, local_sems
        columns = pl.ds(0, width)
        self.blocks = partial.reshape(16, 2, BLOCK, PADDED).at[:, :, :, columns]
        self.grid = partial.reshape(4, 4, 2, BLOCK, PADDED).at[:, :, :, :, columns]
        self.sent = []

    def mine(self, first, second):
        return lax.div(self.place.block(first, second), 2)

    def to_sibling(self):
        p = self.place
        copy = remote(self.blocks.at[:, 1 - p.core], self.sib_recv, self.sems, 0, p.sibling())
        copy.start()
        self.sent.append(copy)

    def fetch(self, source, count):
        target = self.stage.at[pl.ds(0, count), :, pl.ds(0, self.width)]
        copy = pltpu.make_async_copy(source, target, self.local_sems.at[0])
        copy.start()
        copy.wait()

    def along_second(self):
        p = self.place
        self.sent[0].wait_recv()
        self.fetch(self.sib_recv, 16)

        @pl.loop(0, 16)
        def _(at):
            both = self.blocks[at, p.core].astype(jnp.float32)
            both = both + self.stage[at, :, : self.width].astype(jnp.float32)
            self.blocks[at, p.core] = both.astype(jnp.bfloat16)

        for by in (1, 3, 2):
            there = p.turn(p.second, by)
            spot = self.second_recv.at[pl.ds((by - 1) * 4, 4)]
            flat = remote(self.grid.at[:, there, 0], spot, self.sems, by, p.along_second(by))
            tall = remote(self.grid.at[there, :, 1], spot, self.sems, by, p.along_second(by))

            @pl.when(p.core == 0)
            def _():
                flat.start()

            @pl.when(p.core == 1)
            def _():
                tall.start()

            self.sent.append(flat)

    def along_first(self):
        p = self.place
        for copy in self.sent[1:4]:
            copy.wait_recv()
        self.fetch(self.second_recv, 12)

        @pl.loop(0, 4)
        def _(first):
            at = self.mine(first, p.second)
            total = self.blocks[at, p.core].astype(jnp.float32)
            for by in range(3):
                total = total + self.stage[by * 4 + first, :, : self.width].astype(jnp.float32)
            self.blocks[at, p.core] = total.astype(jnp.bfloat16)

        for by in (1, 3, 2):
            source = self.blocks.at[self.mine(p.turn(p.first, by), p.second), p.core]
            copy = remote(
                source, self.first_recv.at[by - 1], self.sems, 3 + by, p.along_first(by)
            )
            copy.start()
            self.sent.append(copy)

    def finish(self):
        p = self.place
        for copy in self.sent[4:7]:
            copy.wait_recv()
        total = self.blocks[self.mine(p.first, p.second), p.core].astype(jnp.float32)
        for by in range(3):
            total = total + self.first_recv[by].astype(jnp.float32)
        self.out[...] = total

    def drain(self):
        for copy in self.sent:
            copy.wait_send()


class TpSum:
    def __init__(self, place, send, recv, own, sems):
        self.place, self.send, self.recv, self.own, self.sems = place, send, recv, own, sems
        self.sent = []

    def give(self, values, column, width, slot):
        p = self.place
        columns = pl.ds(column, width)
        self.send[:, columns] = values.astype(jnp.bfloat16)
        for by in (2, 1, 3):
            rows = pl.ds(pl.multiple_of(p.turn(p.tp, by) * QUARTER, QUARTER), QUARTER)
            copy = remote(
                self.send.at[rows, columns],
                self.recv.at[by - 1, :, columns],
                self.sems,
                slot * 3 + by - 1,
                p.along_tp(by),
            )
            copy.start()
            self.sent.append(copy)

    def take(self):
        p = self.place
        for copy in self.sent:
            copy.wait_recv()
        rows = pl.ds(pl.multiple_of(p.tp * QUARTER, QUARTER), QUARTER)
        total = self.send[rows, :].astype(jnp.float32)
        for by in range(3):
            total = total + self.recv[by].astype(jnp.float32)
        return total

    def drain(self):
        for copy in self.sent:
            copy.wait_send()


class TpSpread:
    def __init__(self, place, source, whole, sems):
        self.place, self.source, self.whole, self.sems = place, source, whole, sems
        self.sent = []

    def start(self):
        p = self.place
        rows = pl.ds(pl.multiple_of(p.tp * QUARTER, QUARTER), QUARTER)
        for by in (2, 1, 3):
            copy = remote(self.source, self.whole.at[rows], self.sems, by - 1, p.along_tp(by))
            copy.start()
            self.sent.append(copy)

    def finish(self):
        for copy in self.sent:
            copy.wait_recv()

    def drain(self):
        for copy in self.sent:
            copy.wait_send()


def dot(left, right):
    return jnp.dot(left, right, preferred_element_type=jnp.float32)


def dot_t(left, right):
    return lax.dot_general(
        left, right, (((1,), (1,)), ((), ())), preferred_element_type=jnp.float32
    )


def turned(source, target):
    @pl.loop(0, WIDTH // TILE)
    def _(at):
        at = pl.multiple_of(at * TILE, TILE)
        target[pl.ds(at, TILE), :] = source[:, pl.ds(at, TILE)].T


def own_rows_of(place):
    return pl.ds(pl.multiple_of(place.tp * QUARTER, QUARTER), QUARTER)


def forward_kernel(
    io_local,
    gud_local,
    x,
    gains,
    taps,
    io_full,
    gud_full,
    second_low,
    residual,
    projected,
    product,
    convolved,
    gated,
    input_low,
    x_send,
    x_recv,
    io_sems,
    gud_sems,
    sum_sems,
    spread_sems,
    halo_sems,
    local_sems,
):
    place = Place()
    place.greet()
    mine = place.block(place.first, place.second)
    keep = [
        pltpu.make_async_copy(io_local, io_full.at[mine], local_sems.at[0]),
        pltpu.make_async_copy(gud_local, gud_full.at[:, mine], local_sems.at[1]),
    ]
    for copy in keep:
        copy.start()
    io = Gather(place, io_local, io_full, io_sems)
    gud = Gather(place, gud_local, gud_full, gud_sems)
    io.start()

    @pl.loop(0, ROWS, step=64)
    def _(at):
        values = x[pl.ds(at, 64), :].astype(jnp.float32)
        inverse = lax.rsqrt(jnp.mean(values * values, axis=-1, keepdims=True) + epsilon)
        input_low[pl.ds(at, 64), :] = (values * inverse * gains[0:1, :]).astype(jnp.bfloat16)

    io.forward_first()
    io.forward_second()
    gud.start()
    io.finish()
    keep[0].wait()

    def weight(member):
        return io_full.reshape(WIDTH, 4 * CHANNELS)[:, member * CHANNELS : (member + 1) * CHANNELS]

    for member in (0, 2):
        projected[member] = dot(input_low[...], weight(member))
    product[:, 8:, :] = (projected[0] * projected[2]).reshape(2, SLOT_ROWS, CHANNELS)
    halo = remote(
        product.at[:, pl.ds(SLOT_ROWS, 8)],
        product.at[:, pl.ds(0, 8)],
        halo_sems,
        0,
        place.along_ctx(1),
    )
    halo.start()
    projected[1] = dot(input_low[...], weight(1))
    halo.wait()
    product[:, :8, :] = jnp.where(place.ctx > 0, product[:, :8, :], 0.0)
    convolved[...] = (
        taps[0:1, :] * product[:, 6 : 6 + SLOT_ROWS, :]
        + taps[1:2, :] * product[:, 7 : 7 + SLOT_ROWS, :]
        + taps[2:3, :] * product[:, 8 : 8 + SLOT_ROWS, :]
    ).reshape(ROWS, CHANNELS)
    gated[...] = (projected[1] * convolved[...]).astype(jnp.bfloat16)

    mixed = TpSum(place, x_send, x_recv, None, sum_sems)
    whole = io_full.reshape(WIDTH, 4 * CHANNELS)
    for slot in range(3):
        part = dot_t(gated[...], whole[slot * 512 : (slot + 1) * 512, 3 * CHANNELS :])
        mixed.give(part, slot * 512, 512, slot)
    gud.forward_first()
    own_rows = own_rows_of(place)
    stream = x[own_rows, :].astype(jnp.float32) + mixed.take()
    residual[...] = stream
    inverse = lax.rsqrt(jnp.mean(stream * stream, axis=-1, keepdims=True) + epsilon)
    second_low[own_rows, :] = (stream * inverse * gains[1:2, :]).astype(jnp.bfloat16)
    spread = TpSpread(place, second_low.at[own_rows], second_low, spread_sems)
    spread.start()
    gud.forward_second()
    gud.finish()
    keep[1].wait()
    spread.finish()
    spread.drain()
    mixed.drain()


def forward(io_local, gud_local, x, gains, taps):
    vmem = pl.BlockSpec(memory_space=pltpu.VMEM)
    hbm = pl.BlockSpec(memory_space=pl.ANY)
    f32, b16 = jnp.float32, jnp.bfloat16
    return pl.pallas_call(
        forward_kernel,
        out_shape=(
            jax.ShapeDtypeStruct((32, BLOCK, 4 * CHANNELS), b16),
            jax.ShapeDtypeStruct((3, 32, BLOCK, PADDED), b16),
            jax.ShapeDtypeStruct((ROWS, WIDTH), b16),
            jax.ShapeDtypeStruct((QUARTER, WIDTH), f32),
            jax.ShapeDtypeStruct((3, ROWS, CHANNELS), f32),
            jax.ShapeDtypeStruct((2, 8 + SLOT_ROWS, CHANNELS), f32),
            jax.ShapeDtypeStruct((ROWS, CHANNELS), f32),
            jax.ShapeDtypeStruct((ROWS, CHANNELS), b16),
            jax.ShapeDtypeStruct((ROWS, WIDTH), b16),
        ),
        in_specs=[hbm, hbm, vmem, vmem, vmem],
        out_specs=(vmem, hbm, vmem, vmem, vmem, vmem, vmem, vmem, vmem),
        scratch_shapes=[
            pltpu.VMEM((ROWS, WIDTH), b16),
            pltpu.VMEM((3, QUARTER, WIDTH), b16),
            pltpu.SemaphoreType.DMA((2, Gather.SEMS)),
            pltpu.SemaphoreType.DMA((2, Gather.SEMS)),
            pltpu.SemaphoreType.DMA((2, 9)),
            pltpu.SemaphoreType.DMA((2, 3)),
            pltpu.SemaphoreType.DMA((2, 1)),
            pltpu.SemaphoreType.DMA((2,)),
        ],
        compiler_params=pltpu.CompilerParams(
            collective_id=0, has_side_effects=True, vmem_limit_bytes=56 * 2**20
        ),
        name="forward",
    )(io_local, gud_local, x, gains, taps)


def backward_kernel(
    io_full,
    gud_full,
    input_low,
    x,
    cotangent,
    second_low,
    residual,
    projected,
    product,
    convolved,
    gated,
    valid,
    gains,
    taps,
    block_out,
    input_out,
    sib_hbm,
    second_hbm,
    io_sib_hbm,
    io_second_hbm,
    io_grad,
    gud_grad,
    small,
    weights,
    io,
    big,
    grad_proj,
    grad_low,
    x_own,
    turn_a,
    turn_b,
    send_a,
    send_b,
    recv_a,
    recv_b,
    recv_c,
    low_full,
    grad_own,
    block_own,
    input_own,
    conv_grad,
    stage,
    first_recv,
    io_first_recv,
    small_recv,
    weight_sems,
    scatter_sems,
    sum_sems,
    spread_sems,
    halo_sems,
    small_sems,
    local_sems,
):
    f32, b16 = jnp.float32, jnp.bfloat16
    place = Place()
    own_rows = own_rows_of(place)
    tiles = PADDED // TILE
    flat_in = gud_full.reshape(3, WIDTH, PADDED)

    def tile_copy(at):
        columns = pl.ds(pl.multiple_of(at * TILE, TILE), TILE)
        return pltpu.make_async_copy(
            flat_in.at[:, :, columns], weights.at[:, :, columns], weight_sems.at[at]
        )

    io_copy = pltpu.make_async_copy(
        io_full.reshape(WIDTH, 4 * CHANNELS), io, local_sems.at[1]
    )
    low_copy = pltpu.make_async_copy(cotangent, grad_low, local_sems.at[3])
    x_copy = pltpu.make_async_copy(x.at[own_rows], x_own, local_sems.at[4])
    low_copy.start()
    for at in range(tiles):
        tile_copy(at).start()
    io_copy.start()
    x_copy.start()
    place.greet()
    low_copy.wait()
    grad_low[...] = (grad_low[...].astype(f32) * valid[...]).astype(b16)

    @pl.loop(0, tiles)
    def _(at):
        tile_copy(at).wait()
        columns = pl.ds(pl.multiple_of(at * TILE, TILE), TILE)
        gate = dot(second_low[...], weights[0, :, columns])
        up = dot(second_low[...], weights[1, :, columns])
        grad_inner = dot(grad_low[...], weights[2, :, columns])
        sigmoid = jax.nn.sigmoid(gate)
        active = gate * sigmoid
        big[0:ROWS, columns] = (active * up).astype(b16)
        big[ROWS : 2 * ROWS, columns] = (
            grad_inner * up * sigmoid * (1.0 + gate * (1.0 - sigmoid))
        ).astype(b16)
        big[2 * ROWS :, columns] = (grad_inner * active).astype(b16)

    branch = TpSum(place, send_a, recv_a, None, sum_sems.at[0])
    for slot in range(3):
        part = dot_t(big[0:ROWS, :], weights[2, slot * 512 : (slot + 1) * 512, :])
        branch.give(part, slot * 512, 512, slot)
    second = TpSum(place, send_b, recv_b, None, sum_sems.at[1])
    for slot in range(3):
        rows = slice(slot * 512, (slot + 1) * 512)
        part = dot_t(big[ROWS : 2 * ROWS, :], weights[0, rows, :])
        part = part + dot_t(big[2 * ROWS :, :], weights[1, rows, :])
        second.give(part, slot * 512, 512, slot)

    def gradient(left, at, member):
        @pl.loop(0, tiles)
        def _(tile):
            columns = pl.ds(pl.multiple_of(tile * TILE, TILE), TILE)
            weights[at, :, columns] = dot(
                left[...], big[member * ROWS : (member + 1) * ROWS, columns]
            ).astype(b16)

    def piece(at):
        return Scatter(
            place,
            weights.at[at],
            PADDED,
            (sib_hbm.at[at], second_hbm.at[at], first_recv.at[at]),
            gud_grad.at[at],
            stage,
            scatter_sems.at[at],
            local_sems,
        )

    gate_piece, up_piece, down_piece = piece(0), piece(1), piece(2)
    turned(grad_low, turn_a)
    gradient(turn_a, 2, 0)
    down_piece.to_sibling()
    turned(second_low, turn_b)
    gradient(turn_b, 0, 1)
    gate_piece.to_sibling()
    down_piece.along_second()
    gradient(turn_b, 1, 2)
    up_piece.to_sibling()
    gate_piece.along_second()

    stream = residual[...]
    block_own[...] = (stream + branch.take()).astype(b16)
    branch.drain()

    def norm_of(values):
        inverse = lax.rsqrt(jnp.mean(values * values, axis=-1, keepdims=True) + epsilon)
        return values * inverse, inverse

    normed, inverse = norm_of(stream)
    grad_second = second.take()
    small[...] = jnp.zeros_like(small)
    small[1:2, :] = jnp.sum(grad_second * normed, axis=0, keepdims=True)
    scaled = grad_second * gains[1:2, :]
    grad_stream = grad_low[own_rows, :].astype(f32) + inverse * (
        scaled - normed * jnp.mean(scaled * normed, axis=-1, keepdims=True)
    )
    grad_own[...] = grad_stream
    low_full[own_rows, :] = grad_stream.astype(b16)
    low_spread = TpSpread(place, low_full.at[own_rows], low_full, spread_sems.at[0])
    low_spread.start()
    block_keep = pltpu.make_async_copy(block_own, block_out.at[own_rows], local_sems.at[2])
    block_keep.start()
    block_spread = TpSpread(place, block_own, block_out, spread_sems.at[1])
    block_spread.start()
    up_piece.along_second()
    second.drain()
    input_copy = pltpu.make_async_copy(input_low, send_b, local_sems.at[5])
    input_copy.start()
    down_piece.along_first()
    gate_piece.along_first()
    low_spread.finish()
    io_copy.wait()

    grad_gated = dot(low_full[...], io[:, 3 * CHANNELS :])
    conv_grad[:, :SLOT_ROWS, :] = (grad_gated * projected[1]).reshape(2, SLOT_ROWS, CHANNELS)
    halo = remote(
        conv_grad.at[:, pl.ds(0, 8)],
        conv_grad.at[:, pl.ds(SLOT_ROWS, 8)],
        halo_sems,
        0,
        place.along_ctx(-1),
    )
    halo.start()
    grad_proj[:, CHANNELS : 2 * CHANNELS] = (grad_gated * convolved[...]).astype(b16)
    own_columns = pl.ds(pl.multiple_of(place.tp * CHANNELS, QUARTER), CHANNELS)
    for tap in range(3):
        small[2 + tap : 3 + tap, own_columns] = jnp.sum(
            conv_grad[:, :SLOT_ROWS, :] * product[:, 6 + tap : 6 + tap + SLOT_ROWS, :], axis=(0, 1)
        ).reshape(1, CHANNELS)
    halo.wait()
    conv_grad[:, SLOT_ROWS:, :] = jnp.where(place.ctx < 15, conv_grad[:, SLOT_ROWS:, :], 0.0)
    grad_product = (
        taps[2:3, :] * conv_grad[:, 0:SLOT_ROWS, :]
        + taps[1:2, :] * conv_grad[:, 1 : 1 + SLOT_ROWS, :]
        + taps[0:1, :] * conv_grad[:, 2 : 2 + SLOT_ROWS, :]
    ).reshape(ROWS, CHANNELS)
    grad_proj[:, 0:CHANNELS] = (grad_product * projected[2]).astype(b16)
    grad_proj[:, 2 * CHANNELS : 3 * CHANNELS] = (grad_product * projected[0]).astype(b16)
    first = TpSum(place, send_a, recv_c, None, sum_sems.at[2])
    for slot in range(3):
        part = dot_t(
            grad_proj[...], io[slot * 512 : (slot + 1) * 512, : 3 * CHANNELS]
        )
        first.give(part, slot * 512, 512, slot)

    input_copy.wait()
    turned(send_b, turn_a)
    turned(low_full, turn_b)
    for member in range(3):
        columns = slice(member * CHANNELS, (member + 1) * CHANNELS)
        big[:, columns] = dot(turn_a[...], grad_proj[:, columns]).astype(b16)
    big[:, 3 * CHANNELS : 4 * CHANNELS] = dot(turn_b[...], gated[...]).astype(b16)
    io_piece = Scatter(
        place,
        big,
        4 * CHANNELS,
        (io_sib_hbm, io_second_hbm, io_first_recv),
        io_grad,
        stage,
        scatter_sems.at[3],
        local_sems,
    )
    io_piece.to_sibling()
    up_piece.along_first()
    io_piece.along_second()

    x_copy.wait()
    normed, inverse = norm_of(x_own[...].astype(f32))
    grad_first = first.take()
    small[0:1, :] = jnp.sum(grad_first * normed, axis=0, keepdims=True)
    scaled = grad_first * gains[0:1, :]
    input_own[...] = (
        grad_own[...]
        + inverse * (scaled - normed * jnp.mean(scaled * normed, axis=-1, keepdims=True))
    ).astype(b16)
    input_keep = pltpu.make_async_copy(input_own, input_out.at[own_rows], local_sems.at[6])
    input_keep.start()
    input_spread = TpSpread(place, input_own, input_out, spread_sems.at[2])
    input_spread.start()

    def exchange(start, devices):
        copies = [
            remote(small, small_recv.at[start + at], small_sems, start + at, device)
            for at, device in enumerate(devices)
        ]
        for copy in copies:
            copy.start()
        for copy in copies:
            copy.wait()
        total = small[...]
        for at in range(len(devices)):
            total = total + small_recv[start + at]
        small[...] = total

    exchange(0, [place.sibling()])
    io_piece.along_first()
    exchange(1, [place.along_tp(by) for by in (1, 2, 3)])
    down_piece.finish()
    gate_piece.finish()
    exchange(4, [place.along_first(by) for by in (1, 2, 3)])
    up_piece.finish()
    exchange(7, [place.along_second(by) for by in (1, 2, 3)])
    io_piece.finish()
    block_keep.wait()
    input_keep.wait()
    block_spread.finish()
    input_spread.finish()
    for part in (low_spread, block_spread, input_spread, first):
        part.drain()
    for part in (down_piece, gate_piece, up_piece, io_piece):
        part.drain()


def backward(*given):
    vmem = pl.BlockSpec(memory_space=pltpu.VMEM)
    hbm = pl.BlockSpec(memory_space=pl.ANY)
    f32, b16 = jnp.float32, jnp.bfloat16
    dma = pltpu.SemaphoreType.DMA
    return pl.pallas_call(
        backward_kernel,
        out_shape=(
            jax.ShapeDtypeStruct((ROWS, WIDTH), b16),
            jax.ShapeDtypeStruct((ROWS, WIDTH), b16),
            jax.ShapeDtypeStruct((3, 16, BLOCK, PADDED), b16),
            jax.ShapeDtypeStruct((3, 12, BLOCK, PADDED), b16),
            jax.ShapeDtypeStruct((16, BLOCK, 4 * CHANNELS), b16),
            jax.ShapeDtypeStruct((12, BLOCK, 4 * CHANNELS), b16),
            jax.ShapeDtypeStruct((BLOCK, 4 * CHANNELS), f32),
            jax.ShapeDtypeStruct((3, BLOCK, PADDED), f32),
            jax.ShapeDtypeStruct((8, WIDTH), f32),
        ),
        in_specs=[hbm] * 5 + [vmem] * 9,
        out_specs=(hbm,) * 6 + (vmem,) * 3,
        scratch_shapes=[
            pltpu.VMEM((3, WIDTH, PADDED), b16),
            pltpu.VMEM((WIDTH, 4 * CHANNELS), b16),
            pltpu.VMEM((WIDTH, PADDED), b16),
            pltpu.VMEM((ROWS, 3 * CHANNELS), b16),
            pltpu.VMEM((ROWS, WIDTH), b16),
            pltpu.VMEM((QUARTER, WIDTH), b16),
            pltpu.VMEM((WIDTH, ROWS), b16),
            pltpu.VMEM((WIDTH, ROWS), b16),
            pltpu.VMEM((ROWS, WIDTH), b16),
            pltpu.VMEM((ROWS, WIDTH), b16),
            pltpu.VMEM((3, QUARTER, WIDTH), b16),
            pltpu.VMEM((3, QUARTER, WIDTH), b16),
            pltpu.VMEM((3, QUARTER, WIDTH), b16),
            pltpu.VMEM((ROWS, WIDTH), b16),
            pltpu.VMEM((QUARTER, WIDTH), f32),
            pltpu.VMEM((QUARTER, WIDTH), b16),
            pltpu.VMEM((QUARTER, WIDTH), b16),
            pltpu.VMEM((2, SLOT_ROWS + 8, CHANNELS), f32),
            pltpu.VMEM((16, BLOCK, PADDED), b16),
            pltpu.VMEM((3, 3, BLOCK, PADDED), b16),
            pltpu.VMEM((3, BLOCK, 4 * CHANNELS), b16),
            pltpu.VMEM((10, 8, WIDTH), f32),
            dma((PADDED // TILE,)),
            dma((4, 2, Scatter.SEMS)),
            dma((3, 2, 9)),
            dma((3, 2, 3)),
            dma((2, 1)),
            dma((2, 10)),
            dma((7,)),
        ],
        compiler_params=pltpu.CompilerParams(
            collective_id=1, has_side_effects=True, vmem_limit_bytes=62 * 2**20
        ),
        name="backward",
    )(*given)


def nesterov(weight, moment, average, gradient, step_rate):
    moment_new = momentum * moment + gradient
    weight_new = weight - step_rate * (gradient + momentum * moment_new)
    average_new = average_decay * average + (1.0 - average_decay) * weight_new
    return (moment_new, weight_new, average_new)


def on_device(
    hidden,
    lengths,
    cotangent,
    in_weight,
    in_moment,
    in_average,
    out_weight,
    out_moment,
    out_average,
    gate_up_weight,
    gate_up_moment,
    gate_up_average,
    down_weight,
    down_moment,
    down_average,
    norm_gains,
    gain_moment,
    gain_average,
    conv_taps,
    taps_moment,
    taps_average,
):
    b16 = jnp.bfloat16
    io_local = jnp.concatenate(
        [in_weight[0], in_weight[1], in_weight[2], out_weight.T], axis=1
    ).astype(b16)
    gud_local = jnp.pad(
        jnp.concatenate([gate_up_weight, down_weight.T[None]], axis=0).astype(b16),
        ((0, 0), (0, 0), (0, PADDED - HIDDEN)),
    )
    slot_count, seq_len, model_width = hidden.shape
    row_count = slot_count * seq_len
    x = hidden.reshape(row_count, model_width)
    positions = lax.axis_index("ctx") * seq_len + jnp.arange(seq_len, dtype=jnp.int32)
    valid_rows = (positions[None, :] < lengths[:, None]).astype(jnp.float32).reshape(row_count, 1)
    (
        io_full,
        gud_full,
        second_low,
        residual,
        projected,
        product,
        convolved,
        gated,
        input_low,
    ) = forward(io_local, gud_local, x, norm_gains, conv_taps)
    block_output, input_low_grad, _, _, _, _, io_sum, gud_sum, small = backward(
        io_full,
        gud_full,
        input_low,
        x,
        cotangent.reshape(row_count, model_width),
        second_low,
        residual,
        projected,
        product,
        convolved,
        gated,
        valid_rows,
        norm_gains,
        conv_taps,
    )
    block_output = block_output.reshape(slot_count, seq_len, model_width)
    input_grad = input_low_grad.astype(jnp.float32).reshape(slot_count, seq_len, model_width)
    in_sum = jnp.moveaxis(io_sum[:, : 3 * CHANNELS].reshape(BLOCK, 3, CHANNELS), 1, 0)
    out_sum = io_sum[:, 3 * CHANNELS :].T
    gate_up_sum = gud_sum[:2, :, :HIDDEN]
    down_sum = gud_sum[2, :, :HIDDEN].T
    gain_total = small[:2]
    taps_total = lax.dynamic_slice_in_dim(
        small[2:5], lax.axis_index("tp") * CHANNELS, CHANNELS, axis=1
    )
    in_new = nesterov(in_weight, in_moment, in_average, in_sum, matrix_rate)
    out_new = nesterov(out_weight, out_moment, out_average, out_sum, matrix_rate)
    gate_up_new = nesterov(
        gate_up_weight, gate_up_moment, gate_up_average, gate_up_sum, matrix_rate
    )
    down_new = nesterov(down_weight, down_moment, down_average, down_sum, matrix_rate)
    gain_new = nesterov(norm_gains, gain_moment, gain_average, gain_total, small_rate)
    taps_new = nesterov(conv_taps, taps_moment, taps_average, taps_total, small_rate)
    return (
        block_output,
        input_grad,
        in_new[0],
        in_new[1],
        in_new[2],
        out_new[0],
        out_new[1],
        out_new[2],
        gate_up_new[0],
        gate_up_new[1],
        gate_up_new[2],
        down_new[0],
        down_new[1],
        down_new[2],
        gain_new[0],
        gain_new[1],
        gain_new[2],
        taps_new[0],
        taps_new[1],
        taps_new[2],
    )


def solution(mesh):
    placed = (
        P("shard", "ctx", None),
        P("shard"),
        P("shard", "ctx", None),
        P(None, ("shard", "ctx"), "tp"),
        P(None, ("shard", "ctx"), "tp"),
        P(None, ("shard", "ctx"), "tp"),
        P("tp", ("shard", "ctx")),
        P("tp", ("shard", "ctx")),
        P("tp", ("shard", "ctx")),
        P(None, ("shard", "ctx"), "tp"),
        P(None, ("shard", "ctx"), "tp"),
        P(None, ("shard", "ctx"), "tp"),
        P("tp", ("shard", "ctx")),
        P("tp", ("shard", "ctx")),
        P("tp", ("shard", "ctx")),
        P(),
        P(),
        P(),
        P(None, "tp"),
        P(None, "tp"),
        P(None, "tp"),
    )
    return jax.shard_map(
        on_device,
        mesh=mesh,
        in_specs=placed,
        out_specs=(
            P("shard", "ctx", None),
            P("shard", "ctx", None),
            P(None, ("shard", "ctx"), "tp"),
            P(None, ("shard", "ctx"), "tp"),
            P(None, ("shard", "ctx"), "tp"),
            P("tp", ("shard", "ctx")),
            P("tp", ("shard", "ctx")),
            P("tp", ("shard", "ctx")),
            P(None, ("shard", "ctx"), "tp"),
            P(None, ("shard", "ctx"), "tp"),
            P(None, ("shard", "ctx"), "tp"),
            P("tp", ("shard", "ctx")),
            P("tp", ("shard", "ctx")),
            P("tp", ("shard", "ctx")),
            P(),
            P(),
            P(),
            P(None, "tp"),
            P(None, "tp"),
            P(None, "tp"),
        ),
        check_vma=False,
    )
```

```python
import functools

import jax
import jax.numpy as jnp
from jax import lax
from jax.experimental import pallas as pl
from jax.experimental.pallas import tpu as pltpu
from jax.sharding import PartitionSpec as P

MESH = pl.DeviceIdType.MESH
epsilon = 1e-05
momentum = 0.9
average_decay = 0.9
matrix_rate = 0.0004
small_rate = 0.005
WIDTH = 1536
CHANNELS = 384
HIDDEN = 1728
TILE = 256
EDGE = 16
WIDE = 4 * CHANNELS
PADDED = 1792
ROWS = 512
QUARTER = 128
SLOT_ROWS = 256
BLOCK = 48
HALF = QUARTER // 2


class Place:
    def __init__(self):
        self.shard = lax.axis_index("shard")
        self.ctx = lax.axis_index("ctx")
        self.tp = lax.axis_index("tp")
        self.y = self.shard * 2 + lax.div(self.ctx, 8)
        self.z = lax.rem(lax.div(self.ctx, 2), 4)
        self.core = lax.rem(self.ctx, 2)
        self.first = self.y * (1 - self.core) + self.z * self.core
        self.second = self.z * (1 - self.core) + self.y * self.core

    def turn(self, value, by):
        return lax.rem(value + by + 4, 4)

    def device(self, y, z, core):
        return (lax.div(y, 2), lax.rem(y, 2) * 8 + z * 2 + core, self.tp)

    def grid_device(self, first, second):
        y = first * (1 - self.core) + second * self.core
        z = second * (1 - self.core) + first * self.core
        return self.device(y, z, self.core)

    def block(self, first, second):
        y = first * (1 - self.core) + second * self.core
        z = second * (1 - self.core) + first * self.core
        return y * 8 + z * 2 + self.core

    def along_first(self, by):
        return self.grid_device(self.turn(self.first, by), self.second)

    def along_second(self, by):
        return self.grid_device(self.first, self.turn(self.second, by))

    def along_tp(self, by):
        return (self.shard, self.ctx, self.turn(self.tp, by))

    def along_ctx(self, by, tp=None):
        return (self.shard, lax.rem(self.ctx + by + 16, 16), self.tp if tp is None else tp)

    def sibling(self):
        return self.device(self.y, self.z, 1 - self.core)

    def greet(self):
        barrier = pltpu.get_barrier_semaphore()
        friends = [self.sibling()]
        for tp in range(4):
            friends += [self.along_ctx(1, tp), self.along_ctx(-1, tp)]
        for by in (1, 2, 3):
            friends += [self.along_first(by), self.along_second(by), self.along_tp(by)]
        for friend in friends:
            pl.semaphore_signal(barrier, inc=1, device_id=friend, device_id_type=MESH)
        pl.semaphore_wait(barrier, len(friends))


def remote(source, target, sems, at, device):
    return pltpu.make_async_remote_copy(
        src_ref=source,
        dst_ref=target,
        send_sem=sems.at[0, at],
        recv_sem=sems.at[1, at],
        device_id=device,
        device_id_type=MESH,
    )


class Gather:
    SEMS = 36

    def __init__(self, place, local, whole, sems):
        self.place, self.local, self.whole, self.sems = place, local, whole, sems
        self.half = local.shape[-1] // 2
        self.sent = []

    def part(self, block, half=None):
        spot = self.whole.at[:, block] if self.whole.ndim == 4 else self.whole.at[block]
        if half is None:
            return spot
        columns = pl.ds(half * self.half, self.half)
        return spot.at[:, :, columns] if self.whole.ndim == 4 else spot.at[:, columns]

    def send(self, source, target, at, device):
        copy = remote(source, target, self.sems, at, device)
        copy.start()
        self.sent.append(copy)

    def arrived(self, spot, at):
        remote(spot, spot, self.sems, at, self.place.sibling()).wait_recv()

    def block(self, back, by):
        p = self.place
        return p.block(p.turn(p.first, -back), p.turn(p.second, -by))

    def to_second(self, source, back, by):
        spot = self.part(self.block(back, 0))
        self.send(source, spot, 4 + 4 * back, self.place.along_second(1))
        self.send(source, spot, 5 + 4 * back, self.place.along_second(-1))
        self.to_sibling(source, back, by)

    def to_sibling(self, source, back, by):
        spot = self.part(self.block(back, by))
        self.send(source, spot, 20 + 4 * back + by, self.place.sibling())

    def start(self):
        p = self.place
        spot = self.part(self.block(0, 0))
        self.send(self.local, spot, 0, p.along_first(1))
        self.send(self.local, spot, 1, p.along_first(-1))
        self.to_second(self.local, 0, 0)

    def first(self):
        p = self.place
        for back, at, half, by in ((1, 0, 0, 1), (3, 1, 1, -1)):
            block = self.block(back, 0)
            self.arrived(self.part(block), at)
            piece = self.part(block, half)
            self.send(piece, piece, 2 + half, p.along_first(by))
            self.to_second(self.part(block), back, 0)

    def first_far(self):
        block = self.block(2, 0)
        for half in range(2):
            self.arrived(self.part(block, half), 2 + half)
        self.to_second(self.part(block), 2, 0)

    def second(self, back):
        p = self.place
        for by, half, step in ((1, 0, 1), (3, 1, -1)):
            block = self.block(back, by)
            self.arrived(self.part(block), 4 + 4 * back + half)
            piece = self.part(block, half)
            self.send(piece, piece, 6 + 4 * back + half, p.along_second(step))
            self.to_sibling(self.part(block), back, by)

    def second_far(self, back):
        block = self.block(back, 2)
        for half in range(2):
            self.arrived(self.part(block, half), 6 + 4 * back + half)
        self.to_sibling(self.part(block), back, 2)

    def finish(self):
        for back in range(4):
            for by in range(4):
                self.arrived(self.part(self.block(back, by)), 20 + 4 * back + by)

    def drain(self):
        for copy in self.sent:
            copy.wait_send()


class Scatter:
    SEMS = 13

    def __init__(self, place, partial, width, recv, out, stage, sems, local_sems):
        self.place, self.width, self.out = place, width, out
        self.sib_recv, self.second_recv, self.first_recv = recv
        self.stage, self.sems, self.local_sems = stage, sems, local_sems
        columns = pl.ds(0, width)
        self.blocks = partial.reshape(16, 2, BLOCK, PADDED).at[:, :, :, columns]
        self.grid = partial.reshape(4, 4, 2, BLOCK, PADDED).at[:, :, :, :, columns]
        self.sent = []

    def mine(self, first, second):
        return lax.div(self.place.block(first, second), 2)

    def arrived(self, spot, at):
        remote(spot, spot, self.sems, at, self.place.sibling()).wait_recv()

    def move(self, source, target, at, device):
        copy = remote(source, target, self.sems, at, device)
        copy.start()
        self.sent.append(copy)

    def to_sibling(self):
        p = self.place
        self.move(self.blocks.at[:, 1 - p.core], self.sib_recv, 0, p.sibling())

    def fetch(self, source, count):
        target = self.stage.at[pl.ds(0, count), :, pl.ds(0, self.width)]
        copy = pltpu.make_async_copy(source, target, self.local_sems.at[0])
        copy.start()
        copy.wait()

    def add_to(self, at, parts):
        total = self.blocks[at, self.place.core].astype(jnp.float32)
        for part in parts:
            total = total + self.stage[part, :, : self.width].astype(jnp.float32)
        self.blocks[at, self.place.core] = total.astype(jnp.bfloat16)

    def pair(self, half, by, target, at, step):
        p = self.place
        there = p.turn(p.second, by)
        two = pl.ds(2 * half, 2)
        flat = remote(self.grid.at[two, there, 0], target, self.sems, at, p.along_second(step))
        tall = remote(self.grid.at[there, two, 1], target, self.sems, at, p.along_second(step))

        @pl.when(p.core == 0)
        def _():
            flat.start()

        @pl.when(p.core == 1)
        def _():
            tall.start()

        self.sent.append(flat)

    def second_start(self):
        p = self.place
        self.arrived(self.sib_recv, 0)
        self.fetch(self.sib_recv, 16)

        @pl.loop(0, 16)
        def _(at):
            self.add_to(at, [at])

        for half, step in ((0, 1), (1, -1)):
            self.pair(half, 2, self.second_recv.at[pl.ds(8 + 2 * half, 2)], 1 + half, step)
        for half, step in ((0, 1), (1, -1)):
            spot = self.second_recv.at[pl.ds(4 * half + 2 * (1 - half), 2)]
            self.pair(1 - half, step, spot, 3 + half, step)

    def second_relay(self):
        p = self.place
        for half in range(2):
            self.arrived(self.second_recv.at[pl.ds(8 + 2 * half, 2)], 1 + half)
        self.fetch(self.second_recv.at[pl.ds(8, 4)], 4)
        for half, step in ((0, 1), (1, -1)):

            @pl.loop(0, 2)
            def _(first):
                at = self.mine(2 * half + first, p.turn(p.second, step))
                self.add_to(at, [2 * half + first])

            spot = self.second_recv.at[pl.ds(4 * half + 2 * half, 2)]
            self.pair(half, step, spot, 5 + half, step)

    def first_start(self):
        p = self.place
        for at in (3, 4, 5, 6):
            self.arrived(self.second_recv.at[pl.ds(0, 2)], at)
        self.fetch(self.second_recv.at[pl.ds(0, 8)], 8)

        @pl.loop(0, 4)
        def _(first):
            self.add_to(self.mine(first, p.second), [first, 4 + first])

        for half, step in ((0, 1), (1, -1)):
            self.strip(half, 2, self.first_recv.at[2], 7 + half, step)
        for half, step in ((0, 1), (1, -1)):
            self.strip(1 - half, step, self.first_recv.at[half], 9 + half, step)

    def columns(self, half):
        return pl.ds(half * (self.width // 2), self.width // 2)

    def strip(self, half, by, target, at, step):
        p = self.place
        source = self.blocks.at[self.mine(p.turn(p.first, by), p.second), p.core]
        columns = self.columns(half)
        self.move(source.at[:, columns], target.at[:, columns], at, p.along_first(step))

    def first_relay(self):
        p = self.place
        for half, step in ((0, 1), (1, -1)):
            columns = self.columns(half)
            self.arrived(self.first_recv.at[2, :, columns], 7 + half)
            at = self.mine(p.turn(p.first, step), p.second)
            both = self.blocks[at, p.core, :, columns].astype(jnp.float32)
            both = both + self.first_recv[2, :, columns].astype(jnp.float32)
            self.blocks[at, p.core, :, columns] = both.astype(jnp.bfloat16)
            self.strip(half, step, self.first_recv.at[half], 11 + half, step)

    def finish(self):
        p = self.place
        for at in (9, 10, 11, 12):
            self.arrived(self.first_recv.at[0, :, self.columns(0)], at)
        total = self.blocks[self.mine(p.first, p.second), p.core].astype(jnp.float32)
        for by in range(2):
            total = total + self.first_recv[by].astype(jnp.float32)
        self.out[...] = total

    def drain(self):
        for copy in self.sent:
            copy.wait_send()


class TpSum:
    SEMS = 18

    def __init__(self, place, send, relay, final, sems):
        self.place, self.send, self.relay_in, self.final = place, send, relay, final
        self.sems = sems
        self.sent = []

    def rows(self, by, half):
        p = self.place
        start = p.turn(p.tp, by) * QUARTER + half * HALF
        return pl.ds(pl.multiple_of(start, HALF), HALF)

    def move(self, source, target, at, by):
        copy = remote(source, target, self.sems, at, self.place.along_tp(by))
        copy.start()
        self.sent.append(copy)

    def give(self, values, slot, width):
        columns = pl.ds(slot * width, width)
        if values is not None:
            self.send[:, columns] = values.astype(jnp.bfloat16)
        for half, by in ((0, 1), (1, -1)):
            self.move(
                self.send.at[self.rows(2, half), columns],
                self.relay_in.at[half, :, columns],
                slot * 6 + half,
                by,
            )
        for half, by in ((0, 1), (1, -1)):
            self.move(
                self.send.at[self.rows(by, 1 - half), columns],
                self.final.at[half, pl.ds((1 - half) * HALF, HALF), columns],
                slot * 6 + 2 + half,
                by,
            )

    def relay(self, slot, width):
        columns = pl.ds(slot * width, width)
        for half, by in ((0, 1), (1, -1)):
            spot = self.relay_in.at[half, :, columns]
            remote(
                spot, spot, self.sems, slot * 6 + half, self.place.along_tp(by)
            ).wait_recv()
            rows = self.rows(by, half)
            both = self.send[rows, columns].astype(jnp.float32) + spot[...].astype(jnp.float32)
            self.send[rows, columns] = both.astype(jnp.bfloat16)
            self.move(
                self.send.at[rows, columns],
                self.final.at[half, pl.ds(half * HALF, HALF), columns],
                slot * 6 + 4 + half,
                by,
            )

    def take(self, slots, width):
        p = self.place
        for slot in range(slots):
            for at in (2, 3, 4, 5):
                half = at % 2
                spot = self.final.at[half, pl.ds(0, HALF), pl.ds(slot * width, width)]
                remote(spot, spot, self.sems, slot * 6 + at, p.along_tp(1)).wait_recv()
        rows = pl.ds(pl.multiple_of(p.tp * QUARTER, QUARTER), QUARTER)
        total = self.send[rows, :].astype(jnp.float32)
        for half in range(2):
            total = total + self.final[half].astype(jnp.float32)
        return total

    def drain(self):
        for copy in self.sent:
            copy.wait_send()


class TpSpread:
    SEMS = 6

    def __init__(self, place, source, whole, sems):
        self.place, self.source, self.whole, self.sems = place, source, whole, sems
        self.sent = []

    def spot(self, by, half):
        p = self.place
        start = p.turn(p.tp, by) * QUARTER + half * HALF
        return self.whole.at[pl.ds(pl.multiple_of(start, HALF), HALF)]

    def move(self, source, target, at, by):
        copy = remote(source, target, self.sems, at, self.place.along_tp(by))
        copy.start()
        self.sent.append(copy)

    def start(self):
        for at, half, by in ((0, 0, 1), (1, 1, -1), (2, 1, 1), (3, 0, -1)):
            self.move(self.source.at[pl.ds(half * HALF, HALF)], self.spot(0, half), at, by)

    def arrived(self, at, by, half):
        spot = self.spot(by, half)
        remote(spot, spot, self.sems, at, self.place.along_tp(1)).wait_recv()

    def relay(self):
        for half, by in ((0, 1), (1, -1)):
            self.arrived(half, -by, half)
            spot = self.spot(-by, half)
            self.move(spot, spot, 4 + half, by)

    def finish(self):
        self.arrived(2, -1, 1)
        self.arrived(3, 1, 0)
        self.arrived(4, 2, 0)
        self.arrived(5, 2, 1)

    def drain(self):
        for copy in self.sent:
            copy.wait_send()


def dot(left, right):
    return jnp.dot(left, right, preferred_element_type=jnp.float32)


def dot_t(left, right):
    return lax.dot_general(
        left, right, (((1,), (1,)), ((), ())), preferred_element_type=jnp.float32
    )


def turned(source, target):
    @pl.loop(0, WIDTH // TILE)
    def _(at):
        at = pl.multiple_of(at * TILE, TILE)
        target[pl.ds(at, TILE), :] = source[pl.ds(0, ROWS), pl.ds(at, TILE)].T


def own_rows_of(place):
    return pl.ds(pl.multiple_of(place.tp * QUARTER, QUARTER), QUARTER)


def norm_of(values):
    inverse = lax.rsqrt(jnp.mean(values * values, axis=-1, keepdims=True) + epsilon)
    return values * inverse, inverse


def norm_back(grad, normed, inverse, gain):
    scaled = grad * gain
    return inverse * (scaled - normed * jnp.mean(scaled * normed, axis=-1, keepdims=True))


def kernel(
    x,
    cotangent,
    lengths,
    in_weight,
    out_weight,
    gate_up_weight,
    down_weight,
    gains,
    taps,
    block_out,
    input_out,
    sib_hbm,
    second_hbm,
    io_sib_hbm,
    io_second_hbm,
    io_grad,
    gud_grad,
    small,
    io_local,
    gud_local,
    io,
    weights,
    big,
    grad_proj,
    grad_low,
    x_own,
    edges,
    input_low,
    turn_a,
    turn_b,
    send_a,
    send_b,
    relays,
    finals,
    second_low,
    residual,
    projected,
    product,
    convolved,
    gated,
    grad_own,
    block_own,
    input_own,
    conv_grad,
    stage,
    first_recv,
    io_first_recv,
    small_recv,
    io_sems,
    down_sems,
    wide_sems,
    scatter_sems,
    sum_sems,
    spread_sems,
    edge_sems,
    small_sems,
    local_sems,
):
    f32, b16 = jnp.float32, jnp.bfloat16
    place = Place()
    own_rows = own_rows_of(place)
    tiles = PADDED // TILE
    mine = place.block(place.first, place.second)
    flat_io = io.reshape(WIDTH, WIDE)
    flat_weights = weights.reshape(3, WIDTH, PADDED)

    x_copy = pltpu.make_async_copy(x, send_b, local_sems.at[1])
    low_copy = pltpu.make_async_copy(cotangent, grad_low, local_sems.at[2])
    own_copy = pltpu.make_async_copy(x.at[own_rows], x_own, local_sems.at[3])
    for copy in (x_copy, low_copy, own_copy):
        copy.start()
    for member in range(3):
        io_local[:, member * CHANNELS : (member + 1) * CHANNELS] = in_weight[member].astype(b16)
    io_local[:, 3 * CHANNELS :] = out_weight[...].astype(b16)
    for member in range(2):
        gud_local[member, :, :HIDDEN] = gate_up_weight[member].astype(b16)
    gud_local[2, :, :HIDDEN] = down_weight[...].astype(b16)
    gud_local[:, :, HIDDEN:] = jnp.zeros((3, BLOCK, PADDED - HIDDEN), b16)
    io[mine] = io_local[...]
    weights[:, mine] = gud_local[...]
    place.greet()
    slots_x = x.reshape(2, SLOT_ROWS, WIDTH)
    edge_copies = [
        remote(slots_x.at[:, pl.ds(SLOT_ROWS - EDGE, EDGE)], edges.at[0], edge_sems, 0, place.along_ctx(1)),
        remote(slots_x.at[:, pl.ds(0, EDGE)], edges.at[1], edge_sems, 1, place.along_ctx(-1)),
    ]
    for copy in edge_copies:
        copy.start()
    io_gather = Gather(place, io_local, io, io_sems)
    down_gather = Gather(place, gud_local.at[2], weights.at[2], down_sems)
    wide_gather = Gather(place, gud_local.at[pl.ds(0, 2)], weights.at[pl.ds(0, 2)], wide_sems)
    io_gather.start()

    def normed_low(values):
        normed, _ = norm_of(values.astype(f32))
        return (normed * gains[0:1, :]).astype(b16)

    x_copy.wait()

    @pl.loop(0, ROWS, step=64)
    def _(at):
        input_low[pl.ds(at, 64), :] = normed_low(send_b[pl.ds(at, 64), :])

    io_gather.first()
    for copy in edge_copies:
        copy.wait()
    for side in range(2):
        rows = pl.ds(ROWS + side * 2 * EDGE, 2 * EDGE)
        input_low[rows, :] = normed_low(edges[side].reshape(2 * EDGE, WIDTH))
    io_gather.second(0)
    io_gather.first_far()
    low_copy.wait()
    positions = place.ctx * SLOT_ROWS + lax.broadcasted_iota(jnp.int32, (SLOT_ROWS, 1), 0)
    for slot in range(2):
        rows = slice(slot * SLOT_ROWS, (slot + 1) * SLOT_ROWS)
        kept = jnp.where(positions < lengths[slot], 1.0, 0.0)
        grad_low[rows, :] = (grad_low[rows, :].astype(f32) * kept).astype(b16)
    io_gather.second(1)
    io_gather.second(3)
    io_gather.second_far(0)
    io_gather.second(2)
    down_gather.start()
    for back in (1, 3, 2):
        io_gather.second_far(back)
    io_gather.finish()
    for member in range(3):
        projected[member] = dot(
            input_low[...], flat_io[:, member * CHANNELS : (member + 1) * CHANNELS]
        )
    down_gather.first()
    down_gather.second(0)
    wide_gather.start()
    product[:, 8:, :] = (projected[0, :ROWS] * projected[2, :ROWS]).reshape(
        2, SLOT_ROWS, CHANNELS
    )
    before = (
        projected[0, ROWS : ROWS + 2 * EDGE] * projected[2, ROWS : ROWS + 2 * EDGE]
    ).reshape(2, EDGE, CHANNELS)
    product[:, :8, :] = jnp.where(place.ctx > 0, before[:, EDGE - 8 :, :], 0.0)
    convolved[...] = (
        taps[0:1, :] * product[:, 6 : 6 + SLOT_ROWS, :]
        + taps[1:2, :] * product[:, 7 : 7 + SLOT_ROWS, :]
        + taps[2:3, :] * product[:, 8 : 8 + SLOT_ROWS, :]
    ).reshape(ROWS, CHANNELS)
    gated[...] = (projected[1, :ROWS] * convolved[...]).astype(b16)

    mixed = TpSum(place, send_a, relays.at[0], finals.at[0], sum_sems.at[0])
    for slot in range(3):
        part = dot_t(gated[...], flat_io[slot * 512 : (slot + 1) * 512, 3 * CHANNELS :])
        mixed.give(part, slot, 512)
    down_gather.first_far()
    mixed.relay(0, 512)
    down_gather.second(1)
    down_gather.second(3)
    down_gather.second_far(0)
    mixed.relay(1, 512)
    mixed.relay(2, 512)
    turned(grad_low, turn_a)
    wide_gather.first()
    wide_gather.second(0)
    own_copy.wait()
    stream = x_own[...].astype(f32) + mixed.take(3, 512)
    residual[...] = stream
    normed, _ = norm_of(stream)
    second_low[own_rows, :] = (normed * gains[1:2, :]).astype(b16)
    second_spread = TpSpread(place, second_low.at[own_rows], second_low, spread_sems.at[0])
    second_spread.start()
    wide_gather.first_far()
    down_gather.second(2)
    for back in (1, 3, 2):
        down_gather.second_far(back)
    wide_gather.second(1)
    wide_gather.second(3)
    second_spread.relay()
    wide_gather.second_far(0)
    down_gather.finish()

    @pl.loop(0, tiles)
    def _(at):
        columns = pl.ds(pl.multiple_of(at * TILE, TILE), TILE)
        big[0:ROWS, columns] = dot(grad_low[...], flat_weights[2, :, columns]).astype(b16)

    wide_gather.second(2)
    second_spread.finish()
    turned(second_low, turn_b)
    for back in (1, 3, 2):
        wide_gather.second_far(back)
    wide_gather.finish()
    for part in (io_gather, down_gather, wide_gather, mixed, second_spread):
        part.drain()

    @pl.loop(0, tiles)
    def _(at):
        columns = pl.ds(pl.multiple_of(at * TILE, TILE), TILE)
        gate = dot(second_low[0:ROWS, :], flat_weights[0, :, columns])
        up = dot(second_low[0:ROWS, :], flat_weights[1, :, columns])
        grad_inner = big[0:ROWS, columns].astype(f32)
        sigmoid = jax.nn.sigmoid(gate)
        active = gate * sigmoid
        big[0:ROWS, columns] = (active * up).astype(b16)
        big[ROWS : 2 * ROWS, columns] = (
            grad_inner * up * sigmoid * (1.0 + gate * (1.0 - sigmoid))
        ).astype(b16)
        big[2 * ROWS :, columns] = (grad_inner * active).astype(b16)

    def gradient(left, at, member):
        @pl.loop(0, tiles)
        def _(tile):
            columns = pl.ds(pl.multiple_of(tile * TILE, TILE), TILE)
            flat_weights[at, :, columns] = dot(
                left[...], big[member * ROWS : (member + 1) * ROWS, columns]
            ).astype(b16)

    def piece(at):
        return Scatter(
            place,
            flat_weights.at[at],
            PADDED,
            (sib_hbm.at[at], second_hbm.at[at], first_recv.at[at]),
            gud_grad.at[at],
            stage,
            scatter_sems.at[at],
            local_sems,
        )

    gate_piece, up_piece, down_piece = piece(0), piece(1), piece(2)
    second = TpSum(place, send_b, relays.at[1], finals.at[1], sum_sems.at[1])
    branch = TpSum(place, send_a, relays.at[2], finals.at[2], sum_sems.at[2])

    def give_second(slot):
        rows = slice(slot * 512, (slot + 1) * 512)
        part = dot_t(big[ROWS : 2 * ROWS, :], flat_weights[0, rows, :])
        part = part + dot_t(big[2 * ROWS :, :], flat_weights[1, rows, :])
        second.give(part, slot, 512)

    give_second(0)
    for slot in range(3):
        columns = slice(slot * 512, (slot + 1) * 512)
        send_a[:, columns] = dot_t(big[0:ROWS, :], flat_weights[2, columns, :]).astype(b16)
    give_second(1)
    second.relay(0, 512)
    give_second(2)
    gradient(turn_a, 2, 0)
    down_piece.to_sibling()
    second.relay(1, 512)
    second.relay(2, 512)
    gradient(turn_b, 0, 1)
    gate_piece.to_sibling()
    down_piece.second_start()
    normed, inverse = norm_of(residual[...])
    grad_second = second.take(3, 512)
    small[...] = jnp.zeros_like(small)
    small[1:2, :] = jnp.sum(grad_second * normed, axis=0, keepdims=True)
    grad_stream = grad_low[own_rows, :].astype(f32) + norm_back(
        grad_second, normed, inverse, gains[1:2, :]
    )
    grad_own[...] = grad_stream
    second_low[own_rows, :] = grad_stream.astype(b16)
    low_spread = TpSpread(place, second_low.at[own_rows], second_low, spread_sems.at[1])
    low_spread.start()
    even = lax.rem(place.tp, 2) == 0
    edge_source = second_low.at[pl.ds(pl.multiple_of(place.tp * QUARTER, QUARTER), EDGE)]
    edge_target = second_low.at[
        pl.ds(pl.multiple_of(ROWS + lax.div(place.tp, 2) * EDGE, EDGE), EDGE)
    ]
    for tp in range(4):

        @pl.when(even)
        def _():
            pltpu.make_async_remote_copy(
                src_ref=edge_source,
                dst_ref=edge_target,
                send_sem=edge_sems.at[0, 2 + tp],
                recv_sem=edge_sems.at[1, 2 + lax.div(place.tp, 2)],
                device_id=place.along_ctx(-1, tp),
                device_id_type=MESH,
            ).start()

    gradient(turn_b, 1, 2)
    up_piece.to_sibling()
    gate_piece.second_start()
    low_spread.relay()
    for slot in range(3):
        branch.give(None, slot, 512)
    down_piece.second_relay()
    up_piece.second_start()
    low_spread.finish()
    for slot in range(2):
        spot = second_low.at[pl.ds(ROWS + slot * EDGE, EDGE)]
        remote(spot, spot, edge_sems, 2 + slot, place.sibling()).wait_recv()
    for tp in range(4):

        @pl.when(even)
        def _():
            remote(edge_source, edge_target, edge_sems, 2 + tp, place.sibling()).wait_send()

    grad_gated = dot(second_low[...], flat_io[:, 3 * CHANNELS :])
    conv_grad[:, :SLOT_ROWS, :] = (grad_gated[:ROWS] * projected[1, :ROWS]).reshape(
        2, SLOT_ROWS, CHANNELS
    )
    after = (grad_gated[ROWS:] * projected[1, ROWS + 2 * EDGE :]).reshape(2, EDGE, CHANNELS)
    conv_grad[:, SLOT_ROWS:, :] = jnp.where(place.ctx < 15, after[:, :8, :], 0.0)
    grad_proj[:, CHANNELS : 2 * CHANNELS] = (grad_gated[:ROWS] * convolved[...]).astype(b16)
    grad_product = (
        taps[2:3, :] * conv_grad[:, 0:SLOT_ROWS, :]
        + taps[1:2, :] * conv_grad[:, 1 : 1 + SLOT_ROWS, :]
        + taps[0:1, :] * conv_grad[:, 2 : 2 + SLOT_ROWS, :]
    ).reshape(ROWS, CHANNELS)
    grad_proj[:, 0:CHANNELS] = (grad_product * projected[2, :ROWS]).astype(b16)
    grad_proj[:, 2 * CHANNELS :] = (grad_product * projected[0, :ROWS]).astype(b16)
    second.drain()
    first = TpSum(place, send_b, relays.at[0], finals.at[0], sum_sems.at[3])
    for slot in range(3):
        part = dot_t(grad_proj[...], flat_io[slot * 512 : (slot + 1) * 512, : 3 * CHANNELS])
        first.give(part, slot, 512)
    for slot in range(3):
        branch.relay(slot, 512)
    gate_piece.second_relay()
    turned(input_low, turn_a)
    turned(second_low, turn_b)
    big[:, : 3 * CHANNELS] = dot(turn_a[...], grad_proj[...]).astype(b16)
    big[:, 3 * CHANNELS : 4 * CHANNELS] = dot(turn_b[...], gated[...]).astype(b16)
    io_piece = Scatter(
        place,
        big,
        WIDE,
        (io_sib_hbm, io_second_hbm, io_first_recv),
        io_grad,
        stage,
        scatter_sems.at[3],
        local_sems,
    )
    io_piece.to_sibling()
    down_piece.first_start()
    first.relay(0, 512)
    block_own[...] = (residual[...] + branch.take(3, 512)).astype(b16)
    block_keep = pltpu.make_async_copy(block_own, block_out.at[own_rows], local_sems.at[4])
    block_keep.start()
    first.relay(1, 512)
    first.relay(2, 512)
    block_spread = TpSpread(place, block_own, block_out, spread_sems.at[2])
    block_spread.start()
    up_piece.second_relay()
    io_piece.second_start()
    own_columns = pl.ds(pl.multiple_of(place.tp * CHANNELS, QUARTER), CHANNELS)
    for tap in range(3):
        small[2 + tap : 3 + tap, own_columns] = jnp.sum(
            conv_grad[:, :SLOT_ROWS, :] * product[:, 6 + tap : 6 + tap + SLOT_ROWS, :], axis=(0, 1)
        ).reshape(1, CHANNELS)
    normed, inverse = norm_of(x_own[...].astype(f32))
    grad_first = first.take(3, 512)
    small[0:1, :] = jnp.sum(grad_first * normed, axis=0, keepdims=True)
    input_own[...] = (
        grad_own[...] + norm_back(grad_first, normed, inverse, gains[0:1, :])
    ).astype(b16)

    def exchange(start, devices):
        copies = [
            remote(small, small_recv.at[start + at], small_sems, start + at, device)
            for at, device in enumerate(devices)
        ]
        for copy in copies:
            copy.start()
        return copies

    def added(start, copies):
        for copy in copies:
            copy.wait()
        total = small[...]
        for at in range(len(copies)):
            total = total + small_recv[start + at]
        small[...] = total

    tp_copies = exchange(0, [place.along_tp(by) for by in (1, 2, 3)])
    input_keep = pltpu.make_async_copy(input_own, input_out.at[own_rows], local_sems.at[5])
    input_keep.start()
    input_spread = TpSpread(place, input_own, input_out, spread_sems.at[3])
    input_spread.start()
    gate_piece.first_start()
    added(0, tp_copies)
    sibling_copies = exchange(3, [place.sibling()])
    down_piece.first_relay()
    block_spread.relay()
    io_piece.second_relay()
    added(3, sibling_copies)
    first_copies = exchange(4, [place.along_first(by) for by in (1, 2, 3)])
    up_piece.first_start()
    gate_piece.first_relay()
    added(4, first_copies)
    second_copies = exchange(7, [place.along_second(by) for by in (1, 2, 3)])
    io_piece.first_start()
    input_spread.relay()
    up_piece.first_relay()
    down_piece.finish()
    gate_piece.finish()
    io_piece.first_relay()
    added(7, second_copies)
    up_piece.finish()
    io_piece.finish()
    block_keep.wait()
    input_keep.wait()
    block_spread.finish()
    input_spread.finish()
    for part in (low_spread, block_spread, input_spread, first, branch):
        part.drain()
    for part in (down_piece, gate_piece, up_piece, io_piece):
        part.drain()


def step(*given):
    vmem = pl.BlockSpec(memory_space=pltpu.VMEM)
    smem = pl.BlockSpec(memory_space=pltpu.SMEM)
    hbm = pl.BlockSpec(memory_space=pl.ANY)
    f32, b16 = jnp.float32, jnp.bfloat16
    dma = pltpu.SemaphoreType.DMA
    own16 = pltpu.VMEM((QUARTER, WIDTH), b16)
    own32 = pltpu.VMEM((QUARTER, WIDTH), f32)
    full = pltpu.VMEM((ROWS, WIDTH), b16)
    across = pltpu.VMEM((WIDTH, ROWS), b16)
    return pl.pallas_call(
        kernel,
        out_shape=(
            jax.ShapeDtypeStruct((ROWS, WIDTH), b16),
            jax.ShapeDtypeStruct((ROWS, WIDTH), b16),
            jax.ShapeDtypeStruct((3, 16, BLOCK, PADDED), b16),
            jax.ShapeDtypeStruct((3, 12, BLOCK, PADDED), b16),
            jax.ShapeDtypeStruct((16, BLOCK, WIDE), b16),
            jax.ShapeDtypeStruct((12, BLOCK, WIDE), b16),
            jax.ShapeDtypeStruct((BLOCK, WIDE), f32),
            jax.ShapeDtypeStruct((3, BLOCK, PADDED), f32),
            jax.ShapeDtypeStruct((8, WIDTH), f32),
        ),
        in_specs=[hbm, hbm, smem] + [vmem] * 6,
        out_specs=(hbm,) * 6 + (vmem,) * 3,
        scratch_shapes=[
            pltpu.VMEM((BLOCK, WIDE), b16),
            pltpu.VMEM((3, BLOCK, PADDED), b16),
            pltpu.VMEM((32, BLOCK, WIDE), b16),
            pltpu.VMEM((3, 32, BLOCK, PADDED), b16),
            pltpu.VMEM((WIDTH, PADDED), b16),
            pltpu.VMEM((ROWS, 3 * CHANNELS), b16),
            full,
            own16,
            pltpu.VMEM((2, 2, EDGE, WIDTH), b16),
            pltpu.VMEM((ROWS + 4 * EDGE, WIDTH), b16),
            across,
            across,
            full,
            full,
            pltpu.VMEM((3, 2, HALF, WIDTH), b16),
            pltpu.VMEM((3, 2, QUARTER, WIDTH), b16),
            pltpu.VMEM((ROWS + 2 * EDGE, WIDTH), b16),
            own32,
            pltpu.VMEM((3, ROWS + 4 * EDGE, CHANNELS), f32),
            pltpu.VMEM((2, 8 + SLOT_ROWS, CHANNELS), f32),
            pltpu.VMEM((ROWS, CHANNELS), f32),
            pltpu.VMEM((ROWS, CHANNELS), b16),
            own32,
            own16,
            own16,
            pltpu.VMEM((2, SLOT_ROWS + 8, CHANNELS), f32),
            pltpu.VMEM((16, BLOCK, PADDED), b16),
            pltpu.VMEM((3, 3, BLOCK, PADDED), b16),
            pltpu.VMEM((3, BLOCK, WIDE), b16),
            pltpu.VMEM((10, 8, WIDTH), f32),
            dma((2, Gather.SEMS)),
            dma((2, Gather.SEMS)),
            dma((2, Gather.SEMS)),
            dma((4, 2, Scatter.SEMS)),
            dma((4, 2, TpSum.SEMS)),
            dma((4, 2, TpSpread.SEMS)),
            dma((2, 6)),
            dma((2, 10)),
            dma((6,)),
        ],
        compiler_params=pltpu.CompilerParams(
            collective_id=0, has_side_effects=True, vmem_limit_bytes=63 * 2**20
        ),
        name="step",
    )(*given)


def nesterov(weight, moment, average, gradient, step_rate):
    moment_new = momentum * moment + gradient
    weight_new = weight - step_rate * (gradient + momentum * moment_new)
    average_new = average_decay * average + (1.0 - average_decay) * weight_new
    return (moment_new, weight_new, average_new)


def on_device(
    hidden,
    lengths,
    cotangent,
    in_weight,
    in_moment,
    in_average,
    out_weight,
    out_moment,
    out_average,
    gate_up_weight,
    gate_up_moment,
    gate_up_average,
    down_weight,
    down_moment,
    down_average,
    norm_gains,
    gain_moment,
    gain_average,
    conv_taps,
    taps_moment,
    taps_average,
):
    slot_count, seq_len, model_width = hidden.shape
    row_count = slot_count * seq_len
    block_output, input_low_grad, _, _, _, _, io_sum, gud_sum, small = step(
        hidden.reshape(row_count, model_width),
        cotangent.reshape(row_count, model_width),
        lengths,
        in_weight,
        out_weight.T,
        gate_up_weight,
        down_weight.T,
        norm_gains,
        conv_taps,
    )
    block_output = block_output.reshape(slot_count, seq_len, model_width)
    input_grad = input_low_grad.astype(jnp.float32).reshape(slot_count, seq_len, model_width)
    in_sum = jnp.moveaxis(io_sum[:, : 3 * CHANNELS].reshape(BLOCK, 3, CHANNELS), 1, 0)
    out_sum = io_sum[:, 3 * CHANNELS :].T
    gate_up_sum = gud_sum[:2, :, :HIDDEN]
    down_sum = gud_sum[2, :, :HIDDEN].T
    gain_total = small[:2]
    taps_total = lax.dynamic_slice_in_dim(
        small[2:5], lax.axis_index("tp") * CHANNELS, CHANNELS, axis=1
    )
    in_new = nesterov(in_weight, in_moment, in_average, in_sum, matrix_rate)
    out_new = nesterov(out_weight, out_moment, out_average, out_sum, matrix_rate)
    gate_up_new = nesterov(
        gate_up_weight, gate_up_moment, gate_up_average, gate_up_sum, matrix_rate
    )
    down_new = nesterov(down_weight, down_moment, down_average, down_sum, matrix_rate)
    gain_new = nesterov(norm_gains, gain_moment, gain_average, gain_total, small_rate)
    taps_new = nesterov(conv_taps, taps_moment, taps_average, taps_total, small_rate)
    return (
        block_output,
        input_grad,
        in_new[0],
        in_new[1],
        in_new[2],
        out_new[0],
        out_new[1],
        out_new[2],
        gate_up_new[0],
        gate_up_new[1],
        gate_up_new[2],
        down_new[0],
        down_new[1],
        down_new[2],
        gain_new[0],
        gain_new[1],
        gain_new[2],
        taps_new[0],
        taps_new[1],
        taps_new[2],
    )


def solution(mesh):
    placed = (
        P("shard", "ctx", None),
        P("shard"),
        P("shard", "ctx", None),
        P(None, ("shard", "ctx"), "tp"),
        P(None, ("shard", "ctx"), "tp"),
        P(None, ("shard", "ctx"), "tp"),
        P("tp", ("shard", "ctx")),
        P("tp", ("shard", "ctx")),
        P("tp", ("shard", "ctx")),
        P(None, ("shard", "ctx"), "tp"),
        P(None, ("shard", "ctx"), "tp"),
        P(None, ("shard", "ctx"), "tp"),
        P("tp", ("shard", "ctx")),
        P("tp", ("shard", "ctx")),
        P("tp", ("shard", "ctx")),
        P(),
        P(),
        P(),
        P(None, "tp"),
        P(None, "tp"),
        P(None, "tp"),
    )
    return jax.shard_map(
        on_device,
        mesh=mesh,
        in_specs=placed,
        out_specs=(
            P("shard", "ctx", None),
            P("shard", "ctx", None),
            P(None, ("shard", "ctx"), "tp"),
            P(None, ("shard", "ctx"), "tp"),
            P(None, ("shard", "ctx"), "tp"),
            P("tp", ("shard", "ctx")),
            P("tp", ("shard", "ctx")),
            P("tp", ("shard", "ctx")),
            P(None, ("shard", "ctx"), "tp"),
            P(None, ("shard", "ctx"), "tp"),
            P(None, ("shard", "ctx"), "tp"),
            P("tp", ("shard", "ctx")),
            P("tp", ("shard", "ctx")),
            P("tp", ("shard", "ctx")),
            P(),
            P(),
            P(),
            P(None, "tp"),
            P(None, "tp"),
            P(None, "tp"),
        ),
        check_vma=False,
    )
```

```python
import functools

import jax
import jax.numpy as jnp
from jax import lax
from jax.experimental import pallas as pl
from jax.experimental.pallas import tpu as pltpu
from jax.sharding import PartitionSpec as P

MESH = pl.DeviceIdType.MESH
epsilon = 1e-05
momentum = 0.9
average_decay = 0.9
matrix_rate = 0.0004
small_rate = 0.005
WIDTH = 1536
CHANNELS = 384
HIDDEN = 1728
TILE = 256
EDGE = 16
EARLY = 4
SLOTS = ((0, 512), (512, 512), (1024, 512))
WIDE = 4 * CHANNELS
PADDED = 1792
ROWS = 512
QUARTER = 128
SLOT_ROWS = 256
BLOCK = 48
HALF = QUARTER // 2


class Place:
    def __init__(self):
        self.shard = lax.axis_index("shard")
        self.ctx = lax.axis_index("ctx")
        self.tp = lax.axis_index("tp")
        self.y = self.shard * 2 + lax.div(self.ctx, 8)
        self.z = lax.rem(lax.div(self.ctx, 2), 4)
        self.core = lax.rem(self.ctx, 2)
        self.first = self.y * (1 - self.core) + self.z * self.core
        self.second = self.z * (1 - self.core) + self.y * self.core

    def turn(self, value, by):
        return lax.rem(value + by + 4, 4)

    def device(self, y, z, core):
        return (lax.div(y, 2), lax.rem(y, 2) * 8 + z * 2 + core, self.tp)

    def grid_device(self, first, second):
        y = first * (1 - self.core) + second * self.core
        z = second * (1 - self.core) + first * self.core
        return self.device(y, z, self.core)

    def block(self, first, second):
        y = first * (1 - self.core) + second * self.core
        z = second * (1 - self.core) + first * self.core
        return y * 8 + z * 2 + self.core

    def along_first(self, by):
        return self.grid_device(self.turn(self.first, by), self.second)

    def along_second(self, by):
        return self.grid_device(self.first, self.turn(self.second, by))

    def along_tp(self, by):
        return (self.shard, self.ctx, self.turn(self.tp, by))

    def along_ctx(self, by, tp=None):
        return (self.shard, lax.rem(self.ctx + by + 16, 16), self.tp if tp is None else tp)

    def sibling(self):
        return self.device(self.y, self.z, 1 - self.core)

    def greet(self):
        barrier = pltpu.get_barrier_semaphore()
        friends = [self.sibling()]
        for tp in range(4):
            friends += [self.along_ctx(1, tp), self.along_ctx(-1, tp)]
        for by in (1, 2, 3):
            friends += [self.along_first(by), self.along_second(by), self.along_tp(by)]
        for friend in friends:
            pl.semaphore_signal(barrier, inc=1, device_id=friend, device_id_type=MESH)
        pl.semaphore_wait(barrier, len(friends))


def remote(source, target, send_sem, recv_sem, device):
    return pltpu.make_async_remote_copy(
        src_ref=source,
        dst_ref=target,
        send_sem=send_sem,
        recv_sem=recv_sem,
        device_id=device,
        device_id_type=MESH,
    )


def wait_bytes(spot, sem):
    pltpu.make_async_copy(spot, spot, sem).wait()


class Gather:
    SEMS = 12

    def __init__(self, place, local, whole, sems):
        self.place, self.local, self.whole, self.sems = place, local, whole, sems
        self.half = local.shape[-1] // 2

    def part(self, block, half=None):
        spot = self.whole.at[:, block] if self.whole.ndim == 4 else self.whole.at[block]
        if half is None:
            return spot
        columns = pl.ds(half * self.half, self.half)
        return spot.at[:, :, columns] if self.whole.ndim == 4 else spot.at[:, columns]

    def send(self, source, target, at, device):
        remote(source, target, self.sems.at[0], self.sems.at[at], device).start()

    def arrived(self, blocks, at):
        few = pl.ds(0, blocks)
        wait_bytes(self.whole.at[:, few] if self.whole.ndim == 4 else self.whole.at[few], self.sems.at[at])

    def block(self, back, by):
        p = self.place
        return p.block(p.turn(p.first, -back), p.turn(p.second, -by))

    def to_second(self, source, back, by):
        spot = self.part(self.block(back, 0))
        self.send(source, spot, 3 + back, self.place.along_second(1))
        self.send(source, spot, 3 + back, self.place.along_second(-1))
        self.to_sibling(source, back, by)

    def to_sibling(self, source, back, by):
        self.send(source, self.part(self.block(back, by)), 11, self.place.sibling())

    def start(self):
        p = self.place
        spot = self.part(self.block(0, 0))
        self.send(self.local, spot, 1, p.along_first(1))
        self.send(self.local, spot, 1, p.along_first(-1))
        self.to_second(self.local, 0, 0)

    def first(self):
        p = self.place
        self.arrived(2, 1)
        for back, half, by in ((1, 0, 1), (3, 1, -1)):
            piece = self.part(self.block(back, 0), half)
            self.send(piece, piece, 2, p.along_first(by))
        for back in (1, 3):
            self.to_second(self.part(self.block(back, 0)), back, 0)

    def first_far(self):
        self.arrived(1, 2)
        self.to_second(self.part(self.block(2, 0)), 2, 0)

    def second(self, back):
        p = self.place
        self.arrived(2, 3 + back)
        for by, half, step in ((1, 0, 1), (3, 1, -1)):
            piece = self.part(self.block(back, by), half)
            self.send(piece, piece, 7 + back, p.along_second(step))
        for by in (1, 3):
            self.to_sibling(self.part(self.block(back, by)), back, by)

    def second_far(self, back):
        self.arrived(1, 7 + back)
        self.to_sibling(self.part(self.block(back, 2)), back, 2)

    def finish(self):
        self.arrived(16, 11)

    def drain(self):
        self.arrived(31, 0)


class Scatter:
    SEMS = 6

    def __init__(self, place, partial, width, recv, out, stage, sems, local_sems):
        self.place, self.width, self.out = place, width, out
        self.sib_recv, self.second_recv, self.first_recv = recv
        self.stage, self.sems, self.local_sems = stage, sems, local_sems
        columns = pl.ds(0, width)
        self.blocks = partial.reshape(16, 2, BLOCK, PADDED).at[:, :, :, columns]
        self.grid = partial.reshape(4, 4, 2, BLOCK, PADDED).at[:, :, :, :, columns]
        self.rows = partial.reshape(32, BLOCK, PADDED).at[:, :, columns]

    def mine(self, first, second):
        return lax.div(self.place.block(first, second), 2)

    def arrived(self, spot, at):
        wait_bytes(spot, self.sems.at[at])

    def move(self, source, target, at, device):
        remote(source, target, self.sems.at[0], self.sems.at[at], device).start()

    def to_sibling(self, start=0, width=None):
        p = self.place
        columns = pl.ds(start, self.width if width is None else width)
        source = self.blocks.at[:, 1 - p.core, :, columns]
        self.move(source, self.sib_recv.at[:, :, columns], 1, p.sibling())

    def fetch(self, source, count):
        if self.stage is None:
            return source
        target = self.stage.at[pl.ds(0, count), :, pl.ds(0, self.width)]
        copy = pltpu.make_async_copy(source, target, self.local_sems.at[0])
        copy.start()
        copy.wait()
        return target

    def add_to(self, at, held, parts):
        core = self.place.core
        if len(parts) == 1:
            self.blocks[at, core] = self.blocks[at, core] + held[parts[0]]
        else:
            total = self.blocks[at, core].astype(jnp.float32)
            for part in parts:
                total = total + held[part].astype(jnp.float32)
            self.blocks[at, core] = total.astype(jnp.bfloat16)

    def pair(self, half, by, target, at, step):
        p = self.place
        there = p.turn(p.second, by)
        two = pl.ds(2 * half, 2)

        @pl.when(p.core == 0)
        def _():
            self.move(self.grid.at[two, there, 0], target, at, p.along_second(step))

        @pl.when(p.core == 1)
        def _():
            self.move(self.grid.at[there, two, 1], target, at, p.along_second(step))

    def second_start(self):
        p = self.place
        self.arrived(self.sib_recv, 1)
        held = self.fetch(self.sib_recv, 16)

        @pl.loop(0, 4)
        def _(first):
            at = self.mine(first, p.turn(p.second, 2))
            self.add_to(at, held, [at])

        for half, step in ((0, 1), (1, -1)):
            self.pair(half, 2, self.second_recv.at[pl.ds(8 + 2 * half, 2)], 2, step)

        @pl.loop(0, 12)
        def _(other):
            away = lax.rem(lax.div(other, 4) + 3, 4)
            at = self.mine(lax.rem(other, 4), p.turn(p.second, away))
            self.add_to(at, held, [at])

        for half, step in ((0, 1), (1, -1)):
            spot = self.second_recv.at[pl.ds(4 * half + 2 * (1 - half), 2)]
            self.pair(1 - half, step, spot, 3, step)

    def second_relay(self):
        p = self.place
        self.arrived(self.second_recv.at[pl.ds(8, 4)], 2)
        held = self.fetch(self.second_recv.at[pl.ds(8, 4)], 4)
        for half, step in ((0, 1), (1, -1)):

            @pl.loop(0, 2)
            def _(first):
                at = self.mine(2 * half + first, p.turn(p.second, step))
                self.add_to(at, held, [2 * half + first])

            spot = self.second_recv.at[pl.ds(4 * half + 2 * half, 2)]
            self.pair(half, step, spot, 3, step)

    def first_start(self):
        p = self.place
        self.arrived(self.second_recv.at[pl.ds(0, 8)], 3)
        held = self.fetch(self.second_recv.at[pl.ds(0, 8)], 8)

        @pl.loop(0, 4)
        def _(first):
            self.add_to(self.mine(first, p.second), held, [first, 4 + first])

        for half, step in ((0, 1), (1, -1)):
            self.strip(half, 2, self.first_recv.at[2], 4, step)
        for half, step in ((0, 1), (1, -1)):
            self.strip(1 - half, step, self.first_recv.at[half], 5, step)

    def columns(self, half):
        return pl.ds(half * (self.width // 2), self.width // 2)

    def strip(self, half, by, target, at, step):
        p = self.place
        source = self.blocks.at[self.mine(p.turn(p.first, by), p.second), p.core]
        columns = self.columns(half)
        self.move(source.at[:, columns], target.at[:, columns], at, p.along_first(step))

    def first_relay(self):
        p = self.place
        self.arrived(self.first_recv.at[2], 4)
        for half, step in ((0, 1), (1, -1)):
            columns = self.columns(half)
            at = self.mine(p.turn(p.first, step), p.second)
            both = self.blocks[at, p.core, :, columns].astype(jnp.float32)
            both = both + self.first_recv[2, :, columns].astype(jnp.float32)
            self.blocks[at, p.core, :, columns] = both.astype(jnp.bfloat16)
            self.strip(half, step, self.first_recv.at[half], 5, step)

    def finish(self):
        p = self.place
        self.arrived(self.first_recv.at[pl.ds(0, 2)], 5)
        total = self.blocks[self.mine(p.first, p.second), p.core].astype(jnp.float32)
        for by in range(2):
            total = total + self.first_recv[by].astype(jnp.float32)
        self.out[...] = total

    def drain(self):
        self.arrived(self.rows.at[pl.ds(0, 31)], 0)


class TpSum:
    SEMS = 5

    def __init__(self, place, send, relay, final, sems):
        self.place, self.send, self.relay_in, self.final = place, send, relay, final
        self.sems = sems

    def rows(self, by, half):
        p = self.place
        start = p.turn(p.tp, by) * QUARTER + half * HALF
        return pl.ds(pl.multiple_of(start, HALF), HALF)

    def move(self, source, target, at, by):
        remote(source, target, self.sems.at[0], self.sems.at[at], self.place.along_tp(by)).start()

    def give(self, values, slot):
        columns = pl.ds(*SLOTS[slot])
        self.send[:, columns] = values.astype(jnp.bfloat16)
        for half, by in ((0, 1), (1, -1)):
            source = self.send.at[self.rows(2, half), columns]
            self.move(source, self.relay_in.at[half, :, columns], 2 + slot, by)
        for half, by in ((0, 1), (1, -1)):
            source = self.send.at[self.rows(by, 1 - half), columns]
            target = self.final.at[half, pl.ds((1 - half) * HALF, HALF), columns]
            self.move(source, target, 1, by)

    def relay(self, slot):
        columns = pl.ds(*SLOTS[slot])
        wait_bytes(self.relay_in.at[:, :, columns], self.sems.at[2 + slot])
        for half, by in ((0, 1), (1, -1)):
            rows = self.rows(by, half)
            both = self.send[rows, columns].astype(jnp.float32)
            both = both + self.relay_in[half, :, columns].astype(jnp.float32)
            self.send[rows, columns] = both.astype(jnp.bfloat16)
            target = self.final.at[half, pl.ds(half * HALF, HALF), columns]
            self.move(self.send.at[rows, columns], target, 1, by)

    def take(self):
        p = self.place
        wait_bytes(self.final, self.sems.at[1])
        rows = pl.ds(pl.multiple_of(p.tp * QUARTER, QUARTER), QUARTER)
        total = self.send[rows, :].astype(jnp.float32)
        for half in range(2):
            total = total + self.final[half].astype(jnp.float32)
        return total

    def drain(self):
        wait_bytes(self.send.at[pl.ds(0, 3 * QUARTER)], self.sems.at[0])


class TpSpread:
    SEMS = 3

    def __init__(self, place, source, whole, sems):
        self.place, self.source, self.whole, self.sems = place, source, whole, sems

    def spot(self, by, half):
        p = self.place
        start = p.turn(p.tp, by) * QUARTER + half * HALF
        return self.whole.at[pl.ds(pl.multiple_of(start, HALF), HALF)]

    def move(self, source, target, at, by):
        remote(source, target, self.sems.at[0], self.sems.at[at], self.place.along_tp(by)).start()

    def start(self):
        for at, half, by in ((1, 0, 1), (1, 1, -1), (2, 1, 1), (2, 0, -1)):
            self.move(self.source.at[pl.ds(half * HALF, HALF)], self.spot(0, half), at, by)

    def arrived(self, rows, at):
        wait_bytes(self.whole.at[pl.ds(0, rows)], self.sems.at[at])

    def relay(self):
        self.arrived(QUARTER, 1)
        for half, by in ((0, 1), (1, -1)):
            spot = self.spot(-by, half)
            self.move(spot, spot, 2, by)

    def finish(self):
        self.arrived(2 * QUARTER, 2)

    def drain(self):
        self.arrived(3 * QUARTER, 0)


def dot(left, right):
    return jnp.dot(left, right, preferred_element_type=jnp.float32)


def dot_t(left, right):
    return lax.dot_general(
        left, right, (((1,), (1,)), ((), ())), preferred_element_type=jnp.float32
    )


def turned(source, target):
    @pl.loop(0, WIDTH // TILE)
    def _(at):
        at = pl.multiple_of(at * TILE, TILE)
        target[pl.ds(at, TILE), :] = source[pl.ds(0, ROWS), pl.ds(at, TILE)].T


def slot_rows(slot):
    start, width = SLOTS[slot]
    return slice(start, start + width)


def own_rows_of(place):
    return pl.ds(pl.multiple_of(place.tp * QUARTER, QUARTER), QUARTER)


def norm_of(values):
    inverse = lax.rsqrt(jnp.mean(values * values, axis=-1, keepdims=True) + epsilon)
    return values * inverse, inverse


def norm_back(grad, normed, inverse, gain):
    scaled = grad * gain
    return inverse * (scaled - normed * jnp.mean(scaled * normed, axis=-1, keepdims=True))


def kernel(
    x,
    cotangent,
    lengths,
    in_weight,
    out_weight,
    gate_up_weight,
    down_weight,
    gains,
    taps,
    block_out,
    input_out,
    sib_hbm,
    second_hbm,
    io_grad,
    gud_grad,
    small,
    io_local,
    gud_local,
    io,
    weights,
    big,
    grad_proj,
    grad_low,
    x_own,
    edges,
    input_low,
    turn_a,
    turn_b,
    send_a,
    send_b,
    relays,
    finals,
    second_low,
    residual,
    projected,
    product,
    convolved,
    gated,
    grad_own,
    block_own,
    input_own,
    conv_grad,
    stage,
    first_recv,
    io_sib_recv,
    io_second_recv,
    small_recv,
    io_sems,
    down_sems,
    early_sems,
    late_sems,
    scatter_sems,
    sum_sems,
    spread_sems,
    edge_sems,
    small_sems,
    local_sems,
):
    f32, b16 = jnp.float32, jnp.bfloat16
    place = Place()
    own_rows = own_rows_of(place)
    tiles = PADDED // TILE
    mine = place.block(place.first, place.second)
    flat_io = io.reshape(WIDTH, WIDE)
    flat_weights = weights.reshape(3, WIDTH, PADDED)

    x_copy = pltpu.make_async_copy(x, send_b, local_sems.at[1])
    low_copy = pltpu.make_async_copy(cotangent, grad_low, local_sems.at[2])
    own_copy = pltpu.make_async_copy(x.at[own_rows], x_own, local_sems.at[3])
    for copy in (x_copy, low_copy, own_copy):
        copy.start()
    for member in range(3):
        io_local[:, member * CHANNELS : (member + 1) * CHANNELS] = in_weight[member].astype(b16)
    io_local[:, 3 * CHANNELS :] = out_weight[...].astype(b16)
    for member in range(2):
        gud_local[member, :, :HIDDEN] = gate_up_weight[member].astype(b16)
    gud_local[2, :, :HIDDEN] = down_weight[...].astype(b16)
    gud_local[:, :, HIDDEN:] = jnp.zeros((3, BLOCK, PADDED - HIDDEN), b16)
    io[mine] = io_local[...]
    weights[:, mine] = gud_local[...]
    place.greet()
    early, late = pl.ds(0, EARLY * TILE), pl.ds(EARLY * TILE, PADDED - EARLY * TILE)
    two = pl.ds(0, 2)
    io_gather = Gather(place, io_local, io, io_sems)
    down_gather = Gather(place, gud_local.at[2], weights.at[2], down_sems)
    early_gather = Gather(
        place, gud_local.at[two, :, early], weights.at[two, :, :, early], early_sems
    )
    late_gather = Gather(
        place, gud_local.at[two, :, late], weights.at[two, :, :, late], late_sems
    )
    mixed = TpSum(place, send_a, relays.at[0], finals.at[0], sum_sems.at[0])
    second = TpSum(place, send_b, relays.at[1], finals.at[1], sum_sems.at[1])
    branch = TpSum(place, send_a, relays.at[0], finals.at[0], sum_sems.at[2])
    first = TpSum(place, send_b, relays.at[1], finals.at[1], sum_sems.at[3])
    second_spread = TpSpread(place, second_low.at[own_rows], second_low, spread_sems.at[0])
    low_spread = TpSpread(place, second_low.at[own_rows], second_low, spread_sems.at[1])
    block_spread = TpSpread(place, block_own, block_out, spread_sems.at[2])
    input_spread = TpSpread(place, input_own, input_out, spread_sems.at[3])
    block_keep = pltpu.make_async_copy(block_own, block_out.at[own_rows], local_sems.at[4])
    input_keep = pltpu.make_async_copy(input_own, input_out.at[own_rows], local_sems.at[5])
    even = lax.rem(place.tp, 2) == 0
    edge_source = second_low.at[pl.ds(pl.multiple_of(place.tp * QUARTER, QUARTER), EDGE)]
    edge_target = second_low.at[
        pl.ds(pl.multiple_of(ROWS + lax.div(place.tp, 2) * EDGE, EDGE), EDGE)
    ]
    own_columns = pl.ds(pl.multiple_of(place.tp * CHANNELS, QUARTER), CHANNELS)

    def piece(at):
        return Scatter(
            place,
            flat_weights.at[at],
            PADDED,
            (sib_hbm.at[at], second_hbm.at[at], first_recv.at[at]),
            gud_grad.at[at],
            stage,
            scatter_sems.at[at],
            local_sems,
        )

    gate_piece, up_piece, down_piece = piece(0), piece(1), piece(2)
    io_piece = Scatter(
        place,
        big,
        WIDE,
        (io_sib_recv, io_second_recv, gud_local.at[:, :, pl.ds(0, WIDE)]),
        io_grad,
        None,
        scatter_sems.at[3],
        local_sems,
    )

    def normed_low(values):
        normed, _ = norm_of(values.astype(f32))
        return (normed * gains[0:1, :]).astype(b16)

    def send_edges():
        slots_x = x.reshape(2, SLOT_ROWS, WIDTH)
        for side, start, by in ((0, SLOT_ROWS - EDGE, 1), (1, 0, -1)):
            remote(
                slots_x.at[:, pl.ds(start, EDGE)],
                edges.at[side],
                edge_sems.at[0],
                edge_sems.at[1],
                place.along_ctx(by),
            ).start()

    def project(member):
        columns = slice(member * CHANNELS, (member + 1) * CHANNELS)
        projected[member] = dot(input_low[...], flat_io[:, columns])

    def give_mixed(slot):
        mixed.give(dot_t(gated[...], flat_io[slot_rows(slot), 3 * CHANNELS :]), slot)

    def inner_grad(at):
        columns = pl.ds(pl.multiple_of(at * TILE, TILE), TILE)
        big[0:ROWS, columns] = dot(grad_low[...], flat_weights[2, :, columns]).astype(b16)

    def gate_up(at):
        columns = pl.ds(at * TILE, TILE)
        gate = dot(second_low[0:ROWS, :], flat_weights[0, :, columns])
        up = dot(second_low[0:ROWS, :], flat_weights[1, :, columns])
        grad_inner = big[0:ROWS, columns].astype(f32)
        sigmoid = jax.nn.sigmoid(gate)
        active = gate * sigmoid
        big[0:ROWS, columns] = (active * up).astype(b16)
        big[ROWS : 2 * ROWS, columns] = (
            grad_inner * up * sigmoid * (1.0 + gate * (1.0 - sigmoid))
        ).astype(b16)
        big[2 * ROWS :, columns] = (grad_inner * active).astype(b16)

    def give_second(slot):
        rows = slot_rows(slot)
        part = dot_t(big[ROWS : 2 * ROWS, :], flat_weights[0, rows, :])
        part = part + dot_t(big[2 * ROWS :, :], flat_weights[1, rows, :])
        second.give(part, slot)

    def give_branch(slot):
        branch.give(dot_t(big[0:ROWS, :], flat_weights[2, slot_rows(slot), :]), slot)

    def give_first(slot):
        first.give(dot_t(grad_proj[...], flat_io[slot_rows(slot), : 3 * CHANNELS]), slot)

    def gradient(left, at, member):
        @pl.loop(0, tiles)
        def _(tile):
            columns = pl.ds(pl.multiple_of(tile * TILE, TILE), TILE)
            flat_weights[at, :, columns] = dot(
                left[...], big[member * ROWS : (member + 1) * ROWS, columns]
            ).astype(b16)

    def exchange(phase, start, devices):
        for at, device in enumerate(devices):
            remote(
                small, small_recv.at[start + at], small_sems.at[0, phase], small_sems.at[1, phase], device
            ).start()

    def added(phase, start, count):
        spots = small_recv.at[pl.ds(start, count)]
        for side in range(2):
            wait_bytes(spots, small_sems.at[side, phase])
        total = small[...]
        for at in range(count):
            total = total + small_recv[start + at]
        small[...] = total

    io_gather.start()
    x_copy.wait()

    @pl.loop(0, ROWS, step=64)
    def _(at):
        input_low[pl.ds(at, 64), :] = normed_low(send_b[pl.ds(at, 64), :])

    down_gather.start()
    io_gather.first()
    io_gather.first_far()
    io_gather.second(0)
    io_gather.second(1)
    low_copy.wait()
    positions = place.ctx * SLOT_ROWS + lax.broadcasted_iota(jnp.int32, (SLOT_ROWS, 1), 0)
    for slot in range(2):
        rows = slice(slot * SLOT_ROWS, (slot + 1) * SLOT_ROWS)
        kept = jnp.where(positions < lengths[slot], 1.0, 0.0)
        grad_low[rows, :] = (grad_low[rows, :].astype(f32) * kept).astype(b16)
    io_gather.second(3)
    io_gather.second(2)
    io_gather.second_far(0)
    send_edges()
    early_gather.start()
    io_gather.second_far(1)
    io_gather.second_far(3)
    io_gather.second_far(2)
    wait_bytes(edges, edge_sems.at[1])
    wait_bytes(edges, edge_sems.at[0])
    for side in range(2):
        rows = pl.ds(ROWS + side * 2 * EDGE, 2 * EDGE)
        input_low[rows, :] = normed_low(edges[side].reshape(2 * EDGE, WIDTH))
    down_gather.first()
    io_gather.finish()
    project(0)
    project(1)
    project(2)
    product[:, 8:, :] = (projected[0, :ROWS] * projected[2, :ROWS]).reshape(
        2, SLOT_ROWS, CHANNELS
    )
    before = (
        projected[0, ROWS : ROWS + 2 * EDGE] * projected[2, ROWS : ROWS + 2 * EDGE]
    ).reshape(2, EDGE, CHANNELS)
    product[:, :8, :] = jnp.where(place.ctx > 0, before[:, EDGE - 8 :, :], 0.0)
    convolved[...] = (
        taps[0:1, :] * product[:, 6 : 6 + SLOT_ROWS, :]
        + taps[1:2, :] * product[:, 7 : 7 + SLOT_ROWS, :]
        + taps[2:3, :] * product[:, 8 : 8 + SLOT_ROWS, :]
    ).reshape(ROWS, CHANNELS)
    gated[...] = (projected[1, :ROWS] * convolved[...]).astype(b16)

    give_mixed(0)
    down_gather.first_far()
    late_gather.start()
    turned(grad_low, turn_a)
    give_mixed(1)
    down_gather.second(1)
    early_gather.first()
    early_gather.second(0)
    mixed.relay(0)
    down_gather.second(3)
    give_mixed(2)
    mixed.relay(1)
    mixed.relay(2)
    down_gather.second(0)
    early_gather.second(3)
    down_gather.second(2)
    own_copy.wait()
    stream = x_own[...].astype(f32) + mixed.take()
    residual[...] = stream
    normed, _ = norm_of(stream)
    second_low[own_rows, :] = (normed * gains[1:2, :]).astype(b16)
    second_spread.start()
    early_gather.first_far()
    down_gather.second_far(3)
    down_gather.second_far(1)
    early_gather.second(1)
    late_gather.first()
    down_gather.second_far(2)
    down_gather.second_far(0)
    second_spread.relay()
    down_gather.finish()
    early_gather.second(2)
    late_gather.first_far()
    pl.loop(3, 5)(inner_grad)
    early_gather.second_far(1)
    early_gather.second_far(0)
    pl.loop(0, 3)(inner_grad)
    early_gather.second_far(3)
    late_gather.second(0)
    late_gather.second(1)
    early_gather.second_far(2)
    late_gather.second(3)
    pl.loop(5, 7)(inner_grad)
    late_gather.second(2)
    early_gather.finish()
    late_gather.second_far(0)
    second_spread.finish()
    gate_up(2)
    late_gather.second_far(1)
    gate_up(3)
    late_gather.second_far(3)
    late_gather.second_far(2)
    gate_up(0)
    gate_up(1)
    late_gather.finish()
    gate_up(4)
    gate_up(6)
    gate_up(5)
    mixed.drain()
    give_branch(0)
    for part in (io_gather, down_gather, early_gather, late_gather, second_spread):
        part.drain()
    give_second(0)
    give_second(1)
    turned(second_low, turn_b)
    give_second(2)
    gradient(turn_b, 0, 1)
    gate_piece.to_sibling()
    second.relay(1)
    second.relay(0)
    second.relay(2)
    give_branch(1)
    branch.relay(0)
    gradient(turn_b, 1, 2)
    up_piece.to_sibling()
    normed, inverse = norm_of(residual[...])
    grad_second = second.take()
    small[...] = jnp.zeros_like(small)
    small[1:2, :] = jnp.sum(grad_second * normed, axis=0, keepdims=True)
    grad_stream = grad_low[own_rows, :].astype(f32) + norm_back(
        grad_second, normed, inverse, gains[1:2, :]
    )
    grad_own[...] = grad_stream
    second_low[own_rows, :] = grad_stream.astype(b16)
    low_spread.start()
    for tp in range(4):

        @pl.when(even)
        def _():
            remote(
                edge_source, edge_target, edge_sems.at[2], edge_sems.at[3], place.along_ctx(-1, tp)
            ).start()

    gate_piece.second_start()
    up_piece.second_start()
    low_spread.relay()
    give_branch(2)
    gradient(turn_a, 2, 0)
    down_piece.to_sibling()
    branch.relay(1)
    up_piece.second_relay()
    low_spread.finish()
    wait_bytes(second_low.at[pl.ds(ROWS, 2 * EDGE)], edge_sems.at[3])

    @pl.when(even)
    def _():
        wait_bytes(second_low.at[pl.ds(0, 4 * EDGE)], edge_sems.at[2])

    grad_gated = dot(second_low[...], flat_io[:, 3 * CHANNELS :])
    conv_grad[:, :SLOT_ROWS, :] = (grad_gated[:ROWS] * projected[1, :ROWS]).reshape(
        2, SLOT_ROWS, CHANNELS
    )
    after = (grad_gated[ROWS:] * projected[1, ROWS + 2 * EDGE :]).reshape(2, EDGE, CHANNELS)
    conv_grad[:, SLOT_ROWS:, :] = jnp.where(place.ctx < 15, after[:, :8, :], 0.0)
    grad_proj[:, CHANNELS : 2 * CHANNELS] = (grad_gated[:ROWS] * convolved[...]).astype(b16)
    branch.relay(2)
    grad_product = (
        taps[2:3, :] * conv_grad[:, 0:SLOT_ROWS, :]
        + taps[1:2, :] * conv_grad[:, 1 : 1 + SLOT_ROWS, :]
        + taps[0:1, :] * conv_grad[:, 2 : 2 + SLOT_ROWS, :]
    ).reshape(ROWS, CHANNELS)
    grad_proj[:, 0:CHANNELS] = (grad_product * projected[2, :ROWS]).astype(b16)
    grad_proj[:, 2 * CHANNELS :] = (grad_product * projected[0, :ROWS]).astype(b16)
    second.drain()
    give_first(0)
    give_first(1)
    gate_piece.second_relay()
    give_first(2)
    for tap in range(3):
        small[2 + tap : 3 + tap, own_columns] = jnp.sum(
            conv_grad[:, :SLOT_ROWS, :] * product[:, 6 + tap : 6 + tap + SLOT_ROWS, :], axis=(0, 1)
        ).reshape(1, CHANNELS)
    down_piece.second_start()
    turned(input_low, turn_a)
    up_piece.first_start()
    first.relay(0)
    turned(second_low, turn_b)
    gate_piece.first_start()
    first.relay(1)
    block_own[...] = (residual[...] + branch.take()).astype(b16)
    block_keep.start()
    first.relay(2)
    block_spread.start()
    big[:, : 2 * CHANNELS] = dot(turn_a[...], grad_proj[:, : 2 * CHANNELS]).astype(b16)
    io_piece.to_sibling(0, 2 * CHANNELS)
    big[:, 2 * CHANNELS : 3 * CHANNELS] = dot(turn_a[...], grad_proj[:, 2 * CHANNELS :]).astype(b16)
    big[:, 3 * CHANNELS : 4 * CHANNELS] = dot(turn_b[...], gated[...]).astype(b16)
    io_piece.to_sibling(2 * CHANNELS, 2 * CHANNELS)
    down_piece.second_relay()
    normed, inverse = norm_of(x_own[...].astype(f32))
    grad_first = first.take()
    small[0:1, :] = jnp.sum(grad_first * normed, axis=0, keepdims=True)
    input_own[...] = (
        grad_own[...] + norm_back(grad_first, normed, inverse, gains[0:1, :])
    ).astype(b16)
    input_keep.start()
    exchange(0, 0, [place.along_tp(by) for by in (1, 2, 3)])
    input_spread.start()
    gate_piece.first_relay()
    io_piece.second_start()
    io_piece.second_relay()
    down_piece.first_start()
    up_piece.first_relay()
    input_spread.relay()
    added(0, 0, 3)
    exchange(1, 3, [place.sibling()])
    down_piece.first_relay()
    added(1, 3, 1)
    exchange(2, 4, [place.along_first(by) for by in (1, 2, 3)])
    block_spread.relay()
    io_piece.first_start()
    gate_piece.finish()
    added(2, 4, 3)
    exchange(3, 7, [place.along_second(by) for by in (1, 2, 3)])
    io_piece.first_relay()
    down_piece.finish()
    input_spread.finish()
    up_piece.finish()
    added(3, 7, 3)
    small[2:5, :CHANNELS] = small[2:5, own_columns]
    io_piece.finish()
    block_spread.finish()
    block_keep.wait()
    input_keep.wait()
    for part in (low_spread, block_spread, input_spread, first, branch):
        part.drain()
    for part in (down_piece, gate_piece, up_piece, io_piece):
        part.drain()


def step(*given):
    vmem = pl.BlockSpec(memory_space=pltpu.VMEM)
    smem = pl.BlockSpec(memory_space=pltpu.SMEM)
    hbm = pl.BlockSpec(memory_space=pl.ANY)
    f32, b16 = jnp.float32, jnp.bfloat16
    dma = pltpu.SemaphoreType.DMA
    own16 = pltpu.VMEM((QUARTER, WIDTH), b16)
    own32 = pltpu.VMEM((QUARTER, WIDTH), f32)
    full = pltpu.VMEM((ROWS, WIDTH), b16)
    across = pltpu.VMEM((WIDTH, ROWS), b16)
    return pl.pallas_call(
        kernel,
        out_shape=(
            jax.ShapeDtypeStruct((ROWS, WIDTH), b16),
            jax.ShapeDtypeStruct((ROWS, WIDTH), b16),
            jax.ShapeDtypeStruct((3, 16, BLOCK, PADDED), b16),
            jax.ShapeDtypeStruct((3, 12, BLOCK, PADDED), b16),
            jax.ShapeDtypeStruct((BLOCK, WIDE), f32),
            jax.ShapeDtypeStruct((3, BLOCK, PADDED), f32),
            jax.ShapeDtypeStruct((8, WIDTH), f32),
        ),
        in_specs=[hbm, hbm, smem] + [vmem] * 6,
        out_specs=(hbm,) * 4 + (vmem,) * 3,
        scratch_shapes=[
            pltpu.VMEM((BLOCK, WIDE), b16),
            pltpu.VMEM((3, BLOCK, PADDED), b16),
            pltpu.VMEM((32, BLOCK, WIDE), b16),
            pltpu.VMEM((3, 32, BLOCK, PADDED), b16),
            pltpu.VMEM((WIDTH, PADDED), b16),
            pltpu.VMEM((ROWS, 3 * CHANNELS), b16),
            full,
            own16,
            pltpu.VMEM((2, 2, EDGE, WIDTH), b16),
            pltpu.VMEM((ROWS + 4 * EDGE, WIDTH), b16),
            across,
            across,
            full,
            full,
            pltpu.VMEM((2, 2, HALF, WIDTH), b16),
            pltpu.VMEM((2, 2, QUARTER, WIDTH), b16),
            pltpu.VMEM((ROWS + 2 * EDGE, WIDTH), b16),
            own32,
            pltpu.VMEM((3, ROWS + 4 * EDGE, CHANNELS), f32),
            pltpu.VMEM((2, 8 + SLOT_ROWS, CHANNELS), f32),
            pltpu.VMEM((ROWS, CHANNELS), f32),
            pltpu.VMEM((ROWS, CHANNELS), b16),
            own32,
            own16,
            own16,
            pltpu.VMEM((2, SLOT_ROWS + 8, CHANNELS), f32),
            pltpu.VMEM((16, BLOCK, PADDED), b16),
            pltpu.VMEM((3, 3, BLOCK, PADDED), b16),
            pltpu.VMEM((16, BLOCK, WIDE), b16),
            pltpu.VMEM((12, BLOCK, WIDE), b16),
            pltpu.VMEM((10, 8, WIDTH), f32),
            dma((Gather.SEMS,)),
            dma((Gather.SEMS,)),
            dma((Gather.SEMS,)),
            dma((Gather.SEMS,)),
            dma((4, Scatter.SEMS)),
            dma((4, TpSum.SEMS)),
            dma((4, TpSpread.SEMS)),
            dma((4,)),
            dma((2, 4)),
            dma((6,)),
        ],
        compiler_params=pltpu.CompilerParams(
            collective_id=0, has_side_effects=True, vmem_limit_bytes=63 * 2**20
        ),
        name="step",
    )(*given)


def nesterov(weight, moment, average, gradient, step_rate):
    moment_new = momentum * moment + gradient
    weight_new = weight - step_rate * (gradient + momentum * moment_new)
    average_new = average_decay * average + (1.0 - average_decay) * weight_new
    return (moment_new, weight_new, average_new)


def update_kernel(*refs):
    block_in, input_in = refs[:2]
    old = [refs[2 + 3 * at : 5 + 3 * at] for at in range(4)]
    small_old = refs[14:20]
    io_grad, gud_grad, small = refs[20:23]
    block_out, input_out = refs[23:25]
    new = [refs[25 + 3 * at : 28 + 3 * at] for at in range(4)]
    small_new = refs[37:43]
    block_held, input_held, wide_held = refs[43:46]
    held = [refs[46 + 3 * at : 49 + 3 * at] for at in range(4)]
    in_sems, out_sems = refs[58:]

    def moved(source, target, sems, at):
        copy = pltpu.make_async_copy(source, target, sems.at[at])
        copy.start()
        return copy

    order = (2, 3, 0, 1)
    loads = {}
    input_load = moved(input_in, input_held, in_sems, 12)
    block_load = moved(block_in, block_held, in_sems, 13)
    for matrix in order:
        loads[matrix] = [
            moved(old[matrix][at], held[matrix][at], in_sems, 3 * matrix + at) for at in range(3)
        ]
    stores = []
    input_load.wait()
    for half in range(2):
        rows = pl.ds(half * SLOT_ROWS, SLOT_ROWS)
        wide_held[rows, :] = input_held[rows, :].astype(jnp.float32)
        stores.append(moved(wide_held.at[rows], input_out.at[rows], out_sems, 12 + half))
    block_load.wait()
    stores.append(moved(block_held, block_out, out_sems, 14))
    for matrix in order:
        for copy in loads[matrix]:
            copy.wait()
        weight, moment, average = held[matrix]
        if matrix == 0:
            parts = [(at, io_grad[:, at * CHANNELS : (at + 1) * CHANNELS]) for at in range(3)]
        elif matrix == 1:
            parts = [(slice(None), io_grad[:, 3 * CHANNELS :])]
        elif matrix == 2:
            parts = [(at, gud_grad[at, :, :HIDDEN]) for at in range(2)]
        else:
            parts = [(slice(None), gud_grad[2, :, :HIDDEN])]
        for at, gradient in parts:
            moment[at], weight[at], average[at] = nesterov(
                weight[at], moment[at], average[at], gradient, matrix_rate
            )
        for at, source in enumerate((moment, weight, average)):
            stores.append(moved(source, new[matrix][at], out_sems, 3 * matrix + at))
    for group, rows, columns in ((0, slice(0, 2), slice(None)), (3, slice(2, 5), slice(0, CHANNELS))):
        weight, moment, average = small_old[group : group + 3]
        results = nesterov(weight[...], moment[...], average[...], small[rows, columns], small_rate)
        for at in range(3):
            small_new[group + at][...] = results[at]
    for copy in stores:
        copy.wait()


def update(block, input_low, matrices, smalls, io_grad, gud_grad, small):
    vmem = pl.BlockSpec(memory_space=pltpu.VMEM)
    hbm = pl.BlockSpec(memory_space=pl.ANY)
    f32 = jnp.float32
    like = lambda a: jax.ShapeDtypeStruct(a.shape, a.dtype)
    return pl.pallas_call(
        update_kernel,
        out_shape=(
            like(block),
            jax.ShapeDtypeStruct((ROWS, WIDTH), f32),
            *[like(a) for a in matrices],
            *[like(a) for a in smalls],
        ),
        in_specs=[hbm] * 14 + [vmem] * 9,
        out_specs=(hbm,) * 14 + (vmem,) * 6,
        scratch_shapes=[
            pltpu.VMEM((ROWS, WIDTH), jnp.bfloat16),
            pltpu.VMEM((ROWS, WIDTH), jnp.bfloat16),
            pltpu.VMEM((ROWS, WIDTH), f32),
            *[pltpu.VMEM(a.shape, f32) for a in matrices],
            pltpu.SemaphoreType.DMA((14,)),
            pltpu.SemaphoreType.DMA((15,)),
        ],
        compiler_params=pltpu.CompilerParams(vmem_limit_bytes=62 * 2**20),
        name="update",
    )(block, input_low, *matrices, *smalls, io_grad, gud_grad, small)


def on_device(
    hidden,
    lengths,
    cotangent,
    in_weight,
    in_moment,
    in_average,
    out_weight,
    out_moment,
    out_average,
    gate_up_weight,
    gate_up_moment,
    gate_up_average,
    down_weight,
    down_moment,
    down_average,
    norm_gains,
    gain_moment,
    gain_average,
    conv_taps,
    taps_moment,
    taps_average,
):
    slot_count, seq_len, model_width = hidden.shape
    row_count = slot_count * seq_len
    block_output, input_low_grad, _, _, io_sum, gud_sum, small = step(
        hidden.reshape(row_count, model_width),
        cotangent.reshape(row_count, model_width),
        lengths,
        in_weight,
        out_weight.T,
        gate_up_weight,
        down_weight.T,
        norm_gains,
        conv_taps,
    )
    matrices = (
        (in_weight, in_moment, in_average),
        (out_weight.T, out_moment.T, out_average.T),
        (gate_up_weight, gate_up_moment, gate_up_average),
        (down_weight.T, down_moment.T, down_average.T),
    )
    smalls = (norm_gains, gain_moment, gain_average, conv_taps, taps_moment, taps_average)
    block_output, input_grad, *new = update(
        block_output,
        input_low_grad,
        [a for group in matrices for a in group],
        smalls,
        io_sum,
        gud_sum,
        small,
    )
    return (
        block_output.reshape(slot_count, seq_len, model_width),
        input_grad.reshape(slot_count, seq_len, model_width),
        *new[0:3],
        *[a.T for a in new[3:6]],
        *new[6:9],
        *[a.T for a in new[9:12]],
        *new[12:18],
    )


def solution(mesh):
    placed = (
        P("shard", "ctx", None),
        P("shard"),
        P("shard", "ctx", None),
        P(None, ("shard", "ctx"), "tp"),
        P(None, ("shard", "ctx"), "tp"),
        P(None, ("shard", "ctx"), "tp"),
        P("tp", ("shard", "ctx")),
        P("tp", ("shard", "ctx")),
        P("tp", ("shard", "ctx")),
        P(None, ("shard", "ctx"), "tp"),
        P(None, ("shard", "ctx"), "tp"),
        P(None, ("shard", "ctx"), "tp"),
        P("tp", ("shard", "ctx")),
        P("tp", ("shard", "ctx")),
        P("tp", ("shard", "ctx")),
        P(),
        P(),
        P(),
        P(None, "tp"),
        P(None, "tp"),
        P(None, "tp"),
    )
    return jax.shard_map(
        on_device,
        mesh=mesh,
        in_specs=placed,
        out_specs=(
            P("shard", "ctx", None),
            P("shard", "ctx", None),
            P(None, ("shard", "ctx"), "tp"),
            P(None, ("shard", "ctx"), "tp"),
            P(None, ("shard", "ctx"), "tp"),
            P("tp", ("shard", "ctx")),
            P("tp", ("shard", "ctx")),
            P("tp", ("shard", "ctx")),
            P(None, ("shard", "ctx"), "tp"),
            P(None, ("shard", "ctx"), "tp"),
            P(None, ("shard", "ctx"), "tp"),
            P("tp", ("shard", "ctx")),
            P("tp", ("shard", "ctx")),
            P("tp", ("shard", "ctx")),
            P(),
            P(),
            P(),
            P(None, "tp"),
            P(None, "tp"),
            P(None, "tp"),
        ),
        check_vma=False,
    )
```

```python
import functools

import jax
import jax.numpy as jnp
from jax import lax
from jax.experimental import pallas as pl
from jax.experimental.pallas import tpu as pltpu
from jax.sharding import PartitionSpec as P

MESH = pl.DeviceIdType.MESH
epsilon = 1e-05
momentum = 0.9
average_decay = 0.9
matrix_rate = 0.0004
small_rate = 0.005
WIDTH = 1536
CHANNELS = 384
HIDDEN = 1728
TILE = 256
EDGE = 16
EARLY = 4
SLOTS = ((0, 512), (512, 512), (1024, 512))
WIDE = 4 * CHANNELS
PADDED = 1792
ROWS = 512
QUARTER = 128
SLOT_ROWS = 256
BLOCK = 48
HALF = QUARTER // 2


class Place:
    def __init__(self):
        self.shard = lax.axis_index("shard")
        self.ctx = lax.axis_index("ctx")
        self.tp = lax.axis_index("tp")
        self.y = self.shard * 2 + lax.div(self.ctx, 8)
        self.z = lax.rem(lax.div(self.ctx, 2), 4)
        self.core = lax.rem(self.ctx, 2)
        self.first = self.y * (1 - self.core) + self.z * self.core
        self.second = self.z * (1 - self.core) + self.y * self.core

    def turn(self, value, by):
        return lax.rem(value + by + 4, 4)

    def device(self, y, z, core):
        return (lax.div(y, 2), lax.rem(y, 2) * 8 + z * 2 + core, self.tp)

    def grid_device(self, first, second):
        y = first * (1 - self.core) + second * self.core
        z = second * (1 - self.core) + first * self.core
        return self.device(y, z, self.core)

    def block(self, first, second):
        y = first * (1 - self.core) + second * self.core
        z = second * (1 - self.core) + first * self.core
        return y * 8 + z * 2 + self.core

    def along_first(self, by):
        return self.grid_device(self.turn(self.first, by), self.second)

    def along_second(self, by):
        return self.grid_device(self.first, self.turn(self.second, by))

    def along_tp(self, by):
        return (self.shard, self.ctx, self.turn(self.tp, by))

    def along_ctx(self, by, tp=None):
        return (self.shard, lax.rem(self.ctx + by + 16, 16), self.tp if tp is None else tp)

    def sibling(self):
        return self.device(self.y, self.z, 1 - self.core)

    def greet(self):
        barrier = pltpu.get_barrier_semaphore()
        friends = [self.sibling()]
        for tp in range(4):
            friends += [self.along_ctx(1, tp), self.along_ctx(-1, tp)]
        for by in (1, 2, 3):
            friends += [self.along_first(by), self.along_second(by), self.along_tp(by)]
        for friend in friends:
            pl.semaphore_signal(barrier, inc=1, device_id=friend, device_id_type=MESH)
        return len(friends)


def remote(source, target, send_sem, recv_sem, device):
    return pltpu.make_async_remote_copy(
        src_ref=source,
        dst_ref=target,
        send_sem=send_sem,
        recv_sem=recv_sem,
        device_id=device,
        device_id_type=MESH,
    )


def wait_bytes(spot, sem):
    pltpu.make_async_copy(spot, spot, sem).wait()


class Gather:
    SEMS = 12

    def __init__(self, place, local, whole, sems):
        self.place, self.local, self.whole, self.sems = place, local, whole, sems
        self.half = local.shape[-1] // 2

    def part(self, block, half=None):
        spot = self.whole.at[:, block] if self.whole.ndim == 4 else self.whole.at[block]
        if half is None:
            return spot
        columns = pl.ds(half * self.half, self.half)
        return spot.at[:, :, columns] if self.whole.ndim == 4 else spot.at[:, columns]

    def send(self, source, target, at, device):
        remote(source, target, self.sems.at[0], self.sems.at[at], device).start()

    def arrived(self, blocks, at):
        few = pl.ds(0, blocks)
        wait_bytes(self.whole.at[:, few] if self.whole.ndim == 4 else self.whole.at[few], self.sems.at[at])

    def block(self, back, by):
        p = self.place
        return p.block(p.turn(p.first, -back), p.turn(p.second, -by))

    def to_second(self, source, back, by):
        spot = self.part(self.block(back, 0))
        self.send(source, spot, 3 + back, self.place.along_second(1))
        self.send(source, spot, 3 + back, self.place.along_second(-1))
        self.to_sibling(source, back, by)

    def to_sibling(self, source, back, by):
        self.send(source, self.part(self.block(back, by)), 11, self.place.sibling())

    def start(self):
        p = self.place
        spot = self.part(self.block(0, 0))
        self.send(self.local, spot, 1, p.along_first(1))
        self.send(self.local, spot, 1, p.along_first(-1))
        self.to_second(self.local, 0, 0)

    def first(self):
        p = self.place
        self.arrived(2, 1)
        for back, half, by in ((1, 0, 1), (3, 1, -1)):
            piece = self.part(self.block(back, 0), half)
            self.send(piece, piece, 2, p.along_first(by))
        for back in (1, 3):
            self.to_second(self.part(self.block(back, 0)), back, 0)

    def first_far(self):
        self.arrived(1, 2)
        self.to_second(self.part(self.block(2, 0)), 2, 0)

    def second(self, back):
        p = self.place
        self.arrived(2, 3 + back)
        for by, half, step in ((1, 0, 1), (3, 1, -1)):
            piece = self.part(self.block(back, by), half)
            self.send(piece, piece, 7 + back, p.along_second(step))
        for by in (1, 3):
            self.to_sibling(self.part(self.block(back, by)), back, by)

    def second_far(self, back):
        self.arrived(1, 7 + back)
        self.to_sibling(self.part(self.block(back, 2)), back, 2)

    def finish(self):
        self.arrived(16, 11)

    def drain(self):
        self.arrived(31, 0)


class Scatter:
    SEMS = 6

    def __init__(self, place, partial, width, recv, out, stage, sems, local_sems):
        self.place, self.width, self.out = place, width, out
        self.sib_recv, self.second_recv, self.first_recv = recv
        self.stage, self.sems, self.local_sems = stage, sems, local_sems
        columns = pl.ds(0, width)
        self.blocks = partial.reshape(16, 2, BLOCK, PADDED).at[:, :, :, columns]
        self.grid = partial.reshape(4, 4, 2, BLOCK, PADDED).at[:, :, :, :, columns]
        self.rows = partial.reshape(32, BLOCK, PADDED).at[:, :, columns]

    def mine(self, first, second):
        return lax.div(self.place.block(first, second), 2)

    def arrived(self, spot, at):
        wait_bytes(spot, self.sems.at[at])

    def move(self, source, target, at, device):
        remote(source, target, self.sems.at[0], self.sems.at[at], device).start()

    def to_sibling(self, start=0, width=None):
        p = self.place
        columns = pl.ds(start, self.width if width is None else width)
        source = self.blocks.at[:, 1 - p.core, :, columns]
        self.move(source, self.sib_recv.at[:, :, columns], 1, p.sibling())

    def fetch(self, source, count):
        if self.stage is None:
            return source
        target = self.stage.at[pl.ds(0, count), :, pl.ds(0, self.width)]
        copy = pltpu.make_async_copy(source, target, self.local_sems.at[0])
        copy.start()
        copy.wait()
        return target

    def add_to(self, at, held, parts):
        core = self.place.core
        if len(parts) == 1:
            self.blocks[at, core] = self.blocks[at, core] + held[parts[0]]
        else:
            total = self.blocks[at, core].astype(jnp.float32)
            for part in parts:
                total = total + held[part].astype(jnp.float32)
            self.blocks[at, core] = total.astype(jnp.bfloat16)

    def pair(self, half, by, target, at, step):
        p = self.place
        there = p.turn(p.second, by)
        two = pl.ds(2 * half, 2)

        @pl.when(p.core == 0)
        def _():
            self.move(self.grid.at[two, there, 0], target, at, p.along_second(step))

        @pl.when(p.core == 1)
        def _():
            self.move(self.grid.at[there, two, 1], target, at, p.along_second(step))

    def second_start(self):
        p = self.place
        self.arrived(self.sib_recv, 1)
        held = self.fetch(self.sib_recv, 16)

        @pl.loop(0, 4)
        def _(first):
            at = self.mine(first, p.turn(p.second, 2))
            self.add_to(at, held, [at])

        for half, step in ((0, 1), (1, -1)):
            self.pair(half, 2, self.second_recv.at[pl.ds(8 + 2 * half, 2)], 2, step)

        @pl.loop(0, 12)
        def _(other):
            away = lax.rem(lax.div(other, 4) + 3, 4)
            at = self.mine(lax.rem(other, 4), p.turn(p.second, away))
            self.add_to(at, held, [at])

        for half, step in ((0, 1), (1, -1)):
            spot = self.second_recv.at[pl.ds(4 * half + 2 * (1 - half), 2)]
            self.pair(1 - half, step, spot, 3, step)

    def second_relay(self):
        p = self.place
        self.arrived(self.second_recv.at[pl.ds(8, 4)], 2)
        held = self.fetch(self.second_recv.at[pl.ds(8, 4)], 4)
        for half, step in ((0, 1), (1, -1)):

            @pl.loop(0, 2)
            def _(first):
                at = self.mine(2 * half + first, p.turn(p.second, step))
                self.add_to(at, held, [2 * half + first])

            spot = self.second_recv.at[pl.ds(4 * half + 2 * half, 2)]
            self.pair(half, step, spot, 3, step)

    def first_start(self):
        p = self.place
        self.arrived(self.second_recv.at[pl.ds(0, 8)], 3)
        held = self.fetch(self.second_recv.at[pl.ds(0, 8)], 8)

        @pl.loop(0, 4)
        def _(first):
            self.add_to(self.mine(first, p.second), held, [first, 4 + first])

        for half, step in ((0, 1), (1, -1)):
            self.strip(half, 2, self.first_recv.at[2], 4, step)
        for half, step in ((0, 1), (1, -1)):
            self.strip(1 - half, step, self.first_recv.at[half], 5, step)

    def columns(self, half):
        return pl.ds(half * (self.width // 2), self.width // 2)

    def strip(self, half, by, target, at, step):
        p = self.place
        source = self.blocks.at[self.mine(p.turn(p.first, by), p.second), p.core]
        columns = self.columns(half)
        self.move(source.at[:, columns], target.at[:, columns], at, p.along_first(step))

    def first_relay(self):
        p = self.place
        self.arrived(self.first_recv.at[2], 4)
        for half, step in ((0, 1), (1, -1)):
            columns = self.columns(half)
            at = self.mine(p.turn(p.first, step), p.second)
            both = self.blocks[at, p.core, :, columns].astype(jnp.float32)
            both = both + self.first_recv[2, :, columns].astype(jnp.float32)
            self.blocks[at, p.core, :, columns] = both.astype(jnp.bfloat16)
            self.strip(half, step, self.first_recv.at[half], 5, step)

    def finish(self):
        p = self.place
        self.arrived(self.first_recv.at[pl.ds(0, 2)], 5)
        total = self.blocks[self.mine(p.first, p.second), p.core].astype(jnp.float32)
        for by in range(2):
            total = total + self.first_recv[by].astype(jnp.float32)
        wide, out, members, columns, sem = self.out
        for member in range(members):
            wide[member] = total[:, member * columns : (member + 1) * columns]
        copy = pltpu.make_async_copy(wide, out, sem)
        copy.start()
        self.store = copy

    def drain(self):
        self.arrived(self.rows.at[pl.ds(0, 31)], 0)
        self.store.wait()


class TpSum:
    SEMS = 5

    def __init__(self, place, send, relay, final, sems):
        self.place, self.send, self.relay_in, self.final = place, send, relay, final
        self.sems = sems

    def rows(self, by, half):
        p = self.place
        start = p.turn(p.tp, by) * QUARTER + half * HALF
        return pl.ds(pl.multiple_of(start, HALF), HALF)

    def move(self, source, target, at, by):
        remote(source, target, self.sems.at[0], self.sems.at[at], self.place.along_tp(by)).start()

    def give(self, values, slot):
        columns = pl.ds(*SLOTS[slot])
        self.send[:, columns] = values.astype(jnp.bfloat16)
        for half, by in ((0, 1), (1, -1)):
            source = self.send.at[self.rows(2, half), columns]
            self.move(source, self.relay_in.at[half, :, columns], 2 + slot, by)
        for half, by in ((0, 1), (1, -1)):
            source = self.send.at[self.rows(by, 1 - half), columns]
            target = self.final.at[half, pl.ds((1 - half) * HALF, HALF), columns]
            self.move(source, target, 1, by)

    def relay(self, slot):
        columns = pl.ds(*SLOTS[slot])
        wait_bytes(self.relay_in.at[:, :, columns], self.sems.at[2 + slot])
        for half, by in ((0, 1), (1, -1)):
            rows = self.rows(by, half)
            both = self.send[rows, columns].astype(jnp.float32)
            both = both + self.relay_in[half, :, columns].astype(jnp.float32)
            self.send[rows, columns] = both.astype(jnp.bfloat16)
            target = self.final.at[half, pl.ds(half * HALF, HALF), columns]
            self.move(self.send.at[rows, columns], target, 1, by)

    def take(self):
        p = self.place
        wait_bytes(self.final, self.sems.at[1])
        rows = pl.ds(pl.multiple_of(p.tp * QUARTER, QUARTER), QUARTER)
        total = self.send[rows, :].astype(jnp.float32)
        for half in range(2):
            total = total + self.final[half].astype(jnp.float32)
        return total

    def drain(self):
        wait_bytes(self.send.at[pl.ds(0, 3 * QUARTER)], self.sems.at[0])


class TpSpread:
    SEMS = 3

    def __init__(self, place, source, whole, sems):
        self.place, self.source, self.whole, self.sems = place, source, whole, sems

    def spot(self, by, half):
        p = self.place
        start = p.turn(p.tp, by) * QUARTER + half * HALF
        return self.whole.at[pl.ds(pl.multiple_of(start, HALF), HALF)]

    def move(self, source, target, at, by):
        remote(source, target, self.sems.at[0], self.sems.at[at], self.place.along_tp(by)).start()

    def start(self):
        for at, half, by in ((1, 0, 1), (1, 1, -1), (2, 1, 1), (2, 0, -1)):
            self.move(self.source.at[pl.ds(half * HALF, HALF)], self.spot(0, half), at, by)

    def arrived(self, rows, at):
        wait_bytes(self.whole.at[pl.ds(0, rows)], self.sems.at[at])

    def relay(self):
        self.arrived(QUARTER, 1)
        for half, by in ((0, 1), (1, -1)):
            spot = self.spot(-by, half)
            self.move(spot, spot, 2, by)

    def finish(self):
        self.arrived(2 * QUARTER, 2)

    def drain(self):
        self.arrived(3 * QUARTER, 0)


def dot(left, right):
    return jnp.dot(left, right, preferred_element_type=jnp.float32)


def dot_t(left, right):
    return lax.dot_general(
        left, right, (((1,), (1,)), ((), ())), preferred_element_type=jnp.float32
    )


def turned(source, target):
    @pl.loop(0, WIDTH // TILE)
    def _(at):
        at = pl.multiple_of(at * TILE, TILE)
        target[pl.ds(at, TILE), :] = source[pl.ds(0, ROWS), pl.ds(at, TILE)].T


def slot_rows(slot):
    start, width = SLOTS[slot]
    return slice(start, start + width)


def own_rows_of(place):
    return pl.ds(pl.multiple_of(place.tp * QUARTER, QUARTER), QUARTER)


def norm_of(values):
    inverse = lax.rsqrt(jnp.mean(values * values, axis=-1, keepdims=True) + epsilon)
    return values * inverse, inverse


def norm_back(grad, normed, inverse, gain):
    scaled = grad * gain
    return inverse * (scaled - normed * jnp.mean(scaled * normed, axis=-1, keepdims=True))


def kernel(
    x,
    cotangent,
    lengths,
    in_weight,
    out_weight,
    gate_up_weight,
    down_weight,
    gains,
    taps,
    block_out,
    input_out,
    sib_hbm,
    second_hbm,
    io_grad,
    gud_grad,
    small,
    io_wide,
    gud_wide,
    io_local,
    gud_local,
    io,
    weights,
    big,
    grad_proj,
    grad_low,
    x_own,
    edges,
    edge_send,
    edge_recv,
    input_low,
    turn_a,
    turn_b,
    send_a,
    send_b,
    relays,
    finals,
    second_low,
    residual,
    projected,
    product,
    convolved,
    gated,
    grad_own,
    block_own,
    input_own,
    conv_grad,
    stage,
    first_recv,
    io_sib_recv,
    io_second_recv,
    small_recv,
    io_sems,
    down_sems,
    early_sems,
    late_sems,
    scatter_sems,
    sum_sems,
    spread_sems,
    edge_sems,
    small_sems,
    local_sems,
):
    f32, b16 = jnp.float32, jnp.bfloat16
    place = Place()
    own_rows = own_rows_of(place)
    tiles = PADDED // TILE
    mine = place.block(place.first, place.second)
    flat_io = io.reshape(WIDTH, WIDE)
    flat_weights = weights.reshape(3, WIDTH, PADDED)

    loads = [
        pltpu.make_async_copy(source, target, local_sems.at[6 + at])
        for at, (source, target) in enumerate(
            (
                (in_weight, io_wide.at[pl.ds(0, 3)]),
                (out_weight, io_wide.at[3]),
                (gate_up_weight, gud_wide.at[pl.ds(0, 2)]),
                (down_weight, gud_wide.at[2]),
            )
        )
    ]
    x_copy = pltpu.make_async_copy(x, send_b, local_sems.at[1])
    low_copy = pltpu.make_async_copy(cotangent, grad_low, local_sems.at[2])
    own_copy = pltpu.make_async_copy(x.at[own_rows], x_own, local_sems.at[3])
    for copy in (*loads, x_copy, low_copy, own_copy):
        copy.start()
    friends = place.greet()
    for copy in loads:
        copy.wait()
    for member in range(4):
        io_local[:, member * CHANNELS : (member + 1) * CHANNELS] = io_wide[member].astype(b16)
        if member < 3:
            gud_local[member, :, :HIDDEN] = gud_wide[member].astype(b16)
    gud_local[:, :, HIDDEN:] = jnp.zeros((3, BLOCK, PADDED - HIDDEN), b16)
    io[mine] = io_local[...]
    weights[:, mine] = gud_local[...]
    pl.semaphore_wait(pltpu.get_barrier_semaphore(), friends)
    early, late = pl.ds(0, EARLY * TILE), pl.ds(EARLY * TILE, PADDED - EARLY * TILE)
    two = pl.ds(0, 2)
    io_gather = Gather(place, io_local, io, io_sems)
    down_gather = Gather(place, gud_local.at[2], weights.at[2], down_sems)
    early_gather = Gather(
        place, gud_local.at[two, :, early], weights.at[two, :, :, early], early_sems
    )
    late_gather = Gather(
        place, gud_local.at[two, :, late], weights.at[two, :, :, late], late_sems
    )
    mixed = TpSum(place, send_a, relays.at[0], finals.at[0], sum_sems.at[0])
    second = TpSum(place, send_b, relays.at[1], finals.at[1], sum_sems.at[1])
    branch = TpSum(place, send_a, relays.at[0], finals.at[0], sum_sems.at[2])
    first = TpSum(place, send_b, relays.at[1], finals.at[1], sum_sems.at[3])
    second_spread = TpSpread(place, second_low.at[own_rows], second_low, spread_sems.at[0])
    low_spread = TpSpread(place, second_low.at[own_rows], second_low, spread_sems.at[1])
    block_spread = TpSpread(place, block_own, block_out, spread_sems.at[2])
    input_spread = TpSpread(place, input_own, input_out, spread_sems.at[3])
    block_keep = pltpu.make_async_copy(block_own, block_out.at[own_rows], local_sems.at[4])
    input_keep = pltpu.make_async_copy(input_own, input_out.at[own_rows], local_sems.at[5])
    even = lax.rem(place.tp, 2) == 0

    def piece(at):
        return Scatter(
            place,
            flat_weights.at[at],
            PADDED,
            (sib_hbm.at[at], second_hbm.at[at], first_recv.at[at]),
            (
                gud_wide.at[pl.ds(at, 1)],
                gud_grad.at[pl.ds(at, 1)],
                1,
                HIDDEN,
                local_sems.at[6 + at],
            ),
            stage,
            scatter_sems.at[at],
            local_sems,
        )

    gate_piece, up_piece, down_piece = piece(0), piece(1), piece(2)
    io_piece = Scatter(
        place,
        big,
        WIDE,
        (io_sib_recv, io_second_recv, gud_local.at[:, :, pl.ds(0, WIDE)]),
        (io_wide, io_grad, 4, CHANNELS, local_sems.at[9]),
        None,
        scatter_sems.at[3],
        local_sems,
    )

    def normed_low(values):
        normed, _ = norm_of(values.astype(f32))
        return (normed * gains[0:1, :]).astype(b16)

    def send_edges():
        slots_x = x.reshape(2, SLOT_ROWS, WIDTH)
        for side, start, by in ((0, SLOT_ROWS - EDGE, 1), (1, 0, -1)):
            remote(
                slots_x.at[:, pl.ds(start, EDGE)],
                edges.at[side],
                edge_sems.at[0],
                edge_sems.at[1],
                place.along_ctx(by),
            ).start()

    def project(member):
        columns = slice(member * CHANNELS, (member + 1) * CHANNELS)
        projected[member] = dot(input_low[...], flat_io[:, columns])

    def give_mixed(slot):
        mixed.give(dot_t(gated[...], flat_io[slot_rows(slot), 3 * CHANNELS :]), slot)

    def inner_grad(at):
        columns = pl.ds(pl.multiple_of(at * TILE, TILE), TILE)
        big[0:ROWS, columns] = dot(grad_low[...], flat_weights[2, :, columns]).astype(b16)

    def gate_up(at):
        columns = pl.ds(at * TILE, TILE)
        gate = dot(second_low[0:ROWS, :], flat_weights[0, :, columns])
        up = dot(second_low[0:ROWS, :], flat_weights[1, :, columns])
        grad_inner = big[0:ROWS, columns].astype(f32)
        sigmoid = 0.5 * jnp.tanh(0.5 * gate) + 0.5
        active = gate * sigmoid
        big[0:ROWS, columns] = (active * up).astype(b16)
        big[ROWS : 2 * ROWS, columns] = (
            grad_inner * up * (sigmoid + active * (1.0 - sigmoid))
        ).astype(b16)
        big[2 * ROWS :, columns] = (grad_inner * active).astype(b16)

    def give_second(slot):
        rows = slot_rows(slot)
        part = dot_t(big[ROWS : 2 * ROWS, :], flat_weights[0, rows, :])
        part = part + dot_t(big[2 * ROWS :, :], flat_weights[1, rows, :])
        second.give(part, slot)

    def give_branch(slot):
        branch.give(dot_t(big[0:ROWS, :], flat_weights[2, slot_rows(slot), :]), slot)

    def give_first(slot):
        first.give(dot_t(grad_proj[...], flat_io[slot_rows(slot), : 3 * CHANNELS]), slot)

    def gradient(left, at, member, start, stop):
        @pl.loop(start, stop)
        def _(tile):
            columns = pl.ds(pl.multiple_of(tile * TILE, TILE), TILE)
            flat_weights[at, :, columns] = dot(
                left[...], big[member * ROWS : (member + 1) * ROWS, columns]
            ).astype(b16)

    def keep_gain(start, values):
        total = jnp.sum(values, axis=0, keepdims=True)
        for at in range(4):
            small[start + at : start + at + 1, :] = total[:, at * CHANNELS : (at + 1) * CHANNELS]

    def exchange(phase, start, devices, rows=16):
        few = pl.ds(0, rows)
        for at, device in enumerate(devices):
            remote(
                small.at[few],
                small_recv.at[start + at, few],
                small_sems.at[0, phase],
                small_sems.at[1, phase],
                device,
            ).start()

    def added(phase, start, count, rows=16):
        spots = small_recv.at[pl.ds(start, count), pl.ds(0, rows)]
        for side in range(2):
            wait_bytes(spots, small_sems.at[side, phase])
        total = small[0:rows, :]
        for at in range(count):
            total = total + small_recv[start + at, 0:rows, :]
        small[0:rows, :] = total

    io_gather.start()
    down_gather.start()
    io_gather.first()
    io_gather.first_far()
    x_copy.wait()

    @pl.loop(0, ROWS, step=64)
    def _(at):
        input_low[pl.ds(at, 64), :] = normed_low(send_b[pl.ds(at, 64), :])

    io_gather.second(1)
    io_gather.second(3)
    io_gather.second(0)
    io_gather.second(2)
    io_gather.second_far(1)
    send_edges()
    down_gather.first()
    io_gather.second_far(0)
    early_gather.start()
    io_gather.second_far(3)
    io_gather.second_far(2)
    wait_bytes(edges, edge_sems.at[1])
    wait_bytes(edges, edge_sems.at[0])
    for side in range(2):
        rows = pl.ds(ROWS + side * 2 * EDGE, 2 * EDGE)
        input_low[rows, :] = normed_low(edges[side].reshape(2 * EDGE, WIDTH))
    io_gather.finish()
    project(1)
    project(2)
    project(0)
    product[:, 8:, :] = (projected[0, :ROWS] * projected[2, :ROWS]).reshape(
        2, SLOT_ROWS, CHANNELS
    )
    before = (
        projected[0, ROWS : ROWS + 2 * EDGE] * projected[2, ROWS : ROWS + 2 * EDGE]
    ).reshape(2, EDGE, CHANNELS)
    product[:, :8, :] = jnp.where(place.ctx > 0, before[:, EDGE - 8 :, :], 0.0)
    convolved[...] = (
        taps[0:1, :] * product[:, 6 : 6 + SLOT_ROWS, :]
        + taps[1:2, :] * product[:, 7 : 7 + SLOT_ROWS, :]
        + taps[2:3, :] * product[:, 8 : 8 + SLOT_ROWS, :]
    ).reshape(ROWS, CHANNELS)
    gated[...] = (projected[1, :ROWS] * convolved[...]).astype(b16)

    give_mixed(0)
    give_mixed(1)
    down_gather.first_far()
    down_gather.second(1)
    down_gather.second(0)
    early_gather.first()
    give_mixed(2)
    down_gather.second(2)
    mixed.relay(0)
    down_gather.second_far(0)
    early_gather.first_far()
    down_gather.second(3)
    mixed.relay(1)
    mixed.relay(2)
    late_gather.start()
    own_copy.wait()
    stream = x_own[...].astype(f32) + mixed.take()
    residual[...] = stream
    normed, _ = norm_of(stream)
    second_low[own_rows, :] = (normed * gains[1:2, :]).astype(b16)
    second_spread.start()
    early_gather.second(0)
    early_gather.second(1)
    early_gather.second(3)
    early_gather.second(2)
    low_copy.wait()
    positions = place.ctx * SLOT_ROWS + lax.broadcasted_iota(jnp.int32, (SLOT_ROWS, 1), 0)
    for slot in range(2):
        rows = slice(slot * SLOT_ROWS, (slot + 1) * SLOT_ROWS)
        kept = jnp.where(positions < lengths[slot], 1.0, 0.0)
        grad_low[rows, :] = (grad_low[rows, :].astype(f32) * kept).astype(b16)
    down_gather.second_far(3)
    down_gather.second_far(2)
    down_gather.second_far(1)
    late_gather.first()
    second_spread.relay()
    down_gather.finish()
    late_gather.first_far()
    pl.loop(0, 3)(inner_grad)
    pl.loop(5, 7)(inner_grad)
    early_gather.second_far(0)
    late_gather.second(1)
    early_gather.second_far(1)
    early_gather.second_far(3)
    early_gather.second_far(2)
    late_gather.second(3)
    late_gather.second(0)
    pl.loop(3, 5)(inner_grad)
    early_gather.finish()
    late_gather.second(2)
    second_spread.finish()
    gate_up(2)
    late_gather.second_far(1)
    gate_up(1)
    late_gather.second_far(3)
    gate_up(0)
    late_gather.second_far(0)
    late_gather.second_far(2)
    gate_up(3)
    late_gather.finish()
    gate_up(4)
    gate_up(5)
    gate_up(6)
    mixed.drain()
    give_branch(0)
    for part in (io_gather, down_gather, early_gather, late_gather, second_spread):
        part.drain()
    give_second(0)
    give_second(1)
    give_second(2)
    turned(second_low, turn_b)
    gradient(turn_b, 1, 2, 0, 4)
    up_piece.to_sibling(0, 4 * TILE)
    gradient(turn_b, 1, 2, 4, 7)
    up_piece.to_sibling(4 * TILE, 3 * TILE)
    second.relay(0)
    second.relay(1)
    gradient(turn_b, 0, 1, 0, 4)
    gate_piece.to_sibling(0, 4 * TILE)
    second.relay(2)
    turned(grad_low, turn_a)
    give_branch(1)
    up_piece.second_start()
    branch.relay(0)
    normed, inverse = norm_of(residual[...])
    grad_second = second.take()
    small[...] = jnp.zeros_like(small)
    keep_gain(4, grad_second * normed)
    grad_stream = grad_low[own_rows, :].astype(f32) + norm_back(
        grad_second, normed, inverse, gains[1:2, :]
    )
    grad_own[...] = grad_stream
    second_low[own_rows, :] = grad_stream.astype(b16)
    low_spread.start()
    pieces = [
        grad_stream[row : row + 1, at * TILE : (at + 1) * TILE] for row in range(2) for at in range(6)
    ]
    pieces.append(jnp.zeros((EDGE - 12, TILE), f32))
    edge_send[...] = jnp.concatenate(pieces, axis=0).astype(b16)
    for tp in range(4):

        @pl.when(even)
        def _():
            remote(
                edge_send,
                edge_recv.at[lax.div(place.tp, 2)],
                edge_sems.at[2],
                edge_sems.at[3],
                place.along_ctx(-1, tp),
            ).start()

    gradient(turn_b, 0, 1, 4, 7)
    gate_piece.to_sibling(4 * TILE, 3 * TILE)
    gate_piece.second_start()
    low_spread.relay()
    up_piece.second_relay()
    give_branch(2)
    branch.relay(1)
    gradient(turn_a, 2, 0, 0, 4)
    down_piece.to_sibling(0, 4 * TILE)
    gradient(turn_a, 2, 0, 4, 7)
    down_piece.to_sibling(4 * TILE, 3 * TILE)
    gate_piece.second_relay()
    low_spread.finish()
    wait_bytes(edge_recv, edge_sems.at[3])

    @pl.when(even)
    def _():
        wait_bytes(second_low.at[pl.ds(0, 4 * EDGE), pl.ds(0, TILE)], edge_sems.at[2])

    for slot in range(2):
        packed = edge_recv[slot].astype(f32)
        rows = [
            jnp.concatenate([packed[6 * row + at : 6 * row + at + 1, :] for at in range(6)], axis=1)
            for row in range(2)
        ]
        rows.append(jnp.zeros((EDGE - 2, WIDTH), f32))
        second_low[ROWS + slot * EDGE : ROWS + (slot + 1) * EDGE, :] = jnp.concatenate(
            rows, axis=0
        ).astype(b16)

    grad_gated = dot(second_low[...], flat_io[:, 3 * CHANNELS :])
    conv_grad[:, :SLOT_ROWS, :] = (grad_gated[:ROWS] * projected[1, :ROWS]).reshape(
        2, SLOT_ROWS, CHANNELS
    )
    after = (grad_gated[ROWS:] * projected[1, ROWS + 2 * EDGE :]).reshape(2, EDGE, CHANNELS)
    conv_grad[:, SLOT_ROWS:, :] = jnp.where(place.ctx < 15, after[:, :8, :], 0.0)
    grad_proj[:, CHANNELS : 2 * CHANNELS] = (grad_gated[:ROWS] * convolved[...]).astype(b16)
    branch.relay(2)
    grad_product = (
        taps[2:3, :] * conv_grad[:, 0:SLOT_ROWS, :]
        + taps[1:2, :] * conv_grad[:, 1 : 1 + SLOT_ROWS, :]
        + taps[0:1, :] * conv_grad[:, 2 : 2 + SLOT_ROWS, :]
    ).reshape(ROWS, CHANNELS)
    grad_proj[:, 0:CHANNELS] = (grad_product * projected[2, :ROWS]).astype(b16)
    grad_proj[:, 2 * CHANNELS :] = (grad_product * projected[0, :ROWS]).astype(b16)
    second.drain()
    give_first(0)
    give_first(1)
    give_first(2)
    down_piece.second_start()
    turned(second_low, turn_b)
    block_own[...] = (residual[...] + branch.take()).astype(b16)
    block_keep.start()
    for tap in range(3):
        small[8 + tap : 9 + tap, :] = jnp.sum(
            conv_grad[:, :SLOT_ROWS, :] * product[:, 6 + tap : 6 + tap + SLOT_ROWS, :], axis=(0, 1)
        ).reshape(1, CHANNELS)
    first.relay(1)
    turned(input_low, turn_a)
    first.relay(0)
    gate_piece.first_start()
    first.relay(2)
    big[:, : 2 * CHANNELS] = dot(turn_a[...], grad_proj[:, : 2 * CHANNELS]).astype(b16)
    io_piece.to_sibling(0, 2 * CHANNELS)
    block_spread.start()
    down_piece.second_relay()
    big[:, 2 * CHANNELS : 3 * CHANNELS] = dot(turn_a[...], grad_proj[:, 2 * CHANNELS :]).astype(b16)
    big[:, 3 * CHANNELS : 4 * CHANNELS] = dot(turn_b[...], gated[...]).astype(b16)
    io_piece.to_sibling(2 * CHANNELS, 2 * CHANNELS)
    gate_piece.first_relay()
    normed, inverse = norm_of(x_own[...].astype(f32))
    grad_first = first.take()
    keep_gain(0, grad_first * normed)
    input_own[...] = (
        grad_own[...] + norm_back(grad_first, normed, inverse, gains[0:1, :])
    ).astype(b16)
    input_keep.start()
    exchange(0, 0, [place.along_tp(by) for by in (1, 2, 3)], 8)
    input_spread.start()
    io_piece.second_start()
    io_piece.second_relay()
    added(0, 0, 3, 8)
    exchange(1, 3, [place.sibling()])
    down_piece.first_start()
    added(1, 3, 1)
    exchange(2, 4, [place.along_first(by) for by in (1, 2, 3)])
    up_piece.first_start()
    input_spread.relay()
    block_spread.relay()
    io_piece.first_start()
    down_piece.first_relay()
    added(2, 4, 3)
    exchange(3, 7, [place.along_second(by) for by in (1, 2, 3)])
    up_piece.first_relay()
    io_piece.first_relay()
    input_spread.finish()
    added(3, 7, 3)
    up_piece.finish()
    gate_piece.finish()
    down_piece.finish()
    io_piece.finish()
    block_spread.finish()
    block_keep.wait()
    input_keep.wait()
    for part in (low_spread, block_spread, input_spread, first, branch):
        part.drain()
    for part in (down_piece, gate_piece, up_piece, io_piece):
        part.drain()


def step(*given):
    vmem = pl.BlockSpec(memory_space=pltpu.VMEM)
    smem = pl.BlockSpec(memory_space=pltpu.SMEM)
    hbm = pl.BlockSpec(memory_space=pl.ANY)
    f32, b16 = jnp.float32, jnp.bfloat16
    dma = pltpu.SemaphoreType.DMA
    own16 = pltpu.VMEM((QUARTER, WIDTH), b16)
    own32 = pltpu.VMEM((QUARTER, WIDTH), f32)
    full = pltpu.VMEM((ROWS, WIDTH), b16)
    across = pltpu.VMEM((WIDTH, ROWS), b16)
    return pl.pallas_call(
        kernel,
        out_shape=(
            jax.ShapeDtypeStruct((ROWS, WIDTH), b16),
            jax.ShapeDtypeStruct((ROWS, WIDTH), b16),
            jax.ShapeDtypeStruct((3, 16, BLOCK, PADDED), b16),
            jax.ShapeDtypeStruct((3, 12, BLOCK, PADDED), b16),
            jax.ShapeDtypeStruct((4, BLOCK, CHANNELS), f32),
            jax.ShapeDtypeStruct((3, BLOCK, HIDDEN), f32),
            jax.ShapeDtypeStruct((16, CHANNELS), f32),
        ),
        in_specs=[hbm, hbm, smem] + [hbm] * 4 + [vmem] * 2,
        out_specs=(hbm,) * 6 + (vmem,),
        scratch_shapes=[
            pltpu.VMEM((4, BLOCK, CHANNELS), f32),
            pltpu.VMEM((3, BLOCK, HIDDEN), f32),
            pltpu.VMEM((BLOCK, WIDE), b16),
            pltpu.VMEM((3, BLOCK, PADDED), b16),
            pltpu.VMEM((32, BLOCK, WIDE), b16),
            pltpu.VMEM((3, 32, BLOCK, PADDED), b16),
            pltpu.VMEM((WIDTH, PADDED), b16),
            pltpu.VMEM((ROWS, 3 * CHANNELS), b16),
            full,
            own16,
            pltpu.VMEM((2, 2, EDGE, WIDTH), b16),
            pltpu.VMEM((EDGE, TILE), b16),
            pltpu.VMEM((2, EDGE, TILE), b16),
            pltpu.VMEM((ROWS + 4 * EDGE, WIDTH), b16),
            across,
            across,
            full,
            full,
            pltpu.VMEM((2, 2, HALF, WIDTH), b16),
            pltpu.VMEM((2, 2, QUARTER, WIDTH), b16),
            pltpu.VMEM((ROWS + 2 * EDGE, WIDTH), b16),
            own32,
            pltpu.VMEM((3, ROWS + 4 * EDGE, CHANNELS), f32),
            pltpu.VMEM((2, 8 + SLOT_ROWS, CHANNELS), f32),
            pltpu.VMEM((ROWS, CHANNELS), f32),
            pltpu.VMEM((ROWS, CHANNELS), b16),
            own32,
            own16,
            own16,
            pltpu.VMEM((2, SLOT_ROWS + 8, CHANNELS), f32),
            pltpu.VMEM((16, BLOCK, PADDED), b16),
            pltpu.VMEM((3, 3, BLOCK, PADDED), b16),
            pltpu.VMEM((16, BLOCK, WIDE), b16),
            pltpu.VMEM((12, BLOCK, WIDE), b16),
            pltpu.VMEM((10, 16, CHANNELS), f32),
            dma((Gather.SEMS,)),
            dma((Gather.SEMS,)),
            dma((Gather.SEMS,)),
            dma((Gather.SEMS,)),
            dma((4, Scatter.SEMS)),
            dma((4, TpSum.SEMS)),
            dma((4, TpSpread.SEMS)),
            dma((4,)),
            dma((2, 4)),
            dma((10,)),
        ],
        compiler_params=pltpu.CompilerParams(
            collective_id=0, has_side_effects=True, vmem_limit_bytes=63 * 2**20
        ),
        name="step",
    )(*given)


def nesterov(weight, moment, average, gradient, step_rate):
    moment_new = momentum * moment + gradient
    weight_new = weight - step_rate * (gradient + momentum * moment_new)
    average_new = average_decay * average + (1.0 - average_decay) * weight_new
    return (moment_new, weight_new, average_new)


def update_kernel(*refs):
    block_in, input_in = refs[:2]
    old = [refs[2 + 3 * at : 5 + 3 * at] for at in range(6)]
    io_grad, gud_grad, small_grad = refs[20:23]
    block_out, input_out = refs[23:25]
    new = [refs[25 + 3 * at : 28 + 3 * at] for at in range(6)]
    block_held, input_held, wide_held, io_held, gud_held, small_held = refs[43:49]
    held = [refs[49 + 3 * at : 52 + 3 * at] for at in range(6)]
    in_sems, out_sems = refs[67:]

    def moved(source, target, sems, at):
        copy = pltpu.make_async_copy(source, target, sems.at[at])
        copy.start()
        return copy

    order = (2, 3, 0, 1, 4, 5)
    input_load = moved(input_in, input_held, in_sems, 18)
    gud_load = moved(gud_grad, gud_held, in_sems, 19)
    loads = {}
    for matrix in order:
        loads[matrix] = [
            moved(old[matrix][at], held[matrix][at], in_sems, 3 * matrix + at) for at in range(3)
        ]
        if matrix == 2:
            io_load = moved(io_grad, io_held, in_sems, 20)
            small_load = moved(small_grad, small_held, in_sems, 21)
    block_load = moved(block_in, block_held, in_sems, 22)
    stores = []
    input_load.wait()
    for half in range(2):
        rows = pl.ds(half * SLOT_ROWS, SLOT_ROWS)
        wide_held[rows, :] = input_held[rows, :].astype(jnp.float32)
        stores.append(moved(wide_held.at[rows], input_out.at[rows], out_sems, 18 + half))
    for matrix in order:
        for copy in loads[matrix]:
            copy.wait()
        weight, moment, average = held[matrix]
        every, rate = slice(None), matrix_rate
        if matrix == 0:
            io_load.wait()
            parts = [(at, io_held[at]) for at in range(3)]
        elif matrix == 1:
            parts = [(every, io_held[3])]
        elif matrix == 2:
            gud_load.wait()
            parts = [(at, gud_held[at]) for at in range(2)]
        elif matrix == 3:
            parts = [(every, gud_held[2])]
        elif matrix == 4:
            small_load.wait()
            rate = small_rate
            parts = [
                (
                    (slice(row, row + 1), slice(at * CHANNELS, (at + 1) * CHANNELS)),
                    small_held[4 * row + at : 4 * row + at + 1, :],
                )
                for row in range(2)
                for at in range(4)
            ]
        else:
            parts, rate = [(every, small_held[8:11, :])], small_rate
        for at, gradient in parts:
            moment[at], weight[at], average[at] = nesterov(
                weight[at], moment[at], average[at], gradient, rate
            )
        for at, source in enumerate((moment, weight, average)):
            stores.append(moved(source, new[matrix][at], out_sems, 3 * matrix + at))
    block_load.wait()
    stores.append(moved(block_held, block_out, out_sems, 20))
    for copy in stores:
        copy.wait()


def update(block, input_low, arrays, io_grad, gud_grad, small):
    hbm = pl.BlockSpec(memory_space=pl.ANY)
    f32 = jnp.float32
    like = lambda a: jax.ShapeDtypeStruct(a.shape, a.dtype)
    held = lambda a: pltpu.VMEM(a.shape, a.dtype)
    return pl.pallas_call(
        update_kernel,
        out_shape=(
            like(block),
            jax.ShapeDtypeStruct((ROWS, WIDTH), f32),
            *[like(a) for a in arrays],
        ),
        in_specs=[hbm] * 23,
        out_specs=(hbm,) * 20,
        scratch_shapes=[
            held(block),
            held(input_low),
            pltpu.VMEM((ROWS, WIDTH), f32),
            held(io_grad),
            held(gud_grad),
            held(small),
            *[held(a) for a in arrays],
            pltpu.SemaphoreType.DMA((23,)),
            pltpu.SemaphoreType.DMA((21,)),
        ],
        compiler_params=pltpu.CompilerParams(vmem_limit_bytes=62 * 2**20),
        name="update",
    )(block, input_low, *arrays, io_grad, gud_grad, small)


def on_device(
    hidden,
    lengths,
    cotangent,
    in_weight,
    in_moment,
    in_average,
    out_weight,
    out_moment,
    out_average,
    gate_up_weight,
    gate_up_moment,
    gate_up_average,
    down_weight,
    down_moment,
    down_average,
    norm_gains,
    gain_moment,
    gain_average,
    conv_taps,
    taps_moment,
    taps_average,
):
    slot_count, seq_len, model_width = hidden.shape
    row_count = slot_count * seq_len
    block_output, input_low_grad, _, _, io_sum, gud_sum, small = step(
        hidden.reshape(row_count, model_width),
        cotangent.reshape(row_count, model_width),
        lengths,
        in_weight,
        out_weight.T,
        gate_up_weight,
        down_weight.T,
        norm_gains,
        conv_taps,
    )
    matrices = (
        (in_weight, in_moment, in_average),
        (out_weight.T, out_moment.T, out_average.T),
        (gate_up_weight, gate_up_moment, gate_up_average),
        (down_weight.T, down_moment.T, down_average.T),
    )
    smalls = (norm_gains, gain_moment, gain_average, conv_taps, taps_moment, taps_average)
    block_output, input_grad, *new = update(
        block_output,
        input_low_grad,
        [a for group in matrices for a in group] + list(smalls),
        io_sum,
        gud_sum,
        small,
    )
    return (
        block_output.reshape(slot_count, seq_len, model_width),
        input_grad.reshape(slot_count, seq_len, model_width),
        *new[0:3],
        *[a.T for a in new[3:6]],
        *new[6:9],
        *[a.T for a in new[9:12]],
        *new[12:18],
    )


def solution(mesh):
    placed = (
        P("shard", "ctx", None),
        P("shard"),
        P("shard", "ctx", None),
        P(None, ("shard", "ctx"), "tp"),
        P(None, ("shard", "ctx"), "tp"),
        P(None, ("shard", "ctx"), "tp"),
        P("tp", ("shard", "ctx")),
        P("tp", ("shard", "ctx")),
        P("tp", ("shard", "ctx")),
        P(None, ("shard", "ctx"), "tp"),
        P(None, ("shard", "ctx"), "tp"),
        P(None, ("shard", "ctx"), "tp"),
        P("tp", ("shard", "ctx")),
        P("tp", ("shard", "ctx")),
        P("tp", ("shard", "ctx")),
        P(),
        P(),
        P(),
        P(None, "tp"),
        P(None, "tp"),
        P(None, "tp"),
    )
    return jax.shard_map(
        on_device,
        mesh=mesh,
        in_specs=placed,
        out_specs=(
            P("shard", "ctx", None),
            P("shard", "ctx", None),
            P(None, ("shard", "ctx"), "tp"),
            P(None, ("shard", "ctx"), "tp"),
            P(None, ("shard", "ctx"), "tp"),
            P("tp", ("shard", "ctx")),
            P("tp", ("shard", "ctx")),
            P("tp", ("shard", "ctx")),
            P(None, ("shard", "ctx"), "tp"),
            P(None, ("shard", "ctx"), "tp"),
            P(None, ("shard", "ctx"), "tp"),
            P("tp", ("shard", "ctx")),
            P("tp", ("shard", "ctx")),
            P("tp", ("shard", "ctx")),
            P(),
            P(),
            P(),
            P(None, "tp"),
            P(None, "tp"),
            P(None, "tp"),
        ),
        check_vma=False,
    )
```

```python
import functools

import jax
import jax.numpy as jnp
from jax import lax
from jax.experimental import pallas as pl
from jax.experimental.pallas import tpu as pltpu
from jax.sharding import PartitionSpec as P

MESH = pl.DeviceIdType.MESH
epsilon = 1e-05
momentum = 0.9
average_decay = 0.9
matrix_rate = 0.0004
small_rate = 0.005
WIDTH = 1536
CHANNELS = 384
HIDDEN = 1728
TILE = 256
EDGE = 16
EARLY = 4
SLOTS = ((0, 512), (512, 512), (1024, 512))
WIDE = 4 * CHANNELS
PADDED = 1792
ROWS = 512
QUARTER = 128
SLOT_ROWS = 256
BLOCK = 48
HALF = QUARTER // 2


class Place:
    def __init__(self, flip=False):
        self.shard = lax.axis_index("shard")
        self.ctx = lax.axis_index("ctx")
        self.tp = lax.axis_index("tp")
        self.y = self.shard * 2 + lax.div(self.ctx, 8)
        self.z = lax.rem(lax.div(self.ctx, 2), 4)
        self.core = lax.rem(self.ctx, 2)
        self.way = 1 - self.core if flip else self.core
        self.first = self.y * (1 - self.way) + self.z * self.way
        self.second = self.z * (1 - self.way) + self.y * self.way

    def turn(self, value, by):
        return lax.rem(value + by + 4, 4)

    def device(self, y, z, core):
        return (lax.div(y, 2), lax.rem(y, 2) * 8 + z * 2 + core, self.tp)

    def grid_device(self, first, second):
        y = first * (1 - self.way) + second * self.way
        z = second * (1 - self.way) + first * self.way
        return self.device(y, z, self.core)

    def block(self, first, second):
        y = first * (1 - self.way) + second * self.way
        z = second * (1 - self.way) + first * self.way
        return y * 8 + z * 2 + self.core

    def along_first(self, by):
        return self.grid_device(self.turn(self.first, by), self.second)

    def along_second(self, by):
        return self.grid_device(self.first, self.turn(self.second, by))

    def along_tp(self, by):
        return (self.shard, self.ctx, self.turn(self.tp, by))

    def along_ctx(self, by, tp=None):
        return (self.shard, lax.rem(self.ctx + by + 16, 16), self.tp if tp is None else tp)

    def sibling(self):
        return self.device(self.y, self.z, 1 - self.core)

    def greet(self):
        barrier = pltpu.get_barrier_semaphore()
        friends = [self.sibling()]
        for tp in range(4):
            friends += [self.along_ctx(1, tp), self.along_ctx(-1, tp)]
        for by in (1, 2, 3):
            friends += [self.along_first(by), self.along_second(by), self.along_tp(by)]
        for friend in friends:
            pl.semaphore_signal(barrier, inc=1, device_id=friend, device_id_type=MESH)
        return len(friends)


def remote(source, target, send_sem, recv_sem, device):
    return pltpu.make_async_remote_copy(
        src_ref=source,
        dst_ref=target,
        send_sem=send_sem,
        recv_sem=recv_sem,
        device_id=device,
        device_id_type=MESH,
    )


def wait_bytes(spot, sem):
    pltpu.make_async_copy(spot, spot, sem).wait()


class Gather:
    SEMS = 12

    def __init__(self, place, local, whole, sems):
        self.place, self.local, self.whole, self.sems = place, local, whole, sems
        self.half = local.shape[-1] // 2

    def part(self, block, half=None):
        spot = self.whole.at[:, block] if self.whole.ndim == 4 else self.whole.at[block]
        if half is None:
            return spot
        columns = pl.ds(half * self.half, self.half)
        return spot.at[:, :, columns] if self.whole.ndim == 4 else spot.at[:, columns]

    def send(self, source, target, at, device):
        remote(source, target, self.sems.at[0], self.sems.at[at], device).start()

    def arrived(self, blocks, at):
        few = pl.ds(0, blocks)
        wait_bytes(self.whole.at[:, few] if self.whole.ndim == 4 else self.whole.at[few], self.sems.at[at])

    def block(self, back, by):
        p = self.place
        return p.block(p.turn(p.first, -back), p.turn(p.second, -by))

    def to_second(self, source, back, by):
        spot = self.part(self.block(back, 0))
        self.send(source, spot, 3 + back, self.place.along_second(1))
        self.send(source, spot, 3 + back, self.place.along_second(-1))
        self.to_sibling(source, back, by)

    def to_sibling(self, source, back, by):
        self.send(source, self.part(self.block(back, by)), 11, self.place.sibling())

    def start(self):
        p = self.place
        spot = self.part(self.block(0, 0))
        self.send(self.local, spot, 1, p.along_first(1))
        self.send(self.local, spot, 1, p.along_first(-1))
        self.to_second(self.local, 0, 0)

    def first(self):
        p = self.place
        self.arrived(2, 1)
        for back, half, by in ((1, 0, 1), (3, 1, -1)):
            piece = self.part(self.block(back, 0), half)
            self.send(piece, piece, 2, p.along_first(by))
        for back in (1, 3):
            self.to_second(self.part(self.block(back, 0)), back, 0)

    def first_far(self):
        self.arrived(1, 2)
        self.to_second(self.part(self.block(2, 0)), 2, 0)

    def second(self, back):
        p = self.place
        self.arrived(2, 3 + back)
        for by, half, step in ((1, 0, 1), (3, 1, -1)):
            piece = self.part(self.block(back, by), half)
            self.send(piece, piece, 7 + back, p.along_second(step))
        for by in (1, 3):
            self.to_sibling(self.part(self.block(back, by)), back, by)

    def second_far(self, back):
        self.arrived(1, 7 + back)
        self.to_sibling(self.part(self.block(back, 2)), back, 2)

    def finish(self):
        self.arrived(16, 11)

    def drain(self):
        self.arrived(31, 0)


class Both:
    def __init__(self, *parts):
        self.parts = parts

    def each(self, name, *given):
        for part in self.parts:
            getattr(part, name)(*given)

    def start(self):
        self.each("start")

    def first(self):
        self.each("first")

    def first_far(self):
        self.each("first_far")

    def second(self, back):
        self.each("second", back)

    def second_far(self, back):
        self.each("second_far", back)

    def finish(self):
        self.each("finish")

    def drain(self):
        self.each("drain")


class Scatter:
    SEMS = 6

    def __init__(self, place, partial, width, recv, out, stage, sems, local_sems):
        self.place, self.width, self.out = place, width, out
        self.sib_recv, self.second_recv, self.first_recv = recv
        self.stage, self.sems, self.local_sems = stage, sems, local_sems
        columns = pl.ds(0, width)
        self.blocks = partial.reshape(16, 2, BLOCK, PADDED).at[:, :, :, columns]
        self.grid = partial.reshape(4, 4, 2, BLOCK, PADDED).at[:, :, :, :, columns]
        self.rows = partial.reshape(32, BLOCK, PADDED).at[:, :, columns]

    def mine(self, first, second):
        return lax.div(self.place.block(first, second), 2)

    def arrived(self, spot, at):
        wait_bytes(spot, self.sems.at[at])

    def move(self, source, target, at, device):
        remote(source, target, self.sems.at[0], self.sems.at[at], device).start()

    def to_sibling(self, start=0, width=None):
        p = self.place
        columns = pl.ds(start, self.width if width is None else width)
        source = self.blocks.at[:, 1 - p.core, :, columns]
        self.move(source, self.sib_recv.at[:, :, columns], 1, p.sibling())

    def fetch(self, source, count):
        if self.stage is None:
            return source
        target = self.stage.at[pl.ds(0, count), :, pl.ds(0, self.width)]
        copy = pltpu.make_async_copy(source, target, self.local_sems.at[0])
        copy.start()
        copy.wait()
        return target

    def add_to(self, at, held, parts):
        core = self.place.core
        if len(parts) == 1:
            self.blocks[at, core] = self.blocks[at, core] + held[parts[0]]
        else:
            total = self.blocks[at, core].astype(jnp.float32)
            for part in parts:
                total = total + held[part].astype(jnp.float32)
            self.blocks[at, core] = total.astype(jnp.bfloat16)

    def pair(self, half, by, target, at, step):
        p = self.place
        there = p.turn(p.second, by)
        two = pl.ds(2 * half, 2)

        @pl.when(p.core == 0)
        def _():
            self.move(self.grid.at[two, there, 0], target, at, p.along_second(step))

        @pl.when(p.core == 1)
        def _():
            self.move(self.grid.at[there, two, 1], target, at, p.along_second(step))

    def second_start(self):
        p = self.place
        self.arrived(self.sib_recv, 1)
        held = self.fetch(self.sib_recv, 16)

        @pl.loop(0, 4)
        def _(first):
            at = self.mine(first, p.turn(p.second, 2))
            self.add_to(at, held, [at])

        for half, step in ((0, 1), (1, -1)):
            self.pair(half, 2, self.second_recv.at[pl.ds(8 + 2 * half, 2)], 2, step)

        @pl.loop(0, 12)
        def _(other):
            away = lax.rem(lax.div(other, 4) + 3, 4)
            at = self.mine(lax.rem(other, 4), p.turn(p.second, away))
            self.add_to(at, held, [at])

        for half, step in ((0, 1), (1, -1)):
            spot = self.second_recv.at[pl.ds(4 * half + 2 * (1 - half), 2)]
            self.pair(1 - half, step, spot, 3, step)

    def second_relay(self):
        p = self.place
        self.arrived(self.second_recv.at[pl.ds(8, 4)], 2)
        held = self.fetch(self.second_recv.at[pl.ds(8, 4)], 4)
        for half, step in ((0, 1), (1, -1)):

            @pl.loop(0, 2)
            def _(first):
                at = self.mine(2 * half + first, p.turn(p.second, step))
                self.add_to(at, held, [2 * half + first])

            spot = self.second_recv.at[pl.ds(4 * half + 2 * half, 2)]
            self.pair(half, step, spot, 3, step)

    def first_start(self):
        p = self.place
        self.arrived(self.second_recv.at[pl.ds(0, 8)], 3)
        held = self.fetch(self.second_recv.at[pl.ds(0, 8)], 8)

        @pl.loop(0, 4)
        def _(first):
            self.add_to(self.mine(first, p.second), held, [first, 4 + first])

        for half, step in ((0, 1), (1, -1)):
            self.strip(half, 2, self.first_recv.at[2], 4, step)
        for half, step in ((0, 1), (1, -1)):
            self.strip(1 - half, step, self.first_recv.at[half], 5, step)

    def columns(self, half):
        return pl.ds(half * (self.width // 2), self.width // 2)

    def strip(self, half, by, target, at, step):
        p = self.place
        source = self.blocks.at[self.mine(p.turn(p.first, by), p.second), p.core]
        columns = self.columns(half)
        self.move(source.at[:, columns], target.at[:, columns], at, p.along_first(step))

    def first_relay(self):
        p = self.place
        self.arrived(self.first_recv.at[2], 4)
        for half, step in ((0, 1), (1, -1)):
            columns = self.columns(half)
            at = self.mine(p.turn(p.first, step), p.second)
            both = self.blocks[at, p.core, :, columns].astype(jnp.float32)
            both = both + self.first_recv[2, :, columns].astype(jnp.float32)
            self.blocks[at, p.core, :, columns] = both.astype(jnp.bfloat16)
            self.strip(half, step, self.first_recv.at[half], 5, step)

    def finish(self):
        p = self.place
        self.arrived(self.first_recv.at[pl.ds(0, 2)], 5)
        total = self.blocks[self.mine(p.first, p.second), p.core].astype(jnp.float32)
        for by in range(2):
            total = total + self.first_recv[by].astype(jnp.float32)
        wide, out, members, columns, sem = self.out
        for member in range(members):
            wide[member] = total[:, member * columns : (member + 1) * columns]
        copy = pltpu.make_async_copy(wide, out, sem)
        copy.start()
        self.store = copy

    def drain(self):
        self.arrived(self.rows.at[pl.ds(0, 31)], 0)
        self.store.wait()


class TpSum:
    SEMS = 5

    def __init__(self, place, send, relay, final, sems):
        self.place, self.send, self.relay_in, self.final = place, send, relay, final
        self.sems = sems

    def rows(self, by, half):
        p = self.place
        start = p.turn(p.tp, by) * QUARTER + half * HALF
        return pl.ds(pl.multiple_of(start, HALF), HALF)

    def move(self, source, target, at, by):
        remote(source, target, self.sems.at[0], self.sems.at[at], self.place.along_tp(by)).start()

    def give(self, values, slot):
        columns = pl.ds(*SLOTS[slot])
        self.send[:, columns] = values.astype(jnp.bfloat16)
        for half, by in ((0, 1), (1, -1)):
            source = self.send.at[self.rows(2, half), columns]
            self.move(source, self.relay_in.at[half, :, columns], 2 + slot, by)
        for half, by in ((0, 1), (1, -1)):
            source = self.send.at[self.rows(by, 1 - half), columns]
            target = self.final.at[half, pl.ds((1 - half) * HALF, HALF), columns]
            self.move(source, target, 1, by)

    def relay(self, slot):
        columns = pl.ds(*SLOTS[slot])
        wait_bytes(self.relay_in.at[:, :, columns], self.sems.at[2 + slot])
        for half, by in ((0, 1), (1, -1)):
            rows = self.rows(by, half)
            both = self.send[rows, columns].astype(jnp.float32)
            both = both + self.relay_in[half, :, columns].astype(jnp.float32)
            self.send[rows, columns] = both.astype(jnp.bfloat16)
            target = self.final.at[half, pl.ds(half * HALF, HALF), columns]
            self.move(self.send.at[rows, columns], target, 1, by)

    def take(self):
        p = self.place
        wait_bytes(self.final, self.sems.at[1])
        rows = pl.ds(pl.multiple_of(p.tp * QUARTER, QUARTER), QUARTER)
        total = self.send[rows, :].astype(jnp.float32)
        for half in range(2):
            total = total + self.final[half].astype(jnp.float32)
        return total

    def drain(self):
        wait_bytes(self.send.at[pl.ds(0, 3 * QUARTER)], self.sems.at[0])


class TpSpread:
    SEMS = 3

    def __init__(self, place, source, whole, sems):
        self.place, self.source, self.whole, self.sems = place, source, whole, sems

    def spot(self, by, half):
        p = self.place
        start = p.turn(p.tp, by) * QUARTER + half * HALF
        return self.whole.at[pl.ds(pl.multiple_of(start, HALF), HALF)]

    def move(self, source, target, at, by):
        remote(source, target, self.sems.at[0], self.sems.at[at], self.place.along_tp(by)).start()

    def start(self):
        for at, half, by in ((1, 0, 1), (1, 1, -1), (2, 1, 1), (2, 0, -1)):
            self.move(self.source.at[pl.ds(half * HALF, HALF)], self.spot(0, half), at, by)

    def arrived(self, rows, at):
        wait_bytes(self.whole.at[pl.ds(0, rows)], self.sems.at[at])

    def relay(self):
        self.arrived(QUARTER, 1)
        for half, by in ((0, 1), (1, -1)):
            spot = self.spot(-by, half)
            self.move(spot, spot, 2, by)

    def finish(self):
        self.arrived(2 * QUARTER, 2)

    def drain(self):
        self.arrived(3 * QUARTER, 0)


def dot(left, right):
    return jnp.dot(left, right, preferred_element_type=jnp.float32)


def dot_t(left, right):
    return lax.dot_general(
        left, right, (((1,), (1,)), ((), ())), preferred_element_type=jnp.float32
    )


def turned(source, target):
    @pl.loop(0, WIDTH // TILE)
    def _(at):
        at = pl.multiple_of(at * TILE, TILE)
        target[pl.ds(at, TILE), :] = source[pl.ds(0, ROWS), pl.ds(at, TILE)].T


def slot_rows(slot):
    start, width = SLOTS[slot]
    return slice(start, start + width)


def own_rows_of(place):
    return pl.ds(pl.multiple_of(place.tp * QUARTER, QUARTER), QUARTER)


def norm_of(values):
    inverse = lax.rsqrt(jnp.mean(values * values, axis=-1, keepdims=True) + epsilon)
    return values * inverse, inverse


def norm_back(grad, normed, inverse, gain):
    scaled = grad * gain
    return inverse * (scaled - normed * jnp.mean(scaled * normed, axis=-1, keepdims=True))


def kernel(
    x,
    cotangent,
    lengths,
    in_weight,
    out_weight,
    gate_up_weight,
    down_weight,
    gains,
    taps,
    block_out,
    input_out,
    sib_hbm,
    second_hbm,
    io_grad,
    gud_grad,
    small,
    io_wide,
    gud_wide,
    io_local,
    gud_local,
    io,
    weights,
    big,
    grad_proj,
    grad_low,
    x_own,
    edges,
    edge_send,
    edge_recv,
    input_low,
    turn_a,
    turn_b,
    send_a,
    send_b,
    relays,
    finals,
    second_low,
    residual,
    projected,
    product,
    convolved,
    gated,
    grad_own,
    block_own,
    input_own,
    conv_grad,
    stage,
    first_recv,
    io_sib_recv,
    io_second_recv,
    small_recv,
    io_sems,
    down_sems,
    early_sems,
    late_sems,
    scatter_sems,
    sum_sems,
    spread_sems,
    edge_sems,
    small_sems,
    local_sems,
):
    f32, b16 = jnp.float32, jnp.bfloat16
    place = Place()
    own_rows = own_rows_of(place)
    tiles = PADDED // TILE
    mine = place.block(place.first, place.second)
    flat_io = io.reshape(WIDTH, WIDE)
    flat_weights = weights.reshape(3, WIDTH, PADDED)

    loads = [
        pltpu.make_async_copy(source, target, local_sems.at[6 + at])
        for at, (source, target) in enumerate(
            (
                (in_weight, io_wide.at[pl.ds(0, 3)]),
                (out_weight, io_wide.at[3]),
                (gate_up_weight, gud_wide.at[pl.ds(0, 2)]),
                (down_weight, gud_wide.at[2]),
            )
        )
    ]
    x_copy = pltpu.make_async_copy(x, send_b, local_sems.at[1])
    low_copy = pltpu.make_async_copy(cotangent, grad_low, local_sems.at[2])
    own_copy = pltpu.make_async_copy(x.at[own_rows], x_own, local_sems.at[3])
    for copy in (*loads, x_copy, low_copy, own_copy):
        copy.start()
    friends = place.greet()
    for copy in loads[:2]:
        copy.wait()
    for member in range(4):
        io_local[:, member * CHANNELS : (member + 1) * CHANNELS] = io_wide[member].astype(b16)
    io[mine] = io_local[...]
    pl.semaphore_wait(pltpu.get_barrier_semaphore(), friends)
    other_place = Place(flip=True)
    two = pl.ds(0, 2)
    io_gather = Gather(place, io_local, io, io_sems)
    down_gather = Gather(place, gud_local.at[2], weights.at[2], down_sems)

    def columns_gather(way, start, width, sems):
        columns = pl.ds(start, width)
        return Gather(
            way, gud_local.at[two, :, columns], weights.at[two, :, :, columns], sems
        )

    early_gather = Both(
        columns_gather(place, 0, 512, early_sems.at[0]),
        columns_gather(other_place, 512, 512, early_sems.at[1]),
    )
    late_gather = Both(
        columns_gather(place, 1024, 256, late_sems.at[0]),
        columns_gather(other_place, 1280, 512, late_sems.at[1]),
    )
    mixed = TpSum(place, send_a, relays.at[0], finals.at[0], sum_sems.at[0])
    second = TpSum(place, send_b, relays.at[1], finals.at[1], sum_sems.at[1])
    branch = TpSum(place, send_a, relays.at[0], finals.at[0], sum_sems.at[2])
    first = TpSum(place, send_b, relays.at[1], finals.at[1], sum_sems.at[3])
    second_spread = TpSpread(place, second_low.at[own_rows], second_low, spread_sems.at[0])
    low_spread = TpSpread(place, second_low.at[own_rows], second_low, spread_sems.at[1])
    block_spread = TpSpread(place, block_own, block_out, spread_sems.at[2])
    input_spread = TpSpread(place, input_own, input_out, spread_sems.at[3])
    block_keep = pltpu.make_async_copy(block_own, block_out.at[own_rows], local_sems.at[4])
    input_keep = pltpu.make_async_copy(input_own, input_out.at[own_rows], local_sems.at[5])
    even = lax.rem(place.tp, 2) == 0

    def piece(at):
        return Scatter(
            place,
            flat_weights.at[at],
            PADDED,
            (sib_hbm.at[at], second_hbm.at[at], first_recv.at[at]),
            (
                gud_wide.at[pl.ds(at, 1)],
                gud_grad.at[pl.ds(at, 1)],
                1,
                HIDDEN,
                local_sems.at[6 + at],
            ),
            stage,
            scatter_sems.at[at],
            local_sems,
        )

    gate_piece, up_piece, down_piece = piece(0), piece(1), piece(2)
    io_piece = Scatter(
        place,
        big,
        WIDE,
        (io_sib_recv, io_second_recv, gud_local.at[:, :, pl.ds(0, WIDE)]),
        (io_wide, io_grad, 4, CHANNELS, local_sems.at[9]),
        None,
        scatter_sems.at[3],
        local_sems,
    )

    def normed_low(values):
        normed, _ = norm_of(values.astype(f32))
        return (normed * gains[0:1, :]).astype(b16)

    def send_edges():
        slots_x = x.reshape(2, SLOT_ROWS, WIDTH)
        for side, start, by in ((0, SLOT_ROWS - EDGE, 1), (1, 0, -1)):
            remote(
                slots_x.at[:, pl.ds(start, EDGE)],
                edges.at[side],
                edge_sems.at[0],
                edge_sems.at[1],
                place.along_ctx(by),
            ).start()

    def project(member):
        if member == 0:
            columns = slice(0, 3 * CHANNELS)
            whole = dot(input_low[...], flat_io[:, columns])
            for at in range(3):
                projected[at] = whole[:, at * CHANNELS : (at + 1) * CHANNELS]

    def give_mixed(slot):
        mixed.give(dot_t(gated[...], flat_io[slot_rows(slot), 3 * CHANNELS :]), slot)

    def inner_grad(at):
        columns = pl.ds(pl.multiple_of(at * TILE, TILE), TILE)
        big[0:ROWS, columns] = dot(grad_low[...], flat_weights[2, :, columns]).astype(b16)

    def gate_up(at):
        columns = pl.ds(at * TILE, TILE)
        parts = [slice(0, SLOT_ROWS), slice(SLOT_ROWS, ROWS)]
        gates = [dot(second_low[rows, :], flat_weights[0, :, columns]) for rows in parts]
        ups = [dot(second_low[rows, :], flat_weights[1, :, columns]) for rows in parts]
        for half, rows in enumerate(parts):
            gate, up = gates[half], ups[half]
            grad_inner = big[rows, columns].astype(f32)
            sigmoid = 0.5 * jnp.tanh(0.5 * gate) + 0.5
            active = gate * sigmoid
            big[rows, columns] = (active * up).astype(b16)
            start = ROWS + rows.start
            big[start : start + SLOT_ROWS, columns] = (
                grad_inner * up * (sigmoid + active * (1.0 - sigmoid))
            ).astype(b16)
            big[start + ROWS : start + ROWS + SLOT_ROWS, columns] = (grad_inner * active).astype(b16)

    def give_second(slot):
        rows = slot_rows(slot)
        part = dot_t(big[ROWS : 2 * ROWS, :], flat_weights[0, rows, :])
        part = part + dot_t(big[2 * ROWS :, :], flat_weights[1, rows, :])
        second.give(part, slot)

    def give_branch(slot):
        branch.give(dot_t(big[0:ROWS, :], flat_weights[2, slot_rows(slot), :]), slot)

    def give_first(slot):
        first.give(dot_t(grad_proj[...], flat_io[slot_rows(slot), : 3 * CHANNELS]), slot)

    def gradient(left, at, member, start, stop):
        @pl.loop(start, stop)
        def _(tile):
            columns = pl.ds(pl.multiple_of(tile * TILE, TILE), TILE)
            flat_weights[at, :, columns] = dot(
                left[...], big[member * ROWS : (member + 1) * ROWS, columns]
            ).astype(b16)

    def keep_gain(start, values):
        total = jnp.sum(values, axis=0, keepdims=True)
        for at in range(4):
            small[start + at : start + at + 1, :] = total[:, at * CHANNELS : (at + 1) * CHANNELS]

    def exchange(phase, start, devices, rows=16):
        few = pl.ds(0, rows)
        for at, device in enumerate(devices):
            remote(
                small.at[few],
                small_recv.at[start + at, few],
                small_sems.at[0, phase],
                small_sems.at[1, phase],
                device,
            ).start()

    def added(phase, start, count, rows=16):
        spots = small_recv.at[pl.ds(start, count), pl.ds(0, rows)]
        for side in range(2):
            wait_bytes(spots, small_sems.at[side, phase])
        total = small[0:rows, :]
        for at in range(count):
            total = total + small_recv[start + at, 0:rows, :]
        small[0:rows, :] = total

    io_gather.start()
    x_copy.wait()

    @pl.loop(0, ROWS, step=64)
    def _(at):
        input_low[pl.ds(at, 64), :] = normed_low(send_b[pl.ds(at, 64), :])

    for copy in loads[2:]:
        copy.wait()
    for member in range(3):
        gud_local[member, :, :HIDDEN] = gud_wide[member].astype(b16)
    gud_local[:, :, HIDDEN:] = jnp.zeros((3, BLOCK, PADDED - HIDDEN), b16)
    weights[:, mine] = gud_local[...]
    down_gather.start()
    io_gather.first()
    send_edges()
    io_gather.first_far()
    io_gather.second(0)
    io_gather.second(1)
    low_copy.wait()
    positions = place.ctx * SLOT_ROWS + lax.broadcasted_iota(jnp.int32, (SLOT_ROWS, 1), 0)
    for slot in range(2):
        rows = slice(slot * SLOT_ROWS, (slot + 1) * SLOT_ROWS)
        kept = jnp.where(positions < lengths[slot], 1.0, 0.0)
        grad_low[rows, :] = (grad_low[rows, :].astype(f32) * kept).astype(b16)
    io_gather.second(3)
    wait_bytes(edges, edge_sems.at[1])
    wait_bytes(edges, edge_sems.at[0])
    for side in range(2):
        rows = pl.ds(ROWS + side * 2 * EDGE, 2 * EDGE)
        input_low[rows, :] = normed_low(edges[side].reshape(2 * EDGE, WIDTH))
    turned(grad_low, turn_a)
    io_gather.second(2)
    io_gather.second_far(0)
    down_gather.first()
    early_gather.start()
    io_gather.second_far(1)
    down_gather.second(0)
    io_gather.second_far(3)
    late_gather.start()
    io_gather.second_far(2)
    io_gather.finish()
    project(0)
    project(1)
    project(2)
    product[:, 8:, :] = (projected[0, :ROWS] * projected[2, :ROWS]).reshape(
        2, SLOT_ROWS, CHANNELS
    )
    before = (
        projected[0, ROWS : ROWS + 2 * EDGE] * projected[2, ROWS : ROWS + 2 * EDGE]
    ).reshape(2, EDGE, CHANNELS)
    product[:, :8, :] = jnp.where(place.ctx > 0, before[:, EDGE - 8 :, :], 0.0)
    convolved[...] = (
        taps[0:1, :] * product[:, 6 : 6 + SLOT_ROWS, :]
        + taps[1:2, :] * product[:, 7 : 7 + SLOT_ROWS, :]
        + taps[2:3, :] * product[:, 8 : 8 + SLOT_ROWS, :]
    ).reshape(ROWS, CHANNELS)
    gated[...] = (projected[1, :ROWS] * convolved[...]).astype(b16)

    give_mixed(0)
    give_mixed(1)
    give_mixed(2)
    down_gather.first_far()
    mixed.relay(1)
    down_gather.second_far(0)
    down_gather.second(1)
    down_gather.second(3)
    late_gather.first()
    mixed.relay(0)
    late_gather.second(0)
    mixed.relay(2)
    down_gather.second(2)
    early_gather.first()
    down_gather.second_far(1)
    own_copy.wait()
    stream = x_own[...].astype(f32) + mixed.take()
    residual[...] = stream
    normed, _ = norm_of(stream)
    second_low[own_rows, :] = (normed * gains[1:2, :]).astype(b16)
    second_spread.start()
    down_gather.second_far(3)
    down_gather.second_far(2)
    late_gather.first_far()
    late_gather.second(3)
    late_gather.second(1)
    down_gather.finish()
    pl.loop(3, 5)(inner_grad)
    early_gather.second(3)
    pl.loop(5, 7)(inner_grad)
    late_gather.second_far(0)
    second_spread.relay()
    early_gather.first_far()
    late_gather.second(2)
    late_gather.second_far(3)
    pl.loop(0, 3)(inner_grad)
    late_gather.second_far(1)
    early_gather.second(0)
    early_gather.second(1)
    early_gather.second(2)
    late_gather.second_far(2)
    early_gather.second_far(3)
    early_gather.second_far(0)
    second_spread.finish()
    late_gather.finish()
    gate_up(4)
    early_gather.second_far(1)
    gate_up(6)
    early_gather.second_far(2)
    gate_up(5)
    early_gather.finish()
    gate_up(3)
    gate_up(1)
    gate_up(2)
    gate_up(0)
    mixed.drain()
    give_branch(0)
    for part in (io_gather, down_gather, early_gather, late_gather, second_spread):
        part.drain()
    give_second(0)
    turned(second_low, turn_b)
    give_second(1)
    give_second(2)
    gradient(turn_b, 1, 2, 0, 4)
    up_piece.to_sibling(0, 4 * TILE)
    gradient(turn_b, 1, 2, 4, 7)
    up_piece.to_sibling(4 * TILE, 3 * TILE)
    second.relay(1)
    second.relay(0)
    gradient(turn_b, 0, 1, 0, 4)
    gate_piece.to_sibling(0, 4 * TILE)
    second.relay(2)
    give_branch(1)
    give_branch(2)
    up_piece.second_start()
    gradient(turn_b, 0, 1, 4, 7)
    gate_piece.to_sibling(4 * TILE, 3 * TILE)
    normed, inverse = norm_of(residual[...])
    grad_second = second.take()
    small[...] = jnp.zeros_like(small)
    keep_gain(4, grad_second * normed)
    grad_stream = grad_low[own_rows, :].astype(f32) + norm_back(
        grad_second, normed, inverse, gains[1:2, :]
    )
    grad_own[...] = grad_stream
    second_low[own_rows, :] = grad_stream.astype(b16)
    low_spread.start()
    pieces = [
        grad_stream[row : row + 1, at * TILE : (at + 1) * TILE] for row in range(2) for at in range(6)
    ]
    pieces.append(jnp.zeros((EDGE - 12, TILE), f32))
    edge_send[...] = jnp.concatenate(pieces, axis=0).astype(b16)
    for tp in range(4):

        @pl.when(even)
        def _():
            remote(
                edge_send,
                edge_recv.at[lax.div(place.tp, 2)],
                edge_sems.at[2],
                edge_sems.at[3],
                place.along_ctx(-1, tp),
            ).start()

    gradient(turn_a, 2, 0, 0, 4)
    down_piece.to_sibling(0, 4 * TILE)
    gate_piece.second_start()
    gradient(turn_a, 2, 0, 4, 7)
    down_piece.to_sibling(4 * TILE, 3 * TILE)
    low_spread.relay()
    turned(input_low, turn_a)
    branch.relay(0)
    up_piece.second_relay()
    branch.relay(2)
    branch.relay(1)
    down_piece.second_start()
    low_spread.finish()
    wait_bytes(edge_recv, edge_sems.at[3])

    @pl.when(even)
    def _():
        wait_bytes(second_low.at[pl.ds(0, 4 * EDGE), pl.ds(0, TILE)], edge_sems.at[2])

    for slot in range(2):
        packed = edge_recv[slot].astype(f32)
        rows = [
            jnp.concatenate([packed[6 * row + at : 6 * row + at + 1, :] for at in range(6)], axis=1)
            for row in range(2)
        ]
        rows.append(jnp.zeros((EDGE - 2, WIDTH), f32))
        second_low[ROWS + slot * EDGE : ROWS + (slot + 1) * EDGE, :] = jnp.concatenate(
            rows, axis=0
        ).astype(b16)

    grad_gated = dot(second_low[...], flat_io[:, 3 * CHANNELS :])
    conv_grad[:, :SLOT_ROWS, :] = (grad_gated[:ROWS] * projected[1, :ROWS]).reshape(
        2, SLOT_ROWS, CHANNELS
    )
    after = (grad_gated[ROWS:] * projected[1, ROWS + 2 * EDGE :]).reshape(2, EDGE, CHANNELS)
    conv_grad[:, SLOT_ROWS:, :] = jnp.where(place.ctx < 15, after[:, :8, :], 0.0)
    grad_proj[:, CHANNELS : 2 * CHANNELS] = (grad_gated[:ROWS] * convolved[...]).astype(b16)
    grad_product = (
        taps[2:3, :] * conv_grad[:, 0:SLOT_ROWS, :]
        + taps[1:2, :] * conv_grad[:, 1 : 1 + SLOT_ROWS, :]
        + taps[0:1, :] * conv_grad[:, 2 : 2 + SLOT_ROWS, :]
    ).reshape(ROWS, CHANNELS)
    grad_proj[:, 0:CHANNELS] = (grad_product * projected[2, :ROWS]).astype(b16)
    grad_proj[:, 2 * CHANNELS :] = (grad_product * projected[0, :ROWS]).astype(b16)
    second.drain()
    give_first(0)
    gate_piece.second_relay()
    give_first(1)
    for tap in range(3):
        small[8 + tap : 9 + tap, :] = jnp.sum(
            conv_grad[:, :SLOT_ROWS, :] * product[:, 6 + tap : 6 + tap + SLOT_ROWS, :], axis=(0, 1)
        ).reshape(1, CHANNELS)
    up_piece.first_start()
    block_own[...] = (residual[...] + branch.take()).astype(b16)
    block_keep.start()
    give_first(2)
    first.relay(1)
    down_piece.second_relay()
    turned(second_low, turn_b)
    first.relay(0)
    first.relay(2)
    block_spread.start()
    big[:, : 2 * CHANNELS] = dot(turn_a[...], grad_proj[:, : 2 * CHANNELS]).astype(b16)
    io_piece.to_sibling(0, 2 * CHANNELS)
    big[:, 2 * CHANNELS : 3 * CHANNELS] = dot(turn_a[...], grad_proj[:, 2 * CHANNELS :]).astype(b16)
    big[:, 3 * CHANNELS : 4 * CHANNELS] = dot(turn_b[...], gated[...]).astype(b16)
    io_piece.to_sibling(2 * CHANNELS, 2 * CHANNELS)
    up_piece.first_relay()
    io_piece.second_start()
    up_piece.finish()
    normed, inverse = norm_of(x_own[...].astype(f32))
    grad_first = first.take()
    keep_gain(0, grad_first * normed)
    input_own[...] = (
        grad_own[...] + norm_back(grad_first, normed, inverse, gains[0:1, :])
    ).astype(b16)
    input_keep.start()
    exchange(0, 0, [place.along_tp(by) for by in (1, 2, 3)], 8)
    block_spread.relay()
    input_spread.start()
    io_piece.second_relay()
    added(0, 0, 3, 8)
    exchange(1, 3, [place.sibling()])
    gate_piece.first_start()
    down_piece.first_start()
    gate_piece.first_relay()
    block_spread.finish()
    added(1, 3, 1)
    exchange(2, 4, [place.along_first(by) for by in (1, 2, 3)])
    io_piece.first_start()
    down_piece.first_relay()
    input_spread.relay()
    added(2, 4, 3)
    exchange(3, 7, [place.along_second(by) for by in (1, 2, 3)])
    io_piece.first_relay()
    added(3, 7, 3)
    down_piece.finish()
    gate_piece.finish()
    io_piece.finish()
    input_spread.finish()
    block_keep.wait()
    input_keep.wait()
    for part in (low_spread, block_spread, input_spread, first, branch):
        part.drain()
    for part in (down_piece, gate_piece, up_piece, io_piece):
        part.drain()


def step(*given):
    vmem = pl.BlockSpec(memory_space=pltpu.VMEM)
    smem = pl.BlockSpec(memory_space=pltpu.SMEM)
    hbm = pl.BlockSpec(memory_space=pl.ANY)
    f32, b16 = jnp.float32, jnp.bfloat16
    dma = pltpu.SemaphoreType.DMA
    own16 = pltpu.VMEM((QUARTER, WIDTH), b16)
    own32 = pltpu.VMEM((QUARTER, WIDTH), f32)
    full = pltpu.VMEM((ROWS, WIDTH), b16)
    across = pltpu.VMEM((WIDTH, ROWS), b16)
    return pl.pallas_call(
        kernel,
        out_shape=(
            jax.ShapeDtypeStruct((ROWS, WIDTH), b16),
            jax.ShapeDtypeStruct((ROWS, WIDTH), b16),
            jax.ShapeDtypeStruct((3, 16, BLOCK, PADDED), b16),
            jax.ShapeDtypeStruct((3, 12, BLOCK, PADDED), b16),
            jax.ShapeDtypeStruct((4, BLOCK, CHANNELS), f32),
            jax.ShapeDtypeStruct((3, BLOCK, HIDDEN), f32),
            jax.ShapeDtypeStruct((16, CHANNELS), f32),
        ),
        in_specs=[hbm, hbm, smem] + [hbm] * 4 + [vmem] * 2,
        out_specs=(hbm,) * 6 + (vmem,),
        scratch_shapes=[
            pltpu.VMEM((4, BLOCK, CHANNELS), f32),
            pltpu.VMEM((3, BLOCK, HIDDEN), f32),
            pltpu.VMEM((BLOCK, WIDE), b16),
            pltpu.VMEM((3, BLOCK, PADDED), b16),
            pltpu.VMEM((32, BLOCK, WIDE), b16),
            pltpu.VMEM((3, 32, BLOCK, PADDED), b16),
            pltpu.VMEM((WIDTH, PADDED), b16),
            pltpu.VMEM((ROWS, 3 * CHANNELS), b16),
            full,
            own16,
            pltpu.VMEM((2, 2, EDGE, WIDTH), b16),
            pltpu.VMEM((EDGE, TILE), b16),
            pltpu.VMEM((2, EDGE, TILE), b16),
            pltpu.VMEM((ROWS + 4 * EDGE, WIDTH), b16),
            across,
            across,
            full,
            full,
            pltpu.VMEM((2, 2, HALF, WIDTH), b16),
            pltpu.VMEM((2, 2, QUARTER, WIDTH), b16),
            pltpu.VMEM((ROWS + 2 * EDGE, WIDTH), b16),
            own32,
            pltpu.VMEM((3, ROWS + 4 * EDGE, CHANNELS), f32),
            pltpu.VMEM((2, 8 + SLOT_ROWS, CHANNELS), f32),
            pltpu.VMEM((ROWS, CHANNELS), f32),
            pltpu.VMEM((ROWS, CHANNELS), b16),
            own32,
            own16,
            own16,
            pltpu.VMEM((2, SLOT_ROWS + 8, CHANNELS), f32),
            pltpu.VMEM((16, BLOCK, PADDED), b16),
            pltpu.VMEM((3, 3, BLOCK, PADDED), b16),
            pltpu.VMEM((16, BLOCK, WIDE), b16),
            pltpu.VMEM((12, BLOCK, WIDE), b16),
            pltpu.VMEM((10, 16, CHANNELS), f32),
            dma((Gather.SEMS,)),
            dma((Gather.SEMS,)),
            dma((2, Gather.SEMS)),
            dma((2, Gather.SEMS)),
            dma((4, Scatter.SEMS)),
            dma((4, TpSum.SEMS)),
            dma((4, TpSpread.SEMS)),
            dma((4,)),
            dma((2, 4)),
            dma((10,)),
        ],
        compiler_params=pltpu.CompilerParams(
            collective_id=0, has_side_effects=True, vmem_limit_bytes=63 * 2**20
        ),
        name="step",
    )(*given)


def nesterov(weight, moment, average, gradient, step_rate):
    moment_new = momentum * moment + gradient
    weight_new = weight - step_rate * (gradient + momentum * moment_new)
    average_new = average_decay * average + (1.0 - average_decay) * weight_new
    return (moment_new, weight_new, average_new)


def update_kernel(*refs):
    block_in, input_in = refs[:2]
    old = [refs[2 + 3 * at : 5 + 3 * at] for at in range(6)]
    io_grad, gud_grad, small_grad = refs[20:23]
    block_out, input_out = refs[23:25]
    new = [refs[25 + 3 * at : 28 + 3 * at] for at in range(6)]
    block_held, input_held, wide_held, io_held, gud_held, small_held = refs[43:49]
    held = [refs[49 + 3 * at : 52 + 3 * at] for at in range(6)]
    in_sems, out_sems = refs[67:]

    def moved(source, target, sems, at):
        copy = pltpu.make_async_copy(source, target, sems.at[at])
        copy.start()
        return copy

    order = (2, 3, 0, 1, 4, 5)
    input_load = moved(input_in, input_held, in_sems, 18)
    gud_load = moved(gud_grad, gud_held, in_sems, 19)
    loads = {}
    for matrix in order:
        loads[matrix] = [
            moved(old[matrix][at], held[matrix][at], in_sems, 3 * matrix + at) for at in range(3)
        ]
        if matrix == 2:
            io_load = moved(io_grad, io_held, in_sems, 20)
            small_load = moved(small_grad, small_held, in_sems, 21)
    block_load = moved(block_in, block_held, in_sems, 22)
    stores = []
    input_load.wait()
    for half in range(2):
        rows = pl.ds(half * SLOT_ROWS, SLOT_ROWS)
        wide_held[rows, :] = input_held[rows, :].astype(jnp.float32)
        stores.append(moved(wide_held.at[rows], input_out.at[rows], out_sems, 18 + half))
    for matrix in order:
        for copy in loads[matrix]:
            copy.wait()
        weight, moment, average = held[matrix]
        every, rate = slice(None), matrix_rate
        if matrix == 0:
            io_load.wait()
            parts = [(at, io_held[at]) for at in range(3)]
        elif matrix == 1:
            parts = [(every, io_held[3])]
        elif matrix == 2:
            gud_load.wait()
            parts = [(at, gud_held[at]) for at in range(2)]
        elif matrix == 3:
            parts = [(every, gud_held[2])]
        elif matrix == 4:
            small_load.wait()
            rate = small_rate
            parts = [
                (
                    (slice(row, row + 1), slice(at * CHANNELS, (at + 1) * CHANNELS)),
                    small_held[4 * row + at : 4 * row + at + 1, :],
                )
                for row in range(2)
                for at in range(4)
            ]
        else:
            parts, rate = [(every, small_held[8:11, :])], small_rate
        for at, gradient in parts:
            moment[at], weight[at], average[at] = nesterov(
                weight[at], moment[at], average[at], gradient, rate
            )
        for at, source in enumerate((moment, weight, average)):
            stores.append(moved(source, new[matrix][at], out_sems, 3 * matrix + at))
    block_load.wait()
    stores.append(moved(block_held, block_out, out_sems, 20))
    for copy in stores:
        copy.wait()


def update(block, input_low, arrays, io_grad, gud_grad, small):
    hbm = pl.BlockSpec(memory_space=pl.ANY)
    f32 = jnp.float32
    like = lambda a: jax.ShapeDtypeStruct(a.shape, a.dtype)
    held = lambda a: pltpu.VMEM(a.shape, a.dtype)
    return pl.pallas_call(
        update_kernel,
        out_shape=(
            like(block),
            jax.ShapeDtypeStruct((ROWS, WIDTH), f32),
            *[like(a) for a in arrays],
        ),
        in_specs=[hbm] * 23,
        out_specs=(hbm,) * 20,
        scratch_shapes=[
            held(block),
            held(input_low),
            pltpu.VMEM((ROWS, WIDTH), f32),
            held(io_grad),
            held(gud_grad),
            held(small),
            *[held(a) for a in arrays],
            pltpu.SemaphoreType.DMA((23,)),
            pltpu.SemaphoreType.DMA((21,)),
        ],
        compiler_params=pltpu.CompilerParams(vmem_limit_bytes=62 * 2**20),
        name="update",
    )(block, input_low, *arrays, io_grad, gud_grad, small)


def on_device(
    hidden,
    lengths,
    cotangent,
    in_weight,
    in_moment,
    in_average,
    out_weight,
    out_moment,
    out_average,
    gate_up_weight,
    gate_up_moment,
    gate_up_average,
    down_weight,
    down_moment,
    down_average,
    norm_gains,
    gain_moment,
    gain_average,
    conv_taps,
    taps_moment,
    taps_average,
):
    slot_count, seq_len, model_width = hidden.shape
    row_count = slot_count * seq_len
    block_output, input_low_grad, _, _, io_sum, gud_sum, small = step(
        hidden.reshape(row_count, model_width),
        cotangent.reshape(row_count, model_width),
        lengths,
        in_weight,
        out_weight.T,
        gate_up_weight,
        down_weight.T,
        norm_gains,
        conv_taps,
    )
    matrices = (
        (in_weight, in_moment, in_average),
        (out_weight.T, out_moment.T, out_average.T),
        (gate_up_weight, gate_up_moment, gate_up_average),
        (down_weight.T, down_moment.T, down_average.T),
    )
    smalls = (norm_gains, gain_moment, gain_average, conv_taps, taps_moment, taps_average)
    block_output, input_grad, *new = update(
        block_output,
        input_low_grad,
        [a for group in matrices for a in group] + list(smalls),
        io_sum,
        gud_sum,
        small,
    )
    return (
        block_output.reshape(slot_count, seq_len, model_width),
        input_grad.reshape(slot_count, seq_len, model_width),
        *new[0:3],
        *[a.T for a in new[3:6]],
        *new[6:9],
        *[a.T for a in new[9:12]],
        *new[12:18],
    )


def solution(mesh):
    placed = (
        P("shard", "ctx", None),
        P("shard"),
        P("shard", "ctx", None),
        P(None, ("shard", "ctx"), "tp"),
        P(None, ("shard", "ctx"), "tp"),
        P(None, ("shard", "ctx"), "tp"),
        P("tp", ("shard", "ctx")),
        P("tp", ("shard", "ctx")),
        P("tp", ("shard", "ctx")),
        P(None, ("shard", "ctx"), "tp"),
        P(None, ("shard", "ctx"), "tp"),
        P(None, ("shard", "ctx"), "tp"),
        P("tp", ("shard", "ctx")),
        P("tp", ("shard", "ctx")),
        P("tp", ("shard", "ctx")),
        P(),
        P(),
        P(),
        P(None, "tp"),
        P(None, "tp"),
        P(None, "tp"),
    )
    return jax.shard_map(
        on_device,
        mesh=mesh,
        in_specs=placed,
        out_specs=(
            P("shard", "ctx", None),
            P("shard", "ctx", None),
            P(None, ("shard", "ctx"), "tp"),
            P(None, ("shard", "ctx"), "tp"),
            P(None, ("shard", "ctx"), "tp"),
            P("tp", ("shard", "ctx")),
            P("tp", ("shard", "ctx")),
            P("tp", ("shard", "ctx")),
            P(None, ("shard", "ctx"), "tp"),
            P(None, ("shard", "ctx"), "tp"),
            P(None, ("shard", "ctx"), "tp"),
            P("tp", ("shard", "ctx")),
            P("tp", ("shard", "ctx")),
            P("tp", ("shard", "ctx")),
            P(),
            P(),
            P(),
            P(None, "tp"),
            P(None, "tp"),
            P(None, "tp"),
        ),
        check_vma=False,
    )
```

```python
import functools

import jax
import jax.numpy as jnp
from jax import lax
from jax.experimental import pallas as pl
from jax.experimental.pallas import tpu as pltpu
from jax.sharding import PartitionSpec as P

MESH = pl.DeviceIdType.MESH
epsilon = 1e-05
momentum = 0.9
average_decay = 0.9
matrix_rate = 0.0004
small_rate = 0.005
WIDTH = 1536
CHANNELS = 384
HIDDEN = 1728
TILE = 256
EDGE = 16
EARLY = 4
SLOTS = ((0, 512), (512, 512), (1024, 512))
WIDE = 4 * CHANNELS
PADDED = 1792
ROWS = 512
QUARTER = 128
SLOT_ROWS = 256
BLOCK = 48
HALF = QUARTER // 2


class Place:
    def __init__(self, flip=False):
        self.shard = lax.axis_index("shard")
        self.ctx = lax.axis_index("ctx")
        self.tp = lax.axis_index("tp")
        self.y = self.shard * 2 + lax.div(self.ctx, 8)
        self.z = lax.rem(lax.div(self.ctx, 2), 4)
        self.core = lax.rem(self.ctx, 2)
        self.way = 1 - self.core if flip else self.core
        self.first = self.y * (1 - self.way) + self.z * self.way
        self.second = self.z * (1 - self.way) + self.y * self.way

    def turn(self, value, by):
        return lax.rem(value + by + 4, 4)

    def device(self, y, z, core):
        return (lax.div(y, 2), lax.rem(y, 2) * 8 + z * 2 + core, self.tp)

    def grid_device(self, first, second):
        y = first * (1 - self.way) + second * self.way
        z = second * (1 - self.way) + first * self.way
        return self.device(y, z, self.core)

    def block(self, first, second):
        y = first * (1 - self.way) + second * self.way
        z = second * (1 - self.way) + first * self.way
        return y * 8 + z * 2 + self.core

    def along_first(self, by):
        return self.grid_device(self.turn(self.first, by), self.second)

    def along_second(self, by):
        return self.grid_device(self.first, self.turn(self.second, by))

    def along_tp(self, by):
        return (self.shard, self.ctx, self.turn(self.tp, by))

    def along_ctx(self, by, tp=None):
        return (self.shard, lax.rem(self.ctx + by + 16, 16), self.tp if tp is None else tp)

    def sibling(self):
        return self.device(self.y, self.z, 1 - self.core)

    def greet(self):
        barrier = pltpu.get_barrier_semaphore()
        friends = [self.sibling()]
        for tp in range(4):
            friends += [self.along_ctx(1, tp), self.along_ctx(-1, tp)]
        for by in (1, 2, 3):
            friends += [self.along_first(by), self.along_second(by), self.along_tp(by)]
        for friend in friends:
            pl.semaphore_signal(barrier, inc=1, device_id=friend, device_id_type=MESH)
        return len(friends)


def remote(source, target, send_sem, recv_sem, device):
    return pltpu.make_async_remote_copy(
        src_ref=source,
        dst_ref=target,
        send_sem=send_sem,
        recv_sem=recv_sem,
        device_id=device,
        device_id_type=MESH,
    )


def wait_bytes(spot, sem):
    pltpu.make_async_copy(spot, spot, sem).wait()


class Gather:
    SEMS = 12

    def __init__(self, place, local, whole, sems, joint=None):
        self.place, self.local, self.whole, self.sems = place, local, whole, sems
        self.joint = joint
        self.half = local.shape[-1] // 2

    def part(self, block, half=None):
        spot = self.whole.at[:, block] if self.whole.ndim == 4 else self.whole.at[block]
        if half is None:
            return spot
        columns = pl.ds(half * self.half, self.half)
        return spot.at[:, :, columns] if self.whole.ndim == 4 else spot.at[:, columns]

    def send(self, source, target, at, device):
        remote(source, target, self.sems.at[0], self.sems.at[at], device).start()

    def arrived(self, blocks, at):
        spot = self.whole if self.joint is None else self.joint
        few = pl.ds(0, blocks)
        if spot is not False:
            wait_bytes(spot.at[:, few] if spot.ndim == 4 else spot.at[few], self.sems.at[at])

    def block(self, back, by):
        p = self.place
        return p.block(p.turn(p.first, -back), p.turn(p.second, -by))

    def to_second(self, source, back, by):
        spot = self.part(self.block(back, 0))
        self.send(source, spot, 3 + back, self.place.along_second(1))
        self.send(source, spot, 3 + back, self.place.along_second(-1))
        self.to_sibling(source, back, by)

    def to_sibling(self, source, back, by):
        self.send(source, self.part(self.block(back, by)), 11, self.place.sibling())

    def start(self):
        p = self.place
        spot = self.part(self.block(0, 0))
        self.send(self.local, spot, 1, p.along_first(1))
        self.send(self.local, spot, 1, p.along_first(-1))
        self.to_second(self.local, 0, 0)

    def first(self):
        p = self.place
        self.arrived(2, 1)
        for back, half, by in ((1, 0, 1), (3, 1, -1)):
            piece = self.part(self.block(back, 0), half)
            self.send(piece, piece, 2, p.along_first(by))
        for back in (1, 3):
            self.to_second(self.part(self.block(back, 0)), back, 0)

    def first_far(self):
        self.arrived(1, 2)
        self.to_second(self.part(self.block(2, 0)), 2, 0)

    def second(self, back):
        p = self.place
        self.arrived(2, 3 + back)
        for by, half, step in ((1, 0, 1), (3, 1, -1)):
            piece = self.part(self.block(back, by), half)
            self.send(piece, piece, 7 + back, p.along_second(step))
        for by in (1, 3):
            self.to_sibling(self.part(self.block(back, by)), back, by)

    def second_far(self, back):
        self.arrived(1, 7 + back)
        self.to_sibling(self.part(self.block(back, 2)), back, 2)

    def finish(self):
        self.arrived(16, 11)

    def drain(self):
        self.arrived(31, 0)


class Both:
    def __init__(self, *parts):
        self.parts = parts

    def each(self, name, *given):
        for part in self.parts:
            getattr(part, name)(*given)

    def start(self):
        self.each("start")

    def first(self):
        self.each("first")

    def first_far(self):
        self.each("first_far")

    def second(self, back):
        self.each("second", back)

    def second_far(self, back):
        self.each("second_far", back)

    def finish(self):
        self.each("finish")

    def drain(self):
        self.each("drain")


class Scatter:
    SEMS = 6

    def __init__(self, place, partial, width, recv, out, stage, sems, local_sems):
        self.place, self.width, self.out = place, width, out
        self.sib_recv, self.second_recv, self.first_recv = recv
        self.stage, self.sems, self.local_sems = stage, sems, local_sems
        columns = pl.ds(0, width)
        self.blocks = partial.reshape(16, 2, BLOCK, PADDED).at[:, :, :, columns]
        self.grid = partial.reshape(4, 4, 2, BLOCK, PADDED).at[:, :, :, :, columns]
        self.rows = partial.reshape(32, BLOCK, PADDED).at[:, :, columns]

    def mine(self, first, second):
        return lax.div(self.place.block(first, second), 2)

    def arrived(self, spot, at):
        wait_bytes(spot, self.sems.at[at])

    def move(self, source, target, at, device):
        remote(source, target, self.sems.at[0], self.sems.at[at], device).start()

    def to_sibling(self, start=0, width=None):
        p = self.place
        columns = pl.ds(start, self.width if width is None else width)
        source = self.blocks.at[:, 1 - p.core, :, columns]
        self.move(source, self.sib_recv.at[:, :, columns], 1, p.sibling())

    def fetch(self, source, count):
        if self.stage is None:
            return source
        target = self.stage.at[pl.ds(0, count), :, pl.ds(0, self.width)]
        copy = pltpu.make_async_copy(source, target, self.local_sems.at[0])
        copy.start()
        copy.wait()
        return target

    def add_to(self, at, held, parts):
        core = self.place.core
        if len(parts) == 1:
            self.blocks[at, core] = self.blocks[at, core] + held[parts[0]]
        else:
            total = self.blocks[at, core].astype(jnp.float32)
            for part in parts:
                total = total + held[part].astype(jnp.float32)
            self.blocks[at, core] = total.astype(jnp.bfloat16)

    def pair(self, half, by, target, at, step):
        p = self.place
        there = p.turn(p.second, by)
        two = pl.ds(2 * half, 2)

        @pl.when(p.core == 0)
        def _():
            self.move(self.grid.at[two, there, 0], target, at, p.along_second(step))

        @pl.when(p.core == 1)
        def _():
            self.move(self.grid.at[there, two, 1], target, at, p.along_second(step))

    def second_start(self):
        p = self.place
        self.arrived(self.sib_recv, 1)
        held = self.fetch(self.sib_recv, 16)

        @pl.loop(0, 4)
        def _(first):
            at = self.mine(first, p.turn(p.second, 2))
            self.add_to(at, held, [at])

        for half, step in ((0, 1), (1, -1)):
            self.pair(half, 2, self.second_recv.at[pl.ds(8 + 2 * half, 2)], 2, step)

        @pl.loop(0, 12)
        def _(other):
            away = lax.rem(lax.div(other, 4) + 3, 4)
            at = self.mine(lax.rem(other, 4), p.turn(p.second, away))
            self.add_to(at, held, [at])

        for half, step in ((0, 1), (1, -1)):
            spot = self.second_recv.at[pl.ds(4 * half + 2 * (1 - half), 2)]
            self.pair(1 - half, step, spot, 3, step)

    def second_relay(self):
        p = self.place
        self.arrived(self.second_recv.at[pl.ds(8, 4)], 2)
        held = self.fetch(self.second_recv.at[pl.ds(8, 4)], 4)
        for half, step in ((0, 1), (1, -1)):

            @pl.loop(0, 2)
            def _(first):
                at = self.mine(2 * half + first, p.turn(p.second, step))
                self.add_to(at, held, [2 * half + first])

            spot = self.second_recv.at[pl.ds(4 * half + 2 * half, 2)]
            self.pair(half, step, spot, 3, step)

    def first_start(self):
        p = self.place
        self.arrived(self.second_recv.at[pl.ds(0, 8)], 3)
        held = self.fetch(self.second_recv.at[pl.ds(0, 8)], 8)

        @pl.loop(0, 4)
        def _(first):
            self.add_to(self.mine(first, p.second), held, [first, 4 + first])

        for half, step in ((0, 1), (1, -1)):
            self.strip(half, 2, self.first_recv.at[2], 4, step)
        for half, step in ((0, 1), (1, -1)):
            self.strip(1 - half, step, self.first_recv.at[half], 5, step)

    def columns(self, half):
        return pl.ds(half * (self.width // 2), self.width // 2)

    def strip(self, half, by, target, at, step):
        p = self.place
        source = self.blocks.at[self.mine(p.turn(p.first, by), p.second), p.core]
        columns = self.columns(half)
        self.move(source.at[:, columns], target.at[:, columns], at, p.along_first(step))

    def first_relay(self):
        p = self.place
        self.arrived(self.first_recv.at[2], 4)
        for half, step in ((0, 1), (1, -1)):
            columns = self.columns(half)
            at = self.mine(p.turn(p.first, step), p.second)
            both = self.blocks[at, p.core, :, columns].astype(jnp.float32)
            both = both + self.first_recv[2, :, columns].astype(jnp.float32)
            self.blocks[at, p.core, :, columns] = both.astype(jnp.bfloat16)
            self.strip(half, step, self.first_recv.at[half], 5, step)

    def finish(self):
        p = self.place
        self.arrived(self.first_recv.at[pl.ds(0, 2)], 5)
        total = self.blocks[self.mine(p.first, p.second), p.core].astype(jnp.float32)
        for by in range(2):
            total = total + self.first_recv[by].astype(jnp.float32)
        wide, out, members, columns, sem = self.out
        for member in range(members):
            wide[member] = total[:, member * columns : (member + 1) * columns]
        copy = pltpu.make_async_copy(wide, out, sem)
        copy.start()
        self.store = copy

    def drain(self):
        self.arrived(self.rows.at[pl.ds(0, 31)], 0)
        self.store.wait()


class TpSum:
    SEMS = 5

    def __init__(self, place, send, relay, final, sems):
        self.place, self.send, self.relay_in, self.final = place, send, relay, final
        self.sems = sems

    def rows(self, by, half):
        p = self.place
        start = p.turn(p.tp, by) * QUARTER + half * HALF
        return pl.ds(pl.multiple_of(start, HALF), HALF)

    def move(self, source, target, at, by):
        remote(source, target, self.sems.at[0], self.sems.at[at], self.place.along_tp(by)).start()

    def give(self, values, slot):
        columns = pl.ds(*SLOTS[slot])
        self.send[:, columns] = values.astype(jnp.bfloat16)
        for half, by in ((0, 1), (1, -1)):
            source = self.send.at[self.rows(2, half), columns]
            self.move(source, self.relay_in.at[half, :, columns], 2 + slot, by)
        for half, by in ((0, 1), (1, -1)):
            source = self.send.at[self.rows(by, 1 - half), columns]
            target = self.final.at[half, pl.ds((1 - half) * HALF, HALF), columns]
            self.move(source, target, 1, by)

    def relay(self, slot):
        columns = pl.ds(*SLOTS[slot])
        wait_bytes(self.relay_in.at[:, :, columns], self.sems.at[2 + slot])
        for half, by in ((0, 1), (1, -1)):
            rows = self.rows(by, half)
            both = self.send[rows, columns].astype(jnp.float32)
            both = both + self.relay_in[half, :, columns].astype(jnp.float32)
            self.send[rows, columns] = both.astype(jnp.bfloat16)
            target = self.final.at[half, pl.ds(half * HALF, HALF), columns]
            self.move(self.send.at[rows, columns], target, 1, by)

    def take(self):
        p = self.place
        wait_bytes(self.final, self.sems.at[1])
        rows = pl.ds(pl.multiple_of(p.tp * QUARTER, QUARTER), QUARTER)
        total = self.send[rows, :].astype(jnp.float32)
        for half in range(2):
            total = total + self.final[half].astype(jnp.float32)
        return total

    def drain(self):
        wait_bytes(self.send.at[pl.ds(0, 3 * QUARTER)], self.sems.at[0])


class TpSpread:
    SEMS = 3

    def __init__(self, place, source, whole, sems):
        self.place, self.source, self.whole, self.sems = place, source, whole, sems

    def spot(self, by, half):
        p = self.place
        start = p.turn(p.tp, by) * QUARTER + half * HALF
        return self.whole.at[pl.ds(pl.multiple_of(start, HALF), HALF)]

    def move(self, source, target, at, by):
        remote(source, target, self.sems.at[0], self.sems.at[at], self.place.along_tp(by)).start()

    def start(self):
        for at, half, by in ((1, 0, 1), (1, 1, -1), (2, 1, 1), (2, 0, -1)):
            self.move(self.source.at[pl.ds(half * HALF, HALF)], self.spot(0, half), at, by)

    def arrived(self, rows, at):
        wait_bytes(self.whole.at[pl.ds(0, rows)], self.sems.at[at])

    def relay(self):
        self.arrived(QUARTER, 1)
        for half, by in ((0, 1), (1, -1)):
            spot = self.spot(-by, half)
            self.move(spot, spot, 2, by)

    def finish(self):
        self.arrived(2 * QUARTER, 2)

    def drain(self):
        self.arrived(3 * QUARTER, 0)


def dot(left, right):
    return jnp.dot(left, right, preferred_element_type=jnp.float32)


def dot_t(left, right):
    return lax.dot_general(
        left, right, (((1,), (1,)), ((), ())), preferred_element_type=jnp.float32
    )


def turned(source, target):
    @pl.loop(0, WIDTH // TILE)
    def _(at):
        at = pl.multiple_of(at * TILE, TILE)
        target[pl.ds(at, TILE), :] = source[pl.ds(0, ROWS), pl.ds(at, TILE)].T


def slot_rows(slot):
    start, width = SLOTS[slot]
    return slice(start, start + width)


def own_rows_of(place):
    return pl.ds(pl.multiple_of(place.tp * QUARTER, QUARTER), QUARTER)


def norm_of(values):
    inverse = lax.rsqrt(jnp.mean(values * values, axis=-1, keepdims=True) + epsilon)
    return values * inverse, inverse


def norm_back(grad, normed, inverse, gain):
    scaled = grad * gain
    return inverse * (scaled - normed * jnp.mean(scaled * normed, axis=-1, keepdims=True))


def kernel(
    x,
    cotangent,
    lengths,
    in_weight,
    out_weight,
    gate_up_weight,
    down_weight,
    gains,
    taps,
    block_out,
    input_out,
    sib_hbm,
    second_hbm,
    io_grad,
    gud_grad,
    small,
    io_wide,
    gud_wide,
    io_local,
    gud_local,
    io,
    weights,
    big,
    grad_proj,
    grad_low,
    x_own,
    edges,
    edge_send,
    edge_recv,
    input_low,
    turn_a,
    turn_b,
    send_a,
    send_b,
    relays,
    finals,
    second_low,
    residual,
    projected,
    product,
    convolved,
    gated,
    grad_own,
    block_own,
    input_own,
    conv_grad,
    stage,
    first_recv,
    io_sib_recv,
    io_second_recv,
    small_recv,
    io_sems,
    down_sems,
    early_sems,
    late_sems,
    scatter_sems,
    sum_sems,
    spread_sems,
    edge_sems,
    small_sems,
    local_sems,
):
    f32, b16 = jnp.float32, jnp.bfloat16
    place = Place()
    own_rows = own_rows_of(place)
    tiles = PADDED // TILE
    mine = place.block(place.first, place.second)
    flat_io = io.reshape(WIDTH, WIDE)
    flat_weights = weights.reshape(3, WIDTH, PADDED)

    loads = [
        pltpu.make_async_copy(source, target, local_sems.at[6 + at])
        for at, (source, target) in enumerate(
            (
                (in_weight, io_wide.at[pl.ds(0, 3)]),
                (out_weight, io_wide.at[3]),
                (gate_up_weight, gud_wide.at[pl.ds(0, 2)]),
                (down_weight, gud_wide.at[2]),
            )
        )
    ]
    x_copy = pltpu.make_async_copy(x, send_b, local_sems.at[1])
    low_copy = pltpu.make_async_copy(cotangent, grad_low, local_sems.at[2])
    own_copy = pltpu.make_async_copy(x.at[own_rows], x_own, local_sems.at[3])
    for copy in (*loads, x_copy, low_copy, own_copy):
        copy.start()
    friends = place.greet()
    for copy in loads[:2]:
        copy.wait()
    for member in range(4):
        io_local[:, member * CHANNELS : (member + 1) * CHANNELS] = io_wide[member].astype(b16)
    io[mine] = io_local[...]
    pl.semaphore_wait(pltpu.get_barrier_semaphore(), friends)
    other_place = Place(flip=True)
    two = pl.ds(0, 2)
    io_gather = Gather(place, io_local, io, io_sems)
    down_gather = Gather(place, gud_local.at[2], weights.at[2], down_sems)

    def columns_pair(start, widths, sems):
        joint, parts = weights.at[two, :, :, pl.ds(start, sum(widths))], []
        for way, width in zip((place, other_place), widths):
            columns = pl.ds(start, width)
            local, whole = gud_local.at[two, :, columns], weights.at[two, :, :, columns]
            parts.append(Gather(way, local, whole, sems, False if parts else joint))
            start += width
        return Both(*parts)

    early_gather = columns_pair(0, (512, 512), early_sems)
    late_gather = columns_pair(1024, (256, 512), late_sems)
    mixed = TpSum(place, send_a, relays.at[0], finals.at[0], sum_sems.at[0])
    second = TpSum(place, send_b, relays.at[1], finals.at[1], sum_sems.at[1])
    branch = TpSum(place, send_a, relays.at[0], finals.at[0], sum_sems.at[2])
    first = TpSum(place, send_b, relays.at[1], finals.at[1], sum_sems.at[3])
    second_spread = TpSpread(place, second_low.at[own_rows], second_low, spread_sems.at[0])
    low_spread = TpSpread(place, second_low.at[own_rows], second_low, spread_sems.at[1])
    block_spread = TpSpread(place, block_own, block_out, spread_sems.at[2])
    input_spread = TpSpread(place, input_own, input_out, spread_sems.at[3])
    block_keep = pltpu.make_async_copy(block_own, block_out.at[own_rows], local_sems.at[4])
    input_keep = pltpu.make_async_copy(input_own, input_out.at[own_rows], local_sems.at[5])
    even = lax.rem(place.tp, 2) == 0

    def piece(at):
        return Scatter(
            place,
            flat_weights.at[at],
            PADDED,
            (sib_hbm.at[at], second_hbm.at[at], first_recv.at[at]),
            (
                gud_wide.at[pl.ds(at, 1)],
                gud_grad.at[pl.ds(at, 1)],
                1,
                HIDDEN,
                local_sems.at[6 + at],
            ),
            stage,
            scatter_sems.at[at],
            local_sems,
        )

    gate_piece, up_piece, down_piece = piece(0), piece(1), piece(2)
    io_piece = Scatter(
        place,
        big,
        WIDE,
        (io_sib_recv, io_second_recv, gud_local.at[:, :, pl.ds(0, WIDE)]),
        (io_wide, io_grad, 4, CHANNELS, local_sems.at[9]),
        None,
        scatter_sems.at[3],
        local_sems,
    )

    def normed_low(values):
        normed, _ = norm_of(values.astype(f32))
        return (normed * gains[0:1, :]).astype(b16)

    def send_edges():
        slots_x = x.reshape(2, SLOT_ROWS, WIDTH)
        for side, start, by in ((0, SLOT_ROWS - EDGE, 1), (1, 0, -1)):
            remote(
                slots_x.at[:, pl.ds(start, EDGE)],
                edges.at[side],
                edge_sems.at[0],
                edge_sems.at[1],
                place.along_ctx(by),
            ).start()

    def project(member):
        if member == 0:
            columns = slice(0, 3 * CHANNELS)
            whole = dot(input_low[...], flat_io[:, columns])
            for at in range(3):
                projected[at] = whole[:, at * CHANNELS : (at + 1) * CHANNELS]

    def give_mixed(slot):
        mixed.give(dot_t(gated[...], flat_io[slot_rows(slot), 3 * CHANNELS :]), slot)

    def inner_grad(at):
        columns = pl.ds(pl.multiple_of(at * TILE, TILE), TILE)
        big[0:ROWS, columns] = dot(grad_low[...], flat_weights[2, :, columns]).astype(b16)

    def gate_up(at):
        columns = pl.ds(at * TILE, TILE)
        parts = [slice(0, SLOT_ROWS), slice(SLOT_ROWS, ROWS)]
        gates = [dot(second_low[rows, :], flat_weights[0, :, columns]) for rows in parts]
        ups = [dot(second_low[rows, :], flat_weights[1, :, columns]) for rows in parts]
        for half, rows in enumerate(parts):
            gate, up = gates[half], ups[half]
            grad_inner = big[rows, columns].astype(f32)
            sigmoid = 0.5 * jnp.tanh(0.5 * gate) + 0.5
            active = gate * sigmoid
            big[rows, columns] = (active * up).astype(b16)
            start = ROWS + rows.start
            big[start : start + SLOT_ROWS, columns] = (
                grad_inner * up * (sigmoid + active * (1.0 - sigmoid))
            ).astype(b16)
            big[start + ROWS : start + ROWS + SLOT_ROWS, columns] = (grad_inner * active).astype(b16)

    def give_second(slot):
        rows = slot_rows(slot)
        part = dot_t(big[ROWS : 2 * ROWS, :], flat_weights[0, rows, :])
        part = part + dot_t(big[2 * ROWS :, :], flat_weights[1, rows, :])
        second.give(part, slot)

    def give_branch(slot):
        branch.give(dot_t(big[0:ROWS, :], flat_weights[2, slot_rows(slot), :]), slot)

    def give_first(slot):
        first.give(dot_t(grad_proj[...], flat_io[slot_rows(slot), : 3 * CHANNELS]), slot)

    def gradient(left, at, member, start, stop):
        @pl.loop(start, stop)
        def _(tile):
            columns = pl.ds(pl.multiple_of(tile * TILE, TILE), TILE)
            flat_weights[at, :, columns] = dot(
                left[...], big[member * ROWS : (member + 1) * ROWS, columns]
            ).astype(b16)

    def keep_gain(start, values):
        total = jnp.sum(values, axis=0, keepdims=True)
        for at in range(4):
            small[start + at : start + at + 1, :] = total[:, at * CHANNELS : (at + 1) * CHANNELS]

    def exchange(phase, start, devices, rows=16):
        few = pl.ds(0, rows)
        for at, device in enumerate(devices):
            remote(
                small.at[few],
                small_recv.at[start + at, few],
                small_sems.at[0, phase],
                small_sems.at[1, phase],
                device,
            ).start()

    def added(phase, start, count, rows=16):
        spots = small_recv.at[pl.ds(start, count), pl.ds(0, rows)]
        for side in range(2):
            wait_bytes(spots, small_sems.at[side, phase])
        total = small[0:rows, :]
        for at in range(count):
            total = total + small_recv[start + at, 0:rows, :]
        small[0:rows, :] = total

    io_gather.start()
    x_copy.wait()

    @pl.loop(0, ROWS, step=64)
    def _(at):
        input_low[pl.ds(at, 64), :] = normed_low(send_b[pl.ds(at, 64), :])

    for copy in loads[2:]:
        copy.wait()
    for member in range(3):
        gud_local[member, :, :HIDDEN] = gud_wide[member].astype(b16)
    gud_local[:, :, HIDDEN:] = jnp.zeros((3, BLOCK, PADDED - HIDDEN), b16)
    weights[:, mine] = gud_local[...]
    down_gather.start()
    io_gather.first()
    send_edges()
    io_gather.first_far()
    io_gather.second(0)
    io_gather.second(1)
    low_copy.wait()
    positions = place.ctx * SLOT_ROWS + lax.broadcasted_iota(jnp.int32, (SLOT_ROWS, 1), 0)
    for slot in range(2):
        rows = slice(slot * SLOT_ROWS, (slot + 1) * SLOT_ROWS)
        kept = jnp.where(positions < lengths[slot], 1.0, 0.0)
        grad_low[rows, :] = (grad_low[rows, :].astype(f32) * kept).astype(b16)
    io_gather.second(3)
    wait_bytes(edges, edge_sems.at[1])
    wait_bytes(edges, edge_sems.at[0])
    for side in range(2):
        rows = pl.ds(ROWS + side * 2 * EDGE, 2 * EDGE)
        input_low[rows, :] = normed_low(edges[side].reshape(2 * EDGE, WIDTH))
    turned(grad_low, turn_a)
    io_gather.second(2)
    io_gather.second_far(0)
    down_gather.first()
    early_gather.start()
    io_gather.second_far(1)
    down_gather.second(0)
    io_gather.second_far(3)
    late_gather.start()
    io_gather.second_far(2)
    io_gather.finish()
    project(0)
    project(1)
    project(2)
    product[:, 8:, :] = (projected[0, :ROWS] * projected[2, :ROWS]).reshape(
        2, SLOT_ROWS, CHANNELS
    )
    before = (
        projected[0, ROWS : ROWS + 2 * EDGE] * projected[2, ROWS : ROWS + 2 * EDGE]
    ).reshape(2, EDGE, CHANNELS)
    product[:, :8, :] = jnp.where(place.ctx > 0, before[:, EDGE - 8 :, :], 0.0)
    convolved[...] = (
        taps[0:1, :] * product[:, 6 : 6 + SLOT_ROWS, :]
        + taps[1:2, :] * product[:, 7 : 7 + SLOT_ROWS, :]
        + taps[2:3, :] * product[:, 8 : 8 + SLOT_ROWS, :]
    ).reshape(ROWS, CHANNELS)
    gated[...] = (projected[1, :ROWS] * convolved[...]).astype(b16)

    give_mixed(0)
    give_mixed(1)
    give_mixed(2)
    down_gather.first_far()
    mixed.relay(1)
    down_gather.second_far(0)
    down_gather.second(1)
    down_gather.second(3)
    late_gather.first()
    mixed.relay(0)
    late_gather.second(0)
    mixed.relay(2)
    down_gather.second(2)
    early_gather.first()
    down_gather.second_far(1)
    own_copy.wait()
    stream = x_own[...].astype(f32) + mixed.take()
    residual[...] = stream
    normed, _ = norm_of(stream)
    second_low[own_rows, :] = (normed * gains[1:2, :]).astype(b16)
    second_spread.start()
    down_gather.second_far(3)
    down_gather.second_far(2)
    late_gather.first_far()
    late_gather.second(3)
    late_gather.second(1)
    down_gather.finish()
    pl.loop(3, 5)(inner_grad)
    early_gather.second(3)
    pl.loop(5, 7)(inner_grad)
    late_gather.second_far(0)
    second_spread.relay()
    early_gather.first_far()
    late_gather.second(2)
    late_gather.second_far(3)
    pl.loop(0, 3)(inner_grad)
    late_gather.second_far(1)
    early_gather.second(0)
    early_gather.second(1)
    early_gather.second(2)
    late_gather.second_far(2)
    early_gather.second_far(3)
    early_gather.second_far(0)
    second_spread.finish()
    late_gather.finish()
    gate_up(4)
    early_gather.second_far(1)
    gate_up(6)
    early_gather.second_far(2)
    gate_up(5)
    early_gather.finish()
    gate_up(3)
    gate_up(1)
    gate_up(2)
    gate_up(0)
    mixed.drain()
    give_branch(0)
    for part in (io_gather, down_gather, early_gather, late_gather, second_spread):
        part.drain()
    give_second(0)
    turned(second_low, turn_b)
    give_second(1)
    give_second(2)
    gradient(turn_b, 1, 2, 0, 4)
    up_piece.to_sibling(0, 4 * TILE)
    gradient(turn_b, 1, 2, 4, 7)
    up_piece.to_sibling(4 * TILE, 3 * TILE)
    second.relay(1)
    second.relay(0)
    gradient(turn_b, 0, 1, 0, 4)
    gate_piece.to_sibling(0, 4 * TILE)
    second.relay(2)
    give_branch(1)
    give_branch(2)
    up_piece.second_start()
    gradient(turn_b, 0, 1, 4, 7)
    gate_piece.to_sibling(4 * TILE, 3 * TILE)
    normed, inverse = norm_of(residual[...])
    grad_second = second.take()
    small[...] = jnp.zeros_like(small)
    keep_gain(4, grad_second * normed)
    grad_stream = grad_low[own_rows, :].astype(f32) + norm_back(
        grad_second, normed, inverse, gains[1:2, :]
    )
    grad_own[...] = grad_stream
    second_low[own_rows, :] = grad_stream.astype(b16)
    low_spread.start()
    pieces = [
        grad_stream[row : row + 1, at * TILE : (at + 1) * TILE] for row in range(2) for at in range(6)
    ]
    pieces.append(jnp.zeros((EDGE - 12, TILE), f32))
    edge_send[...] = jnp.concatenate(pieces, axis=0).astype(b16)
    for tp in range(4):

        @pl.when(even)
        def _():
            remote(
                edge_send,
                edge_recv.at[lax.div(place.tp, 2)],
                edge_sems.at[2],
                edge_sems.at[3],
                place.along_ctx(-1, tp),
            ).start()

    gradient(turn_a, 2, 0, 0, 4)
    down_piece.to_sibling(0, 4 * TILE)
    gate_piece.second_start()
    gradient(turn_a, 2, 0, 4, 7)
    down_piece.to_sibling(4 * TILE, 3 * TILE)
    low_spread.relay()
    turned(input_low, turn_a)
    branch.relay(0)
    up_piece.second_relay()
    branch.relay(2)
    branch.relay(1)
    down_piece.second_start()
    low_spread.finish()
    wait_bytes(edge_recv, edge_sems.at[3])

    @pl.when(even)
    def _():
        wait_bytes(second_low.at[pl.ds(0, 4 * EDGE), pl.ds(0, TILE)], edge_sems.at[2])

    for slot in range(2):
        packed = edge_recv[slot].astype(f32)
        rows = [
            jnp.concatenate([packed[6 * row + at : 6 * row + at + 1, :] for at in range(6)], axis=1)
            for row in range(2)
        ]
        rows.append(jnp.zeros((EDGE - 2, WIDTH), f32))
        second_low[ROWS + slot * EDGE : ROWS + (slot + 1) * EDGE, :] = jnp.concatenate(
            rows, axis=0
        ).astype(b16)

    grad_gated = dot(second_low[...], flat_io[:, 3 * CHANNELS :])
    conv_grad[:, :SLOT_ROWS, :] = (grad_gated[:ROWS] * projected[1, :ROWS]).reshape(
        2, SLOT_ROWS, CHANNELS
    )
    after = (grad_gated[ROWS:] * projected[1, ROWS + 2 * EDGE :]).reshape(2, EDGE, CHANNELS)
    conv_grad[:, SLOT_ROWS:, :] = jnp.where(place.ctx < 15, after[:, :8, :], 0.0)
    grad_proj[:, CHANNELS : 2 * CHANNELS] = (grad_gated[:ROWS] * convolved[...]).astype(b16)
    grad_product = (
        taps[2:3, :] * conv_grad[:, 0:SLOT_ROWS, :]
        + taps[1:2, :] * conv_grad[:, 1 : 1 + SLOT_ROWS, :]
        + taps[0:1, :] * conv_grad[:, 2 : 2 + SLOT_ROWS, :]
    ).reshape(ROWS, CHANNELS)
    grad_proj[:, 0:CHANNELS] = (grad_product * projected[2, :ROWS]).astype(b16)
    grad_proj[:, 2 * CHANNELS :] = (grad_product * projected[0, :ROWS]).astype(b16)
    second.drain()
    give_first(0)
    gate_piece.second_relay()
    give_first(1)
    for tap in range(3):
        small[8 + tap : 9 + tap, :] = jnp.sum(
            conv_grad[:, :SLOT_ROWS, :] * product[:, 6 + tap : 6 + tap + SLOT_ROWS, :], axis=(0, 1)
        ).reshape(1, CHANNELS)
    up_piece.first_start()
    block_own[...] = (residual[...] + branch.take()).astype(b16)
    block_keep.start()
    give_first(2)
    first.relay(1)
    down_piece.second_relay()
    turned(second_low, turn_b)
    first.relay(0)
    first.relay(2)
    block_spread.start()
    big[:, : 2 * CHANNELS] = dot(turn_a[...], grad_proj[:, : 2 * CHANNELS]).astype(b16)
    io_piece.to_sibling(0, 2 * CHANNELS)
    big[:, 2 * CHANNELS : 3 * CHANNELS] = dot(turn_a[...], grad_proj[:, 2 * CHANNELS :]).astype(b16)
    big[:, 3 * CHANNELS : 4 * CHANNELS] = dot(turn_b[...], gated[...]).astype(b16)
    io_piece.to_sibling(2 * CHANNELS, 2 * CHANNELS)
    up_piece.first_relay()
    io_piece.second_start()
    up_piece.finish()
    normed, inverse = norm_of(x_own[...].astype(f32))
    grad_first = first.take()
    keep_gain(0, grad_first * normed)
    input_own[...] = (
        grad_own[...] + norm_back(grad_first, normed, inverse, gains[0:1, :])
    ).astype(b16)
    input_keep.start()
    exchange(0, 0, [place.along_tp(by) for by in (1, 2, 3)], 8)
    block_spread.relay()
    input_spread.start()
    io_piece.second_relay()
    added(0, 0, 3, 8)
    exchange(1, 3, [place.sibling()])
    gate_piece.first_start()
    down_piece.first_start()
    gate_piece.first_relay()
    block_spread.finish()
    added(1, 3, 1)
    exchange(2, 4, [place.along_first(by) for by in (1, 2, 3)])
    io_piece.first_start()
    down_piece.first_relay()
    input_spread.relay()
    added(2, 4, 3)
    exchange(3, 7, [place.along_second(by) for by in (1, 2, 3)])
    io_piece.first_relay()
    added(3, 7, 3)
    down_piece.finish()
    gate_piece.finish()
    io_piece.finish()
    input_spread.finish()
    block_keep.wait()
    input_keep.wait()
    for part in (low_spread, block_spread, input_spread, first, branch):
        part.drain()
    for part in (down_piece, gate_piece, up_piece, io_piece):
        part.drain()


def step(*given):
    vmem = pl.BlockSpec(memory_space=pltpu.VMEM)
    smem = pl.BlockSpec(memory_space=pltpu.SMEM)
    hbm = pl.BlockSpec(memory_space=pl.ANY)
    f32, b16 = jnp.float32, jnp.bfloat16
    dma = pltpu.SemaphoreType.DMA
    own16 = pltpu.VMEM((QUARTER, WIDTH), b16)
    own32 = pltpu.VMEM((QUARTER, WIDTH), f32)
    full = pltpu.VMEM((ROWS, WIDTH), b16)
    across = pltpu.VMEM((WIDTH, ROWS), b16)
    return pl.pallas_call(
        kernel,
        out_shape=(
            jax.ShapeDtypeStruct((ROWS, WIDTH), b16),
            jax.ShapeDtypeStruct((ROWS, WIDTH), b16),
            jax.ShapeDtypeStruct((3, 16, BLOCK, PADDED), b16),
            jax.ShapeDtypeStruct((3, 12, BLOCK, PADDED), b16),
            jax.ShapeDtypeStruct((4, BLOCK, CHANNELS), f32),
            jax.ShapeDtypeStruct((3, BLOCK, HIDDEN), f32),
            jax.ShapeDtypeStruct((16, CHANNELS), f32),
        ),
        in_specs=[hbm, hbm, smem] + [hbm] * 4 + [vmem] * 2,
        out_specs=(hbm,) * 6 + (vmem,),
        scratch_shapes=[
            pltpu.VMEM((4, BLOCK, CHANNELS), f32),
            pltpu.VMEM((3, BLOCK, HIDDEN), f32),
            pltpu.VMEM((BLOCK, WIDE), b16),
            pltpu.VMEM((3, BLOCK, PADDED), b16),
            pltpu.VMEM((32, BLOCK, WIDE), b16),
            pltpu.VMEM((3, 32, BLOCK, PADDED), b16),
            pltpu.VMEM((WIDTH, PADDED), b16),
            pltpu.VMEM((ROWS, 3 * CHANNELS), b16),
            full,
            own16,
            pltpu.VMEM((2, 2, EDGE, WIDTH), b16),
            pltpu.VMEM((EDGE, TILE), b16),
            pltpu.VMEM((2, EDGE, TILE), b16),
            pltpu.VMEM((ROWS + 4 * EDGE, WIDTH), b16),
            across,
            across,
            full,
            full,
            pltpu.VMEM((2, 2, HALF, WIDTH), b16),
            pltpu.VMEM((2, 2, QUARTER, WIDTH), b16),
            pltpu.VMEM((ROWS + 2 * EDGE, WIDTH), b16),
            own32,
            pltpu.VMEM((3, ROWS + 4 * EDGE, CHANNELS), f32),
            pltpu.VMEM((2, 8 + SLOT_ROWS, CHANNELS), f32),
            pltpu.VMEM((ROWS, CHANNELS), f32),
            pltpu.VMEM((ROWS, CHANNELS), b16),
            own32,
            own16,
            own16,
            pltpu.VMEM((2, SLOT_ROWS + 8, CHANNELS), f32),
            pltpu.VMEM((16, BLOCK, PADDED), b16),
            pltpu.VMEM((3, 3, BLOCK, PADDED), b16),
            pltpu.VMEM((16, BLOCK, WIDE), b16),
            pltpu.VMEM((12, BLOCK, WIDE), b16),
            pltpu.VMEM((10, 16, CHANNELS), f32),
            dma((Gather.SEMS,)),
            dma((Gather.SEMS,)),
            dma((Gather.SEMS,)),
            dma((Gather.SEMS,)),
            dma((4, Scatter.SEMS)),
            dma((4, TpSum.SEMS)),
            dma((4, TpSpread.SEMS)),
            dma((4,)),
            dma((2, 4)),
            dma((10,)),
        ],
        compiler_params=pltpu.CompilerParams(
            collective_id=0, has_side_effects=True, vmem_limit_bytes=63 * 2**20
        ),
        name="step",
    )(*given)


def nesterov(weight, moment, average, gradient, step_rate):
    moment_new = momentum * moment + gradient
    weight_new = weight - step_rate * (gradient + momentum * moment_new)
    average_new = average_decay * average + (1.0 - average_decay) * weight_new
    return (moment_new, weight_new, average_new)


def update_kernel(*refs):
    block_in, input_in = refs[:2]
    old = [refs[2 + 3 * at : 5 + 3 * at] for at in range(6)]
    io_grad, gud_grad, small_grad = refs[20:23]
    block_out, input_out = refs[23:25]
    new = [refs[25 + 3 * at : 28 + 3 * at] for at in range(6)]
    block_held, input_held, wide_held, io_held, gud_held, small_held = refs[43:49]
    held = [refs[49 + 3 * at : 52 + 3 * at] for at in range(6)]
    in_sems, out_sems = refs[67:]

    def moved(source, target, sems, at):
        copy = pltpu.make_async_copy(source, target, sems.at[at])
        copy.start()
        return copy

    order = (2, 3, 0, 1, 4, 5)
    quarters = [pl.ds(at * QUARTER, QUARTER) for at in range(4)]
    input_loads = [
        moved(input_in.at[rows], input_held.at[rows], in_sems, (18, 22, 23, 24)[at])
        for at, rows in enumerate(quarters)
    ]
    block_load = moved(block_in, block_held, in_sems, 25)
    stores = []
    gud_load = moved(gud_grad, gud_held, in_sems, 19)
    loads = {}
    for matrix in order:
        loads[matrix] = [
            moved(old[matrix][at], held[matrix][at], in_sems, 3 * matrix + at) for at in range(3)
        ]
        if matrix == 2:
            io_load = moved(io_grad, io_held, in_sems, 20)
            small_load = moved(small_grad, small_held, in_sems, 21)
    for at, rows in enumerate(quarters):
        input_loads[at].wait()
        wide_held[rows, :] = input_held[rows, :].astype(jnp.float32)
        stores.append(moved(wide_held.at[rows], input_out.at[rows], out_sems, (18, 19, 21, 22)[at]))
    block_load.wait()
    stores.append(moved(block_held, block_out, out_sems, 20))
    for matrix in order:
        for copy in loads[matrix]:
            copy.wait()
        weight, moment, average = held[matrix]
        every, rate = slice(None), matrix_rate
        if matrix == 0:
            io_load.wait()
            parts = [(at, io_held[at]) for at in range(3)]
        elif matrix == 1:
            parts = [(every, io_held[3])]
        elif matrix == 2:
            gud_load.wait()
            parts = [(at, gud_held[at]) for at in range(2)]
        elif matrix == 3:
            parts = [(every, gud_held[2])]
        elif matrix == 4:
            small_load.wait()
            rate = small_rate
            parts = [
                (
                    (slice(row, row + 1), slice(at * CHANNELS, (at + 1) * CHANNELS)),
                    small_held[4 * row + at : 4 * row + at + 1, :],
                )
                for row in range(2)
                for at in range(4)
            ]
        else:
            parts, rate = [(every, small_held[8:11, :])], small_rate
        for at, gradient in parts:
            moment[at], weight[at], average[at] = nesterov(
                weight[at], moment[at], average[at], gradient, rate
            )
        for at, source in enumerate((moment, weight, average)):
            stores.append(moved(source, new[matrix][at], out_sems, 3 * matrix + at))
    for copy in stores:
        copy.wait()


def update(block, input_low, arrays, io_grad, gud_grad, small):
    hbm = pl.BlockSpec(memory_space=pl.ANY)
    f32 = jnp.float32
    like = lambda a: jax.ShapeDtypeStruct(a.shape, a.dtype)
    held = lambda a: pltpu.VMEM(a.shape, a.dtype)
    return pl.pallas_call(
        update_kernel,
        out_shape=(
            like(block),
            jax.ShapeDtypeStruct((ROWS, WIDTH), f32),
            *[like(a) for a in arrays],
        ),
        in_specs=[hbm] * 23,
        out_specs=(hbm,) * 20,
        scratch_shapes=[
            held(block),
            held(input_low),
            pltpu.VMEM((ROWS, WIDTH), f32),
            held(io_grad),
            held(gud_grad),
            held(small),
            *[held(a) for a in arrays],
            pltpu.SemaphoreType.DMA((26,)),
            pltpu.SemaphoreType.DMA((23,)),
        ],
        compiler_params=pltpu.CompilerParams(vmem_limit_bytes=62 * 2**20),
        name="update",
    )(block, input_low, *arrays, io_grad, gud_grad, small)


def on_device(
    hidden,
    lengths,
    cotangent,
    in_weight,
    in_moment,
    in_average,
    out_weight,
    out_moment,
    out_average,
    gate_up_weight,
    gate_up_moment,
    gate_up_average,
    down_weight,
    down_moment,
    down_average,
    norm_gains,
    gain_moment,
    gain_average,
    conv_taps,
    taps_moment,
    taps_average,
):
    slot_count, seq_len, model_width = hidden.shape
    row_count = slot_count * seq_len
    block_output, input_low_grad, _, _, io_sum, gud_sum, small = step(
        hidden.reshape(row_count, model_width),
        cotangent.reshape(row_count, model_width),
        lengths,
        in_weight,
        out_weight.T,
        gate_up_weight,
        down_weight.T,
        norm_gains,
        conv_taps,
    )
    matrices = (
        (in_weight, in_moment, in_average),
        (out_weight.T, out_moment.T, out_average.T),
        (gate_up_weight, gate_up_moment, gate_up_average),
        (down_weight.T, down_moment.T, down_average.T),
    )
    smalls = (norm_gains, gain_moment, gain_average, conv_taps, taps_moment, taps_average)
    block_output, input_grad, *new = update(
        block_output,
        input_low_grad,
        [a for group in matrices for a in group] + list(smalls),
        io_sum,
        gud_sum,
        small,
    )
    return (
        block_output.reshape(slot_count, seq_len, model_width),
        input_grad.reshape(slot_count, seq_len, model_width),
        *new[0:3],
        *[a.T for a in new[3:6]],
        *new[6:9],
        *[a.T for a in new[9:12]],
        *new[12:18],
    )


def solution(mesh):
    placed = (
        P("shard", "ctx", None),
        P("shard"),
        P("shard", "ctx", None),
        P(None, ("shard", "ctx"), "tp"),
        P(None, ("shard", "ctx"), "tp"),
        P(None, ("shard", "ctx"), "tp"),
        P("tp", ("shard", "ctx")),
        P("tp", ("shard", "ctx")),
        P("tp", ("shard", "ctx")),
        P(None, ("shard", "ctx"), "tp"),
        P(None, ("shard", "ctx"), "tp"),
        P(None, ("shard", "ctx"), "tp"),
        P("tp", ("shard", "ctx")),
        P("tp", ("shard", "ctx")),
        P("tp", ("shard", "ctx")),
        P(),
        P(),
        P(),
        P(None, "tp"),
        P(None, "tp"),
        P(None, "tp"),
    )
    return jax.shard_map(
        on_device,
        mesh=mesh,
        in_specs=placed,
        out_specs=(
            P("shard", "ctx", None),
            P("shard", "ctx", None),
            P(None, ("shard", "ctx"), "tp"),
            P(None, ("shard", "ctx"), "tp"),
            P(None, ("shard", "ctx"), "tp"),
            P("tp", ("shard", "ctx")),
            P("tp", ("shard", "ctx")),
            P("tp", ("shard", "ctx")),
            P(None, ("shard", "ctx"), "tp"),
            P(None, ("shard", "ctx"), "tp"),
            P(None, ("shard", "ctx"), "tp"),
            P("tp", ("shard", "ctx")),
            P("tp", ("shard", "ctx")),
            P("tp", ("shard", "ctx")),
            P(),
            P(),
            P(),
            P(None, "tp"),
            P(None, "tp"),
            P(None, "tp"),
        ),
        check_vma=False,
    )
```
